128 devices in a mesh: lat: 8 (over x, z_hi), lon: 16 (over y, z_lo, core).
Axes of the slice: x: 4, y: 4, z: 4 (z_hi: 2, z_lo: 2; z = z_hi * 2 + z_lo), core: 2. Of those that a mesh axis runs over, the one named last changes fastest.
Arguments:
- features: bfloat16 [128, 16, 128, 256], P(('lat', 'lon')), may hold values from -6 to 6
- offsets: float32 [2, 128, 16, 128], P(None, ('lat', 'lon')), may hold values from -1 to 1
- counts: int32 [128, 128], P(('lat', 'lon')), may hold values from 1 to 16, as said below
- cell_index: int32 [128, 16, 128], P(('lat', 'lon')), may hold values from 0 to 4095
- kernel: bfloat16 [3, 3, 256, 256], replicated, may hold values from -0.125 to 0.125
- conv_bias: float32 [256], replicated, may hold values from -3 to 3
- cotangent: bfloat16 [256, 2048, 256], P('lat', 'lon'), may hold values from -6 to 6
Outputs:
- encoded: bfloat16 [256, 2048, 256], P('lat', 'lon')
- weight_grad: float32 [3, 3, 256, 256], replicated
- bias_grad: float32 [256], replicated
- obs_grad: bfloat16 [128, 16, 128, 256], P(('lat', 'lon'))
The draws below stay inside these ranges and needn't reach their ends.
Inputs may be any that keep to these rules, and one draw needn't show every extreme that they name: `counts`: each destination tile receives 16 live slots from every device in some draws; in every draw at least one tile does, and every device sends 16 live slots to some tile.
All inputs are finite; a program needn't handle non-finite values.
Results may differ from the reference program's by a relative error of at most 0.008.
Values may be sent and summed in bfloat16 or wider, within the bound.
A program may use at most 128 MiB of HBM per device.

```python
import jax
import jax.numpy as jnp
from jax import lax

C = 256
LAT_DEV = 32
LON_DEV = 128
CAP = 16
NLAT = 256
NLON = 2048
N_LON = 16
DEVICES = 128


def draw_counts(key, part):
    key = jax.random.fold_in(key, 11)
    keys = jax.random.split(key, 5)
    heavy = jax.random.randint(keys[0], (DEVICES,), 0, 4) == 0
    light = jax.random.randint(keys[1], (DEVICES, DEVICES), 1, CAP // 2 + 2)
    nearly = CAP - jax.random.randint(keys[2], (DEVICES, DEVICES), 0, CAP // 4 + 1)
    loads = jnp.where(heavy[None, :], nearly, light)
    column = jax.random.randint(keys[3], (), 0, DEVICES)
    offset = jax.random.randint(keys[4], (), 0, DEVICES)
    source = jnp.arange(DEVICES)[:, None]
    target = jnp.arange(DEVICES)[None, :]
    forced = (target == column) | (target == (source + offset) % DEVICES)
    return jnp.where(forced, CAP, loads).astype(jnp.int32)


def place_ends(values, key, smallest, largest):
    dims = values.shape
    place = [jax.random.randint(jax.random.fold_in(key, axis), (), 0, dims[axis]) for axis in range(len(dims))]
    values = values.at[tuple(place)].set(smallest)
    longest = dims.index(max(dims))
    place[longest] = (place[longest] + 1) % dims[longest]
    return values.at[tuple(place)].set(largest)


def level_of(key, shape, pieces, low, largest):
    gain, own = 1.0, jax.random.fold_in(key, 6)
    for dim, blocks in pieces:
        heights = jnp.exp(jax.random.uniform(jax.random.fold_in(own, dim), (blocks,), jnp.float32, low / len(pieces), largest / len(pieces)))
        gain = gain * jnp.repeat(heights, shape[dim] // blocks).reshape([-1 if axis == dim else 1 for axis in range(len(shape))])
    return gain


def noise(own_key, dims, scale, limit, cuts=(), held_as=jnp.bfloat16):
    entries = jax.random.normal(own_key, dims, jnp.float32) * scale
    if len(cuts) > 0:
        entries = level_of(own_key, dims, cuts, -0.22, 0.18) * entries
    return jnp.clip(entries, min=-limit, max=limit).astype(held_as)


def setup_inputs(seed: int = 0) -> dict:
    streams_of = jax.random.split(jax.random.key(seed), 8)
    return {
        "features": noise(streams_of[0], (DEVICES, CAP, DEVICES, C), 1.0, 6.0, ((0, 128),)),
        "offsets": jnp.clip(jax.random.uniform(streams_of[1], (2, DEVICES, CAP, DEVICES), jnp.float32, -1.0, 1.0) * level_of(streams_of[1], (2, DEVICES, CAP, DEVICES), ((1, 128),), -0.4, 0.0), -1.0, 1.0),
        "counts": draw_counts(jax.random.fold_in(streams_of[7], 71), 0),
        "cell_index": place_ends(jax.random.randint(streams_of[3], (DEVICES, CAP, DEVICES), 0, LAT_DEV * LON_DEV), jax.random.fold_in(streams_of[3], 1), 0, (LAT_DEV * LON_DEV) - 1).astype(jnp.int32),
        "kernel": noise(streams_of[4], (3, 3, C, C), (9 * C) ** -0.5, 0.125),
        "conv_bias": noise(streams_of[5], (C,), 0.5, 3.0, (), jnp.float32),
        "cotangent": noise(streams_of[6], (NLAT, NLON, C), 1.0, 6.0, ((0, 8), (1, 16))),
    }


def wrap_pad(grid):
    padded = jnp.pad(grid, ((1, 1), (0, 0), (0, 0)))
    return jnp.concatenate([padded[:, -1:], padded, padded[:, :1]], axis=1)

def convolve(padded, kernel, rows, cols):
    channels = padded.shape[2]
    total = jnp.zeros((rows * cols, kernel.shape[3]), jnp.float32)
    for row_off in range(3):
        for col_off in range(3):
            window = padded[row_off:row_off + rows, col_off:col_off + cols].reshape(-1, channels)
            total = total + jnp.dot(window, kernel[row_off, col_off], preferred_element_type=jnp.float32)
    return total.reshape(rows, cols, -1)

def back_convolve(padded, kernel, rows, cols):
    channels = padded.shape[2]
    total = jnp.zeros((rows * cols, kernel.shape[2]), jnp.float32)
    for row_off in range(3):
        for col_off in range(3):
            window = padded[2 - row_off:2 - row_off + rows, 2 - col_off:2 - col_off + cols].reshape(-1, channels)
            total = total + lax.dot_general(window, kernel[row_off, col_off], (((1,), (1,)), ((), ())), preferred_element_type=jnp.float32)
    return total.reshape(rows, cols, -1)

def reference(features, offsets, counts, cell_index, kernel, conv_bias, cotangent):
    slot_ids = jnp.arange(CAP, dtype=jnp.int32)
    live_mask = slot_ids[None, :, None] < counts[:, None, :]
    radius = offsets[0] * offsets[0] + offsets[1] * offsets[1]
    weights = jnp.where(live_mask, jnp.exp(-2.0 * radius), 0.0).astype(jnp.bfloat16)
    dest_ids = jnp.arange(DEVICES, dtype=jnp.int32)
    lat_band = dest_ids // N_LON
    sector = dest_ids % N_LON
    grid_row = lat_band[None, None, :] * LAT_DEV + cell_index // LON_DEV
    grid_col = sector[None, None, :] * LON_DEV + cell_index % LON_DEV
    grid_place = (grid_row * NLON + grid_col).reshape(-1).astype(jnp.int32)
    weight_flat = weights.reshape(-1).astype(jnp.float32)
    flat_features = features.reshape(-1, C).astype(jnp.float32)
    gathered = jax.ops.segment_sum(weight_flat[:, None] * flat_features, grid_place, num_segments=NLAT * NLON)
    density = jax.ops.segment_sum(weight_flat, grid_place, num_segments=NLAT * NLON)
    grid_field = (gathered / (density[:, None] + 1.0)).astype(jnp.bfloat16).reshape(NLAT, NLON, C)
    padded = wrap_pad(grid_field)
    activation = convolve(padded, kernel, NLAT, NLON) + conv_bias
    sigmoid_gate = jax.nn.sigmoid(activation)
    encoded = (grid_field.astype(jnp.float32) + activation * sigmoid_gate).astype(jnp.bfloat16)
    grad_act = (cotangent.astype(jnp.float32) * sigmoid_gate * (1.0 + activation * (1.0 - sigmoid_gate))).astype(jnp.bfloat16)
    norm_scale = 1.0 / jnp.sqrt(jnp.float32(NLAT * NLON))
    grad_flat = grad_act.reshape(-1, C)
    blocks = []
    for row_off in range(3):
        for col_off in range(3):
            window = padded[row_off:row_off + NLAT, col_off:col_off + NLON].reshape(-1, C)
            blocks.append(lax.dot_general(window, grad_flat, (((0,), (0,)), ((), ())), preferred_element_type=jnp.float32))
    weight_grad = jnp.stack(blocks).reshape(3, 3, C, C) * norm_scale
    bias_grad = lax.optimization_barrier(jnp.sum(grad_flat.astype(jnp.float32), axis=0)) * norm_scale
    field_grad = cotangent.astype(jnp.float32) + back_convolve(wrap_pad(grad_act), kernel, NLAT, NLON)
    scaled = (field_grad.reshape(-1, C) / (density[:, None] + 1.0)).astype(jnp.bfloat16)
    picked = jnp.take(scaled, grid_place, axis=0).astype(jnp.float32)
    obs_grad = (weight_flat[:, None] * picked).astype(jnp.bfloat16).reshape(DEVICES, CAP, DEVICES, C)
    return (encoded, weight_grad, bias_grad, obs_grad)
```

```python
import functools
import math

import jax
import jax.numpy as jnp
from jax import lax
from jax.experimental import pallas as pl
from jax.experimental.pallas import tpu as pltpu
from jax.sharding import PartitionSpec as P

BF = jnp.bfloat16
F32 = jnp.float32
MESH = pl.DeviceIdType.MESH
ROWS, COLS, CH, CAP = 32, 128, 256, 16
NLAT, NLON = 8, 16
DEV = NLAT * NLON
SLOTS = DEV * CAP
CELLS = ROWS * COLS
PAIRS = DEV // 2
CHUNKS = 73
EXTRAS = CHUNKS - PAIRS


def iota(shape, dim):
    return lax.broadcasted_iota(jnp.int32, shape, dim)


def fiota(shape, dim):
    return iota(shape, dim).astype(F32)


def aligned(value, unit=128):
    return pl.multiple_of(value, unit)


def remote(src, dst, send, recv, lat, lon):
    return pltpu.make_async_remote_copy(
        src_ref=src, dst_ref=dst, send_sem=send, recv_sem=recv, device_id=(lat, lon), device_id_type=MESH
    )


def wait_bytes(ref, sem):
    pltpu.make_async_copy(ref, ref, sem).wait()


def expand_lanes(meta, onehot, wrf, wrb, dens, edges, edge_inv):
    per_dev = meta[...].reshape(DEV, 128).astype(BF)
    lane = iota((128, 384), 1)
    pick = jnp.where(iota((128, 384), 0) == (lane // 128) * CAP + lane % CAP, 1.0, 0.0).astype(BF)
    spread = jnp.dot(per_dev, pick, preferred_element_type=F32).reshape(16, 8, 384)
    lane8 = iota((8, 384), 1)
    mine = jnp.where(iota((8, 384), 0) == (lane8 % 128) // CAP, 1.0, 0.0)
    flat = (spread * mine[None]).sum(1)
    total = jnp.zeros((2 * ROWS, 128), F32)
    for g in range(16):
        wide = slice(g * 128, g * 128 + 128)
        w, row, col = flat[g : g + 1, 0:128], flat[g : g + 1, 128:256], flat[g : g + 1, 256:384]
        onehot[:, wide] = jnp.where(fiota((COLS, 128), 0) == col, 1.0, 0.0).astype(BF)
        by_row = jnp.where(fiota((ROWS, 128), 0) == row, w, 0.0)
        wrf[:, wide] = by_row
        first = jnp.where(col == 0.0, by_row, 0.0)
        last = jnp.where(col == float(COLS - 1), by_row, 0.0)
        both = jnp.concatenate([first, last], 0)
        edges[:, wide] = both.astype(BF)
        total = total + both
    edge_inv[...] = jnp.broadcast_to(1.0 / (total.sum(1, keepdims=True) + 1.0), (2 * ROWS, 128))

    def widen(r, _):
        wrb[r] = jnp.broadcast_to(wrf[pl.ds(r, 1), :], (16, SLOTS)).astype(BF)
        return 0

    lax.fori_loop(0, ROWS, widen, 0)
    density = lax.dot_general(
        onehot[...], wrf[...].astype(BF), (((1,), (1,)), ((), ())), preferred_element_type=F32
    )
    inv = 1.0 / (density + 1.0)
    for r in range(ROWS):
        dens[r * COLS : (r + 1) * COLS, :] = jnp.broadcast_to(inv[:, r : r + 1], (COLS, 128))


def expand_rows(meta, col_weight, row_of):
    lane = iota((128, 384), 1)
    pick = jnp.where(iota((128, 384), 0) // CAP == lane // 128, 1.0, 0.0).astype(BF)
    slot_lane = iota((CAP, 128), 1)
    mine = jnp.where(slot_lane % CAP == iota((CAP, 128), 0), 1.0, 0.0)

    def step(i, _):
        block = meta[pl.ds(i * 16, 16)]
        masked = (jnp.broadcast_to(block, (16, CAP, 128)) * mine[None]).reshape(256, 128).astype(BF)
        spread = jnp.dot(masked, pick, preferred_element_type=F32)
        base = aligned(i * 256, 256)
        col_weight[pl.ds(base, 256), :] = jnp.where(
            spread[:, 256:384] == fiota((256, 128), 1), spread[:, 0:128], 0.0
        ).astype(BF)
        row_of[pl.ds(base, 256), :] = spread[:, 128:256].astype(BF)
        return 0

    lax.fori_loop(0, DEV // 16, step, 0)


def twice(inv):
    return jnp.concatenate([inv, inv], 1)


def splat_edges(feats, onehot, wrb, dens, edges, edge_inv, rows_out, cols_out):
    hot = onehot[...].reshape(8, 16, SLOTS)
    lhs = jnp.concatenate(
        [(hot * wrb[0][None]).reshape(COLS, SLOTS), (hot * wrb[ROWS - 1][None]).reshape(COLS, SLOTS), edges[...]], 0
    )
    acc = jnp.dot(lhs, feats[...].reshape(SLOTS, CH), preferred_element_type=F32)
    rows_out[0] = (acc[0:COLS] * twice(dens[0:COLS, :])).astype(BF)
    rows_out[1] = (acc[COLS : 2 * COLS] * twice(dens[CELLS - COLS : CELLS, :])).astype(BF)
    cols = (acc[2 * COLS :] * twice(edge_inv[...])).astype(BF)
    cols_out[0] = cols[0:ROWS]
    cols_out[1] = cols[ROWS:]


def splat(feats, onehot, wrb, dens, x3, per=4):
    def step(i, _):
        r0 = i * per
        hot = onehot[...].reshape(8, 16, SLOTS)
        lhs = jnp.concatenate([(hot * wrb[r0 + k][None]).reshape(COLS, SLOTS) for k in range(per)], 0)
        acc = jnp.dot(lhs, feats[...].reshape(SLOTS, CH), preferred_element_type=F32)
        for k in range(per):
            base = aligned((r0 + k) * COLS)
            field = (acc[k * COLS : (k + 1) * COLS] * twice(dens[pl.ds(base, COLS), :])).astype(BF)
            wide = field.astype(F32)
            x3[pl.ds(base + COLS, COLS), 256:512] = field
            x3[pl.ds(base + COLS, COLS), 0:256] = pltpu.roll(wide, 1, 0).astype(BF)
            x3[pl.ds(base + COLS, COLS), 512:768] = pltpu.roll(wide, COLS - 1, 0).astype(BF)
        return 0

    lax.fori_loop(0, ROWS // per, step, 0)


def exchange_edges(lat, lon, rows, cols, h_row, h_col, h_cor, sems):
    up, down = lax.rem(lat + NLAT - 1, NLAT), lax.rem(lat + 1, NLAT)
    west, east = lax.rem(lon + NLON - 1, NLON), lax.rem(lon + 1, NLON)
    plan = (
        (rows[0], h_row.at[1], up, lon),
        (rows[1], h_row.at[0], down, lon),
        (cols.at[0], h_col.at[1], lat, west),
        (cols.at[1], h_col.at[0], lat, east),
        (cols.at[1, pl.ds(16, 16)], h_cor.at[0], down, east),
        (cols.at[0, pl.ds(16, 16)], h_cor.at[1], down, west),
        (cols.at[1, pl.ds(0, 16)], h_cor.at[2], up, east),
        (cols.at[0, pl.ds(0, 16)], h_cor.at[3], up, west),
    )
    return [remote(s, d, sems.at[0, i], sems.at[1, i], a, b) for i, (s, d, a, b) in enumerate(plan)]


def patch(arr, lat, h_row, h_col, h_cor, col_vals, left, right):
    top = jnp.where(lat == 0, 0.0, 1.0)
    bottom = jnp.where(lat == NLAT - 1, 0.0, 1.0)
    for side in range(2):
        col_vals[side, 0:32, :] = h_col[side].astype(F32)
        col_vals[side, 32:40, :] = jnp.broadcast_to(h_cor[side].astype(F32)[15:16] * top, (8, CH))
        col_vals[side, 40:48, :] = jnp.broadcast_to(h_cor[2 + side].astype(F32)[0:1] * bottom, (8, CH))
    sub = iota((16, CH), 0)

    def step(r, _):
        base = aligned((r + 1) * COLS)
        old = arr[pl.ds(base, 16), left : left + CH].astype(F32)
        arr[pl.ds(base, 16), left : left + CH] = jnp.where(sub == 0, col_vals[0, pl.ds(r, 1), :], old).astype(BF)
        far = aligned(base + COLS - 16, 16)
        old = arr[pl.ds(far, 16), right : right + CH].astype(F32)
        arr[pl.ds(far, 16), right : right + CH] = jnp.where(sub == 15, col_vals[1, pl.ds(r, 1), :], old).astype(BF)
        return 0

    lax.fori_loop(0, ROWS, step, 0)
    full = iota((COLS, CH), 0)
    for side, (base, keep) in enumerate(((0, top), ((ROWS + 1) * COLS, bottom))):
        at = 32 + 8 * side
        wide = h_row[side].astype(F32) * keep
        arr[base : base + COLS, 256:512] = wide.astype(BF)
        arr[base : base + COLS, left : left + CH] = jnp.where(
            full == 0, col_vals[0, at : at + 1, :], pltpu.roll(wide, 1, 0)
        ).astype(BF)
        arr[base : base + COLS, right : right + CH] = jnp.where(
            full == COLS - 1, col_vals[1, at : at + 1, :], pltpu.roll(wide, COLS - 1, 0)
        ).astype(BF)


def conv(x3, kc, bias, cot, enc, g3, gsum, gcol, per=4):
    gsum[...] = jnp.zeros_like(gsum)

    def step(i, _):
        r0 = i * per
        acc = jnp.broadcast_to(bias[...], (per * COLS, CH))
        for a in range(3):
            acc = acc + jnp.dot(
                x3[pl.ds(aligned((r0 + a) * COLS), per * COLS), :], kc[a], preferred_element_type=F32
            )
        base = aligned(r0 * COLS)
        gate = 0.5 * jnp.tanh(0.5 * acc) + 0.5
        silu = acc * gate
        field = x3[pl.ds(base + COLS, per * COLS), 256:512].astype(F32)
        enc[pl.ds(base, per * COLS), :] = (field + silu).astype(BF)
        grad = (cot[pl.ds(base, per * COLS), :].astype(F32) * (gate + silu * (1.0 - gate))).astype(BF)
        wide = grad.astype(F32)
        gsum[...] += wide.reshape(per * COLS // 8, 8, CH).sum(0)
        g3[pl.ds(base + COLS, per * COLS), 256:512] = grad
        for k in range(per):
            row = wide[k * COLS : (k + 1) * COLS]
            at = pl.ds(base + COLS + k * COLS, COLS)
            g3[at, 0:256] = pltpu.roll(row, COLS - 1, 0).astype(BF)
            g3[at, 512:768] = pltpu.roll(row, 1, 0).astype(BF)
            gcol[0, pl.ds(r0 + k, 1), :] = row[0:1]
            gcol[1, pl.ds(r0 + k, 1), :] = row[COLS - 1 : COLS]
        return 0

    lax.fori_loop(0, ROWS // per, step, 0)


def back_conv(g3, kt, cot, dens, scaled, per=4):
    def step(i, _):
        r0 = i * per
        base = aligned(r0 * COLS)
        acc = cot[pl.ds(base, per * COLS), :].astype(F32)
        for a in range(3):
            acc = acc + jnp.dot(
                g3[pl.ds(aligned((r0 + 2 - a) * COLS), per * COLS), :], kt[a], preferred_element_type=F32
            )
        scaled[pl.ds(base, per * COLS), :] = (acc * twice(dens[pl.ds(base, per * COLS), :])).astype(BF)
        return 0

    lax.fori_loop(0, ROWS // per, step, 0)


def kernel(
    feat_in, meta_in, kern_in, bias, cot_in,
    enc_out, sums_out, ret_out,
    feats, meta, kc, kt, cot, enc, onehot, wrf, wrb, dens, edges, edge_inv, col_weight, row_of,
    edge_rows, edge_cols, h_row, h_col, h_cor, col_vals, x3, g3, gsum, gcol, grad_cols, scaled, slot_grad,
    dw, pair_dw, pair_sum, half, rs, rs_extra, reduced,
    load_sems, a2a_sems, halo_sems, grad_halo_sems, pair_sems, rs_sems, ag_sems, swap_sems, ret_sems,
):
    lat, lon = lax.axis_index("lat"), lax.axis_index("lon")
    me = lat * NLON + lon
    core = lax.rem(lon, 2)
    mate = lon + 1 - 2 * core
    owner = lat * (NLON // 2) + lon // 2

    def send_meta(j, _):
        to = lax.rem(me + j, DEV)
        remote(meta_in.at[to], meta.at[me], a2a_sems.at[0], a2a_sems.at[1], to // NLON, lax.rem(to, NLON)).start()
        return 0

    def send_feats(j, _):
        to = lax.rem(me + j, DEV)
        remote(feat_in.at[to], feats.at[me], a2a_sems.at[2], a2a_sems.at[3], to // NLON, lax.rem(to, NLON)).start()
        return 0

    own_meta = pltpu.make_async_copy(meta_in.at[me], meta.at[me], load_sems.at[0])
    own_feats = pltpu.make_async_copy(feat_in.at[me], feats.at[me], load_sems.at[1])
    load_kern = pltpu.make_async_copy(kern_in, kc, load_sems.at[2])
    load_cot = pltpu.make_async_copy(cot_in, cot, load_sems.at[3])
    own_meta.start()
    lax.fori_loop(1, DEV, send_meta, 0)
    lax.fori_loop(1, DEV, send_feats, 0)
    own_feats.start()
    load_kern.start()
    load_cot.start()

    load_kern.wait()
    for a in range(3):
        for b in range(3):
            kt[a, b * CH : (b + 1) * CH, :] = kc[a, b * CH : (b + 1) * CH, :].T

    own_meta.wait()
    wait_bytes(meta.at[pl.ds(0, DEV - 1)], a2a_sems.at[1])
    expand_lanes(meta, onehot, wrf, wrb, dens, edges, edge_inv)
    expand_rows(meta, col_weight, row_of)

    own_feats.wait()
    wait_bytes(feats.at[pl.ds(0, DEV - 1)], a2a_sems.at[3])
    splat_edges(feats, onehot, wrb, dens, edges, edge_inv, edge_rows, edge_cols)
    halo = exchange_edges(
        lat, lon, (edge_rows.at[0], edge_rows.at[1]), edge_cols, h_row.at[0], h_col.at[0], h_cor.at[0], halo_sems
    )
    for copy in halo:
        copy.start()
    splat(feats, onehot, wrb, dens, x3)
    for copy in halo:
        copy.wait_recv()
    patch(x3, lat, h_row.at[0], h_col.at[0], h_cor.at[0], col_vals, 0, 512)

    load_cot.wait()
    conv(x3, kc, bias, cot, enc, g3, gsum, gcol)
    store_enc = pltpu.make_async_copy(enc, enc_out, load_sems.at[4])
    store_enc.start()
    grad_cols[...] = gcol[...].astype(BF)
    last = ROWS * COLS
    grad_halo = exchange_edges(
        lat, lon, (g3.at[pl.ds(COLS, COLS), pl.ds(CH, CH)], g3.at[pl.ds(last, COLS), pl.ds(CH, CH)]),
        grad_cols, h_row.at[1], h_col.at[1], h_cor.at[1], grad_halo_sems,
    )
    for copy in grad_halo:
        copy.start()

    pair = []
    for tap in range(9):
        a, b = tap // 3, tap % 3
        dw[tap * CH : (tap + 1) * CH, :] = lax.dot_general(
            x3[a * COLS : a * COLS + CELLS, b * CH : (b + 1) * CH], g3[COLS : COLS + CELLS, CH : 2 * CH],
            (((0,), (0,)), ((), ())), preferred_element_type=F32,
        )
        pair.append(
            remote(
                dw.at[pl.ds(aligned(tap * CH + 128 * (1 - core)), 128)], pair_dw.at[pl.ds(tap * 128, 128)],
                pair_sems.at[0, tap], pair_sems.at[1, tap], lat, mate,
            )
        )
        pair[-1].start()
    pair.append(remote(gsum, pair_sum, pair_sems.at[0, 9], pair_sems.at[1, 9], lat, mate))
    pair[-1].start()

    for copy in grad_halo:
        copy.wait()
    patch(g3, lat, h_row.at[1], h_col.at[1], h_cor.at[1], col_vals, 512, 0)

    for tap in range(9):
        pair[tap].wait()
        mine = dw[pl.ds(aligned(tap * CH + 128 * core), 128), :] + pair_dw[tap * 128 : (tap + 1) * 128, :]
        half[tap * 8 : (tap + 1) * 8] = mine.astype(BF).reshape(8, 16, CH)
    pair[9].wait()
    bias_row = (gsum[...] + pair_sum[...]).sum(0, keepdims=True)
    half[CHUNKS - 1] = jnp.where(iota((16, CH), 0) == 0, bias_row, 0.0).astype(BF)

    def send_chunk(j, _):
        to = lax.rem(owner + j, PAIRS)
        remote(
            half.at[to], rs.at[owner], rs_sems.at[0], rs_sems.at[1], to // 8, lax.rem(to, 8) * 2 + core
        ).start()
        return 0

    lax.fori_loop(1, PAIRS, send_chunk, 0)
    rs[owner] = half[owner]
    for e in range(EXTRAS):
        to = (9 * e) % PAIRS

        @pl.when(owner != to)
        def _():
            remote(
                half.at[PAIRS + e], rs_extra.at[owner], rs_sems.at[2], rs_sems.at[3], to // 8, (to % 8) * 2 + core
            ).start()

        @pl.when(owner == to)
        def _():
            rs_extra[owner] = half[PAIRS + e]

    back_conv(g3, kt, cot, dens, scaled)

    def send_sum(src, dst, send, recv):
        def step(j, _):
            to = lax.rem(owner + j, PAIRS)
            remote(src, dst, send, recv, to // 8, lax.rem(to, 8) * 2 + core).start()
            return 0

        lax.fori_loop(1, PAIRS, step, 0)

    wait_bytes(rs.at[pl.ds(0, PAIRS - 1)], rs_sems.at[1])
    reduced[0] = rs[...].astype(F32).sum(0).astype(BF)
    send_sum(reduced.at[0], sums_out.at[core, owner], ag_sems.at[0], ag_sems.at[1])
    own_sum = pltpu.make_async_copy(reduced.at[0], sums_out.at[core, owner], load_sems.at[5])
    own_sum.start()
    for e in range(EXTRAS):

        @pl.when(owner == (9 * e) % PAIRS)
        def _():
            wait_bytes(rs_extra.at[pl.ds(0, PAIRS - 1)], rs_sems.at[3])
            reduced[1] = rs_extra[...].astype(F32).sum(0).astype(BF)
            spot = sums_out.at[core, PAIRS + e]
            send_sum(reduced.at[1], spot, ag_sems.at[2], ag_sems.at[1])
            own_extra = pltpu.make_async_copy(reduced.at[1], spot, load_sems.at[6])
            own_extra.start()
            own_extra.wait()

    def band(i, _):
        to_lat = lax.rem(lat + i, NLAT)
        base = aligned(to_lat * 256, 256)
        weight, row = col_weight[pl.ds(base, 256), :], row_of[pl.ds(base, 256), :]
        lhs = jnp.concatenate(
            [jnp.where(row == jnp.array(r, BF), weight, jnp.zeros_like(weight)) for r in range(ROWS)], 1
        )
        grads = jnp.dot(lhs, scaled[...], preferred_element_type=F32).astype(BF)
        slot_grad[pl.ds(to_lat * NLON, NLON)] = grads.reshape(NLON, CAP, CH)

        def back(j, _):
            to_lon = lax.rem(lon + j, NLON)
            block = slot_grad.at[to_lat * NLON + to_lon]

            @pl.when(jnp.logical_or(i != 0, j != 0))
            def _():
                remote(block, ret_out.at[me], ret_sems.at[0], ret_sems.at[1], to_lat, to_lon).start()

            return 0

        lax.fori_loop(0, NLON, back, 0)
        return 0

    lax.fori_loop(0, NLAT, band, 0)
    own_ret = pltpu.make_async_copy(slot_grad.at[me], ret_out.at[me], load_sems.at[7])
    own_ret.start()

    own_sum.wait()
    has_extra = functools.reduce(jnp.logical_or, [owner == (9 * e) % PAIRS for e in range(EXTRAS)])

    @pl.when(has_extra)
    def _():
        wait_bytes(sums_out.at[core, pl.ds(0, CHUNKS - 2)], ag_sems.at[1])

    @pl.when(jnp.logical_not(has_extra))
    def _():
        wait_bytes(sums_out.at[core, pl.ds(0, CHUNKS - 1)], ag_sems.at[1])

    swap = remote(sums_out.at[core], sums_out.at[core], swap_sems.at[0], swap_sems.at[1], lat, mate)
    swap.start()

    wait_bytes(ret_out.at[pl.ds(0, DEV - 1)], ret_sems.at[1])
    wait_bytes(slot_grad.at[pl.ds(0, DEV - 1)], ret_sems.at[0])
    wait_bytes(meta.at[pl.ds(0, DEV - 1)], a2a_sems.at[0])
    wait_bytes(feats.at[pl.ds(0, DEV - 1)], a2a_sems.at[2])
    for copy in halo:
        copy.wait_send()
    wait_bytes(rs.at[pl.ds(0, PAIRS - 1)], rs_sems.at[0])
    wait_bytes(rs.at[pl.ds(0, PAIRS - 1)], ag_sems.at[0])

    @pl.when(has_extra)
    def _():
        wait_bytes(rs.at[pl.ds(0, PAIRS - 1)], ag_sems.at[2])
        wait_bytes(half.at[pl.ds(0, EXTRAS - 1)], rs_sems.at[2])

    @pl.when(jnp.logical_not(has_extra))
    def _():
        wait_bytes(half.at[pl.ds(0, EXTRAS)], rs_sems.at[2])

    own_ret.wait()
    store_enc.wait()
    swap.wait()


def fused(feat, meta, kern, bias, cot):
    vm = pltpu.VMEM
    dma = pltpu.SemaphoreType.DMA
    scratch = [
        vm((DEV, CAP, CH), BF),
        vm((DEV, 1, 128), F32),
        vm((3, 3 * CH, CH), BF),
        vm((3, 3 * CH, CH), BF),
        vm((CELLS, CH), BF),
        vm((CELLS, CH), BF),
        vm((COLS, SLOTS), BF),
        vm((ROWS, SLOTS), F32),
        vm((ROWS, 16, SLOTS), BF),
        vm((CELLS, 128), F32),
        vm((2 * ROWS, SLOTS), BF),
        vm((2 * ROWS, 128), F32),
        vm((SLOTS, 128), BF),
        vm((SLOTS, 128), BF),
        vm((2, COLS, CH), BF),
        vm((2, ROWS, CH), BF),
        vm((2, 2, COLS, CH), BF),
        vm((2, 2, ROWS, CH), BF),
        vm((2, 4, 16, CH), BF),
        vm((2, 48, CH), F32),
        vm(((ROWS + 2) * COLS, 3 * CH), BF),
        vm(((ROWS + 2) * COLS, 3 * CH), BF),
        vm((8, CH), F32),
        vm((2, ROWS, CH), F32),
        vm((2, ROWS, CH), BF),
        vm((CELLS, CH), BF),
        vm((DEV, CAP, CH), BF),
        vm((9 * CH, CH), F32),
        vm((9 * 128, CH), F32),
        vm((8, CH), F32),
        vm((CHUNKS, 16, CH), BF),
        vm((PAIRS, 16, CH), BF),
        vm((PAIRS, 16, CH), BF),
        vm((2, 16, CH), BF),
        dma((8,)),
        dma((4,)),
        dma((2, 8)),
        dma((2, 8)),
        dma((2, 10)),
        dma((4,)),
        dma((3,)),
        dma((2,)),
        dma((2,)),
    ]
    anywhere = pl.BlockSpec(memory_space=pl.ANY)
    return pl.pallas_call(
        kernel,
        out_shape=[
            jax.ShapeDtypeStruct((CELLS, CH), BF),
            jax.ShapeDtypeStruct((2, CHUNKS, 16, CH), BF),
            jax.ShapeDtypeStruct((DEV, CAP, CH), BF),
        ],
        in_specs=[anywhere, anywhere, anywhere, pl.BlockSpec(memory_space=pltpu.VMEM), anywhere],
        out_specs=[anywhere] * 3,
        scratch_shapes=scratch,
        compiler_params=pltpu.CompilerParams(has_side_effects=True, vmem_limit_bytes=60 * 2**20),
        name="fused",
    )(feat, meta, kern, bias, cot)


def body(features, offsets, counts, cell_index, kern, conv_bias, cotangent):
    live = jnp.arange(CAP, dtype=jnp.int32)[:, None] < counts[0][None, :]
    radius = offsets[0, 0] * offsets[0, 0] + offsets[1, 0] * offsets[1, 0]
    weights = jnp.where(live, jnp.exp(-2.0 * radius), 0.0)
    row = (cell_index[0] // COLS).astype(F32)
    col = (cell_index[0] % COLS).astype(F32)
    meta = jnp.concatenate([weights, row, col, jnp.zeros((128 - 3 * CAP, DEV), F32)], 0).T.reshape(DEV, 1, 128)
    feat = jnp.transpose(features[0], (1, 0, 2))
    encoded, sums, ret = fused(
        feat, meta, kern.reshape(3, 3 * CH, CH), conv_bias.reshape(1, CH), cotangent.reshape(CELLS, CH)
    )
    scale = 1.0 / math.sqrt(CELLS * DEV)
    taps = sums[:, : CHUNKS - 1].reshape(2, 3, 3, 128, CH).transpose(1, 2, 0, 3, 4).reshape(3, 3, CH, CH)
    weight_grad = taps.astype(F32) * scale
    bias_grad = sums[0, CHUNKS - 1, 0].astype(F32) * scale
    obs_grad = jnp.transpose(ret, (1, 0, 2))[None]
    return encoded.reshape(ROWS, COLS, CH), weight_grad, bias_grad, obs_grad


def solution(mesh):
    return jax.shard_map(
        body,
        mesh=mesh,
        in_specs=(
            P(("lat", "lon"), None, None, None),
            P(None, ("lat", "lon"), None, None),
            P(("lat", "lon"), None),
            P(("lat", "lon"), None, None),
            P(),
            P(),
            P("lat", "lon", None),
        ),
        out_specs=(P("lat", "lon", None), P(), P(), P(("lat", "lon"), None, None, None)),
        check_vma=False,
    )
```

```python
import functools
import math

import jax
import jax.numpy as jnp
from jax import lax
from jax.experimental import pallas as pl
from jax.experimental.pallas import tpu as pltpu
from jax.sharding import PartitionSpec as P

BF = jnp.bfloat16
F32 = jnp.float32
MESH = pl.DeviceIdType.MESH
ROWS, COLS, CH, CAP = 32, 128, 256, 16
NLAT, NLON = 8, 16
DEV = NLAT * NLON
SLOTS = DEV * CAP
CELLS = ROWS * COLS
PAIRS = DEV // 2
CHIPS = NLON // 2
CHUNKS = 72


def iota(shape, dim):
    return lax.broadcasted_iota(jnp.int32, shape, dim)


def fiota(shape, dim):
    return iota(shape, dim).astype(F32)


def aligned(value, unit=128):
    return pl.multiple_of(value, unit)


def remote(src, dst, send, recv, lat, lon):
    return pltpu.make_async_remote_copy(
        src_ref=src, dst_ref=dst, send_sem=send, recv_sem=recv, device_id=(lat, lon), device_id_type=MESH
    )


def wait_bytes(ref, sem):
    pltpu.make_async_copy(ref, ref, sem).wait()


def expand_lanes(meta, onehot, wrf, wrb, dens, edges, edge_inv):
    per_dev = meta[...].reshape(DEV, 128).astype(BF)
    lane = iota((128, 384), 1)
    pick = jnp.where(iota((128, 384), 0) == (lane // 128) * CAP + lane % CAP, 1.0, 0.0).astype(BF)
    spread = jnp.dot(per_dev, pick, preferred_element_type=F32).reshape(16, 8, 384)
    lane8 = iota((8, 384), 1)
    mine = jnp.where(iota((8, 384), 0) == (lane8 % 128) // CAP, 1.0, 0.0)
    flat = (spread * mine[None]).sum(1)
    total = jnp.zeros((2 * ROWS, 128), F32)
    for g in range(16):
        wide = slice(g * 128, g * 128 + 128)
        w, row, col = flat[g : g + 1, 0:128], flat[g : g + 1, 128:256], flat[g : g + 1, 256:384]
        onehot[:, wide] = jnp.where(fiota((COLS, 128), 0) == col, 1.0, 0.0).astype(BF)
        by_row = jnp.where(fiota((ROWS, 128), 0) == row, w, 0.0)
        wrf[:, wide] = by_row
        first = jnp.where(col == 0.0, by_row, 0.0)
        last = jnp.where(col == float(COLS - 1), by_row, 0.0)
        both = jnp.concatenate([first, last], 0)
        edges[:, wide] = both.astype(BF)
        total = total + both
    edge_inv[...] = jnp.broadcast_to(1.0 / (total.sum(1, keepdims=True) + 1.0), (2 * ROWS, 128))

    def widen(r, _):
        wrb[r] = jnp.broadcast_to(wrf[pl.ds(r, 1), :], (16, SLOTS)).astype(BF)
        return 0

    lax.fori_loop(0, ROWS, widen, 0)
    density = lax.dot_general(
        onehot[...], wrf[...].astype(BF), (((1,), (1,)), ((), ())), preferred_element_type=F32
    )
    inv = 1.0 / (density + 1.0)
    for r in range(ROWS):
        dens[r * COLS : (r + 1) * COLS, :] = jnp.broadcast_to(inv[:, r : r + 1], (COLS, 128))


def expand_rows(meta, col_weight, row_of):
    lane = iota((128, 384), 1)
    pick = jnp.where(iota((128, 384), 0) // CAP == lane // 128, 1.0, 0.0).astype(BF)
    slot_lane = iota((CAP, 128), 1)
    mine = jnp.where(slot_lane % CAP == iota((CAP, 128), 0), 1.0, 0.0)

    def step(i, _):
        block = meta[pl.ds(i * 16, 16)]
        masked = (jnp.broadcast_to(block, (16, CAP, 128)) * mine[None]).reshape(256, 128).astype(BF)
        spread = jnp.dot(masked, pick, preferred_element_type=F32)
        base = aligned(i * 256, 256)
        col_weight[pl.ds(base, 256), :] = jnp.where(
            spread[:, 256:384] == fiota((256, 128), 1), spread[:, 0:128], 0.0
        ).astype(BF)
        row_of[pl.ds(base, 256), :] = spread[:, 128:256].astype(BF)
        return 0

    lax.fori_loop(0, DEV // 16, step, 0)


def twice(inv):
    return jnp.concatenate([inv, inv], 1)


def splat_edges(feats, onehot, wrb, dens, edges, edge_inv, rows_out, cols_out):
    hot = onehot[...].reshape(8, 16, SLOTS)
    lhs = jnp.concatenate(
        [(hot * wrb[0][None]).reshape(COLS, SLOTS), (hot * wrb[ROWS - 1][None]).reshape(COLS, SLOTS), edges[...]], 0
    )
    acc = jnp.dot(lhs, feats[...].reshape(SLOTS, CH), preferred_element_type=F32)
    rows_out[0] = (acc[0:COLS] * twice(dens[0:COLS, :])).astype(BF)
    rows_out[1] = (acc[COLS : 2 * COLS] * twice(dens[CELLS - COLS : CELLS, :])).astype(BF)
    cols = (acc[2 * COLS :] * twice(edge_inv[...])).astype(BF)
    cols_out[0] = cols[0:ROWS]
    cols_out[1] = cols[ROWS:]


def splat(feats, onehot, wrb, dens, x3, per=4):
    def step(i, _):
        r0 = i * per
        hot = onehot[...].reshape(8, 16, SLOTS)
        lhs = jnp.concatenate([(hot * wrb[r0 + k][None]).reshape(COLS, SLOTS) for k in range(per)], 0)
        acc = jnp.dot(lhs, feats[...].reshape(SLOTS, CH), preferred_element_type=F32)
        for k in range(per):
            base = aligned((r0 + k) * COLS)
            field = (acc[k * COLS : (k + 1) * COLS] * twice(dens[pl.ds(base, COLS), :])).astype(BF)
            wide = field.astype(F32)
            x3[pl.ds(base + COLS, COLS), 256:512] = field
            x3[pl.ds(base + COLS, COLS), 0:256] = pltpu.roll(wide, 1, 0).astype(BF)
            x3[pl.ds(base + COLS, COLS), 512:768] = pltpu.roll(wide, COLS - 1, 0).astype(BF)
        return 0

    lax.fori_loop(0, ROWS // per, step, 0)


def exchange_edges(lat, lon, rows, cols, h_row, h_col, h_cor, sems):
    up, down = lax.rem(lat + NLAT - 1, NLAT), lax.rem(lat + 1, NLAT)
    west, east = lax.rem(lon + NLON - 1, NLON), lax.rem(lon + 1, NLON)
    plan = (
        (rows[0], h_row.at[1], up, lon),
        (rows[1], h_row.at[0], down, lon),
        (cols.at[0], h_col.at[1], lat, west),
        (cols.at[1], h_col.at[0], lat, east),
        (cols.at[1, pl.ds(16, 16)], h_cor.at[0], down, east),
        (cols.at[0, pl.ds(16, 16)], h_cor.at[1], down, west),
        (cols.at[1, pl.ds(0, 16)], h_cor.at[2], up, east),
        (cols.at[0, pl.ds(0, 16)], h_cor.at[3], up, west),
    )
    return [remote(s, d, sems.at[0, i], sems.at[1, i], a, b) for i, (s, d, a, b) in enumerate(plan)]


def patch(arr, lat, h_row, h_col, h_cor, col_vals, left, right):
    top = jnp.where(lat == 0, 0.0, 1.0)
    bottom = jnp.where(lat == NLAT - 1, 0.0, 1.0)
    for side in range(2):
        col_vals[side, 0:32, :] = h_col[side].astype(F32)
        col_vals[side, 32:40, :] = jnp.broadcast_to(h_cor[side].astype(F32)[15:16] * top, (8, CH))
        col_vals[side, 40:48, :] = jnp.broadcast_to(h_cor[2 + side].astype(F32)[0:1] * bottom, (8, CH))
    sub = iota((16, CH), 0)

    def step(r, _):
        base = aligned((r + 1) * COLS)
        old = arr[pl.ds(base, 16), left : left + CH].astype(F32)
        arr[pl.ds(base, 16), left : left + CH] = jnp.where(sub == 0, col_vals[0, pl.ds(r, 1), :], old).astype(BF)
        far = aligned(base + COLS - 16, 16)
        old = arr[pl.ds(far, 16), right : right + CH].astype(F32)
        arr[pl.ds(far, 16), right : right + CH] = jnp.where(sub == 15, col_vals[1, pl.ds(r, 1), :], old).astype(BF)
        return 0

    lax.fori_loop(0, ROWS, step, 0)
    full = iota((COLS, CH), 0)
    for side, (base, keep) in enumerate(((0, top), ((ROWS + 1) * COLS, bottom))):
        at = 32 + 8 * side
        wide = h_row[side].astype(F32) * keep
        arr[base : base + COLS, 256:512] = wide.astype(BF)
        arr[base : base + COLS, left : left + CH] = jnp.where(
            full == 0, col_vals[0, at : at + 1, :], pltpu.roll(wide, 1, 0)
        ).astype(BF)
        arr[base : base + COLS, right : right + CH] = jnp.where(
            full == COLS - 1, col_vals[1, at : at + 1, :], pltpu.roll(wide, COLS - 1, 0)
        ).astype(BF)


def conv(x3, kc, bias, cot, enc, g3, gsum, gcol, per=4):
    gsum[...] = jnp.zeros_like(gsum)

    def step(i, _):
        r0 = i * per
        acc = jnp.broadcast_to(bias[...], (per * COLS, CH))
        for a in range(3):
            acc = acc + jnp.dot(
                x3[pl.ds(aligned((r0 + a) * COLS), per * COLS), :], kc[a], preferred_element_type=F32
            )
        base = aligned(r0 * COLS)
        gate = 0.5 * jnp.tanh(0.5 * acc) + 0.5
        silu = acc * gate
        field = x3[pl.ds(base + COLS, per * COLS), 256:512].astype(F32)
        enc[pl.ds(base, per * COLS), :] = (field + silu).astype(BF)
        grad = (cot[pl.ds(base, per * COLS), :].astype(F32) * (gate + silu * (1.0 - gate))).astype(BF)
        wide = grad.astype(F32)
        gsum[...] += wide.reshape(per * COLS // 8, 8, CH).sum(0)
        g3[pl.ds(base + COLS, per * COLS), 256:512] = grad
        for k in range(per):
            row = wide[k * COLS : (k + 1) * COLS]
            at = pl.ds(base + COLS + k * COLS, COLS)
            g3[at, 0:256] = pltpu.roll(row, COLS - 1, 0).astype(BF)
            g3[at, 512:768] = pltpu.roll(row, 1, 0).astype(BF)
            gcol[0, pl.ds(r0 + k, 1), :] = row[0:1]
            gcol[1, pl.ds(r0 + k, 1), :] = row[COLS - 1 : COLS]
        return 0

    lax.fori_loop(0, ROWS // per, step, 0)


def wgrad_tap(tap, x3, g3, dw):
    a, b = tap // 3, tap % 3
    dw[tap * CH : (tap + 1) * CH, :] = lax.dot_general(
        x3[a * COLS : a * COLS + CELLS, b * CH : (b + 1) * CH], g3[COLS : COLS + CELLS, CH : 2 * CH],
        (((0,), (0,)), ((), ())), preferred_element_type=F32,
    )


def grad_band(i, col_weight, row_of, scaled, slot_grad):
    base = aligned(i * 256, 256)
    weight, row = col_weight[pl.ds(base, 256), :], row_of[pl.ds(base, 256), :]
    lhs = jnp.concatenate(
        [jnp.where(row == jnp.array(r, BF), weight, jnp.zeros_like(weight)) for r in range(ROWS)], 1
    )
    grads = jnp.dot(lhs, scaled[...], preferred_element_type=F32).astype(BF)
    slot_grad[pl.ds(i * 16, 16)] = grads.reshape(16, CAP, CH)


def transpose_kernel(kc, kt):
    for a in range(3):
        for b in range(3):
            kt[a, b * CH : (b + 1) * CH, :] = kc[a, b * CH : (b + 1) * CH, :].T


def back_conv(g3, kt, cot, dens, scaled, per=4):
    def step(i, _):
        r0 = i * per
        base = aligned(r0 * COLS)
        acc = cot[pl.ds(base, per * COLS), :].astype(F32)
        for a in range(3):
            acc = acc + jnp.dot(
                g3[pl.ds(aligned((r0 + 2 - a) * COLS), per * COLS), :], kt[a], preferred_element_type=F32
            )
        scaled[pl.ds(base, per * COLS), :] = (acc * twice(dens[pl.ds(base, per * COLS), :])).astype(BF)
        return 0

    lax.fori_loop(0, ROWS // per, step, 0)


def place(p):
    q = lax.rem(p, 16)
    a = q // 2
    return a, lax.rem(2 * (p // 16 + a) + lax.rem(q, 2), NLON)


def spread_over(j):
    b = lax.rem(j, CHIPS)
    return lax.rem(j // CHIPS + b, NLAT), b


def first_chunk(lat, chip):
    rank = lax.rem(chip - lat + CHIPS, CHIPS)
    return rank, 9 * lat + rank + jnp.where(rank > 0, 1, 0)


def slot_meta(offsets, counts, cells, turned, meta_src):
    live = iota((CAP, DEV), 0) < counts[...]
    radius = offsets[0] * offsets[0] + offsets[1] * offsets[1]
    weight = jnp.where(live, jnp.exp(-2.0 * radius), 0.0)
    row, col = cells[...] // COLS, cells[...] % COLS
    table = jnp.concatenate([weight, row.astype(F32), col.astype(F32), jnp.zeros((128 - 3 * CAP, DEV), F32)], 0)
    turned[...] = table.T

    def step(t, _):
        meta_src[lax.rem(t, NLON), t // NLON] = turned[pl.ds(t, 1), :]
        return 0

    lax.fori_loop(0, DEV, step, 0, unroll=8)


def turn_slots(by_slot, wide, by_dest):
    flat = by_slot[...].reshape(SLOTS, CH).astype(F32)
    wide[0], wide[1] = flat[:, :128], flat[:, 128:]

    def step(t, _):
        halves = [wide[h, pl.ds(t, CAP, stride=DEV), :] for h in range(2)]
        by_dest[t] = jnp.concatenate(halves, 1).astype(BF)
        return 0

    lax.fori_loop(0, DEV, step, 0, unroll=8)


def kernel(
    feat_in, offsets, counts, cells, kern_in, bias, cot_in,
    enc_out, sums_out, ret_out, bias_out,
    by_slot, wide, by_dest, turned, meta_src, meta_mid, meta_nat,
    feats, meta, kc, kt, cot, enc, onehot, wrf, wrb, dens, edges, edge_inv, col_weight, row_of,
    edge_rows, edge_cols, h_row, h_col, h_cor, col_vals, x3, g3, gsum, gcol, grad_cols, scaled, slot_grad,
    dw, pair_dw, pair_sum, half, rs, reduced, bias_lat, bias_mid, bias_lon,
    round_sem, load_sems, a2a_sems, halo_sems, grad_halo_sems, pair_sems, rs_sems, ag_sems, swap_sems, ret_sems, bias_sems,
):
    lat, lon = lax.axis_index("lat"), lax.axis_index("lon")
    me = lat * NLON + lon
    core = lax.rem(lon, 2)
    mate = lon + 1 - 2 * core
    chip = lon // 2
    owner = lat * CHIPS + chip
    rank, mine = first_chunk(lat, chip)

    def over_lat(j):
        return lax.rem(lat + j, NLAT)

    def over_lon(j):
        return lax.rem(lon + j, NLON)

    load_feat = pltpu.make_async_copy(feat_in, by_slot, load_sems.at[1])
    load_kern = pltpu.make_async_copy(kern_in, kc, load_sems.at[2])
    load_cot = pltpu.make_async_copy(cot_in, cot, load_sems.at[3])
    load_feat.start()
    load_kern.start()
    load_cot.start()

    barrier = pltpu.get_barrier_semaphore()

    def greet_lon(j, _):
        pl.semaphore_signal(barrier, inc=1, device_id=(lat, over_lon(j)), device_id_type=MESH)
        return 0

    def greet_lat(j, _):
        pl.semaphore_signal(barrier, inc=1, device_id=(over_lat(j), lon), device_id_type=MESH)
        return 0

    def vouch(j, _):
        pl.semaphore_signal(round_sem, inc=1, device_id=(over_lat(j), lon), device_id_type=MESH)
        return 0

    lax.fori_loop(1, NLON, greet_lon, 0)
    lax.fori_loop(1, NLAT, greet_lat, 0)
    slot_meta(offsets, counts, cells, turned, meta_src)
    load_feat.wait()
    turn_slots(by_slot, wide, by_dest)
    pl.semaphore_wait(barrier, NLON + NLAT - 2)
    lax.fori_loop(1, NLAT, vouch, 0)

    def meta_lon(j, _):
        to = over_lon(j)
        remote(meta_src.at[to], meta_mid.at[lon], a2a_sems.at[0], a2a_sems.at[1], lat, to).start()
        return 0

    def meta_lat(j, _):
        to = over_lat(j)
        remote(meta_mid.at[pl.ds(0, NLON), to], meta_nat.at[lat], a2a_sems.at[2], a2a_sems.at[3], to, lon).start()
        return 0

    def send_feats(p, _):
        a, b = place(p)
        to_lat, to_lon = lax.rem(lat - a + NLAT, NLAT), lax.rem(lon - b + NLON, NLON)
        remote(by_dest.at[to_lat * NLON + to_lon], feats.at[p], a2a_sems.at[4], a2a_sems.at[5], to_lat, to_lon).start()
        return 0

    lax.fori_loop(1, NLON, meta_lon, 0)
    meta_mid[lon] = meta_src[lon]
    pl.semaphore_wait(round_sem, NLAT - 1)
    lax.fori_loop(1, DEV // 2, send_feats, 0)
    wait_bytes(meta_mid.at[pl.ds(0, NLON - 1)], a2a_sems.at[1])
    lax.fori_loop(1, NLAT, meta_lat, 0)
    meta_nat[lat] = meta_mid[:, lat]
    lax.fori_loop(DEV // 2, DEV, send_feats, 0)
    feats[0] = by_dest[me]

    load_kern.wait()
    transpose_kernel(kc, kt)
    wait_bytes(meta_nat.at[pl.ds(0, NLAT - 1)], a2a_sems.at[3])

    def reorder(p, _):
        a, b = place(p)
        meta[p] = meta_nat[over_lat(a), over_lon(b)]
        return 0

    lax.fori_loop(0, DEV, reorder, 0, unroll=4)
    expand_lanes(meta, onehot, wrf, wrb, dens, edges, edge_inv)
    expand_rows(meta, col_weight, row_of)

    wait_bytes(feats.at[pl.ds(0, DEV - 1)], a2a_sems.at[5])
    splat_edges(feats, onehot, wrb, dens, edges, edge_inv, edge_rows, edge_cols)
    halo = exchange_edges(
        lat, lon, (edge_rows.at[0], edge_rows.at[1]), edge_cols, h_row.at[0], h_col.at[0], h_cor.at[0], halo_sems
    )
    for copy in halo:
        copy.start()
    splat(feats, onehot, wrb, dens, x3)
    for copy in halo:
        copy.wait_recv()
    patch(x3, lat, h_row.at[0], h_col.at[0], h_cor.at[0], col_vals, 0, 512)

    load_cot.wait()
    conv(x3, kc, bias, cot, enc, g3, gsum, gcol)
    store_enc = pltpu.make_async_copy(enc, enc_out, load_sems.at[4])
    store_enc.start()
    grad_cols[...] = gcol[...].astype(BF)
    last = ROWS * COLS
    grad_halo = exchange_edges(
        lat, lon, (g3.at[pl.ds(COLS, COLS), pl.ds(CH, CH)], g3.at[pl.ds(last, COLS), pl.ds(CH, CH)]),
        grad_cols, h_row.at[1], h_col.at[1], h_cor.at[1], grad_halo_sems,
    )
    for copy in grad_halo:
        copy.start()

    pair = [remote(gsum, pair_sum, pair_sems.at[0, 9], pair_sems.at[1, 9], lat, mate)]
    pair[0].start()
    for tap in range(9):
        wgrad_tap(tap, x3, g3, dw)
        pair.append(
            remote(
                dw.at[pl.ds(aligned(tap * CH + 128 * (1 - core)), 128)], pair_dw.at[pl.ds(tap * 128, 128)],
                pair_sems.at[0, tap], pair_sems.at[1, tap], lat, mate,
            )
        )
        pair[-1].start()

    for copy in grad_halo:
        copy.wait()
    patch(g3, lat, h_row.at[1], h_col.at[1], h_cor.at[1], col_vals, 512, 0)

    pair[0].wait()
    bias_lat[lat] = gsum[...] + pair_sum[...]
    for tap in range(9):
        pair[tap + 1].wait()
        total = dw[pl.ds(aligned(tap * CH + 128 * core), 128), :] + pair_dw[tap * 128 : (tap + 1) * 128, :]
        half[tap * 8 : (tap + 1) * 8] = total.astype(BF).reshape(8, 16, CH)

    def send_chunk(j, _):
        a, b = spread_over(j)
        to_lat, to_chip = over_lat(a), lax.rem(chip + b, CHIPS)
        to_rank, at = first_chunk(to_lat, to_chip)

        def send(count):
            remote(
                half.at[pl.ds(at, count)], rs.at[owner, pl.ds(0, count)], rs_sems.at[0], rs_sems.at[1],
                to_lat, to_chip * 2 + core,
            ).start()

        @pl.when(to_rank == 0)
        def _():
            send(2)

        @pl.when(to_rank != 0)
        def _():
            send(1)

        return 0

    def send_bias_lat(j, _):
        remote(bias_lat.at[lat], bias_lat.at[lat], bias_sems.at[0], bias_sems.at[1], over_lat(j), lon).start()
        return 0

    lax.fori_loop(1, PAIRS, send_chunk, 0)
    lax.fori_loop(1, NLAT, send_bias_lat, 0)
    rs[owner, 0] = half[mine]

    @pl.when(rank == 0)
    def _():
        rs[owner, 1] = half[mine + 1]

    back_conv(g3, kt, cot, dens, scaled)

    def send_sum(count):
        spot = sums_out.at[core, pl.ds(mine, count)]
        own = pltpu.make_async_copy(reduced.at[pl.ds(0, count)], spot, load_sems.at[5])
        own.start()

        def step(j, _):
            a, b = spread_over(j)
            to_chip = lax.rem(chip + b, CHIPS)
            remote(
                reduced.at[pl.ds(0, count)], spot, ag_sems.at[0], ag_sems.at[1], over_lat(a), to_chip * 2 + core
            ).start()
            return 0

        lax.fori_loop(1, PAIRS, step, 0)

    @pl.when(rank == 0)
    def _():
        wait_bytes(rs.at[pl.ds(0, PAIRS - 1)], rs_sems.at[1])
        reduced[...] = rs[...].astype(F32).sum(0).astype(BF)
        send_sum(2)

    @pl.when(rank != 0)
    def _():
        wait_bytes(half.at[pl.ds(0, PAIRS - 1)], rs_sems.at[1])
        reduced[0] = rs[:, 0].astype(F32).sum(0).astype(BF)
        send_sum(1)

    wait_bytes(bias_lat.at[pl.ds(0, NLAT - 1)], bias_sems.at[1])
    bias_mid[...] = bias_lat[...].sum(0)
    bias_lon[chip] = bias_mid[...]

    def send_bias_lon(j, _):
        to_chip = lax.rem(chip + j, CHIPS)
        remote(bias_mid, bias_lon.at[chip], bias_sems.at[2], bias_sems.at[3], lat, to_chip * 2 + core).start()
        return 0

    lax.fori_loop(1, CHIPS, send_bias_lon, 0)

    def band(i, _):
        grad_band(i, col_weight, row_of, scaled, slot_grad)

        def back(j, _):
            p = i * 16 + j
            a, b = place(p)

            @pl.when(p != 0)
            def _():
                remote(
                    slot_grad.at[p], ret_out.at[me], ret_sems.at[0], ret_sems.at[1], over_lat(a), over_lon(b)
                ).start()

            return 0

        lax.fori_loop(0, 16, back, 0)
        return 0

    lax.fori_loop(0, DEV // 16, band, 0)
    own_ret = pltpu.make_async_copy(slot_grad.at[0], ret_out.at[me], load_sems.at[7])
    own_ret.start()

    @pl.when(rank == 0)
    def _():
        pltpu.make_async_copy(reduced, sums_out.at[core, pl.ds(mine, 2)], load_sems.at[5]).wait()
        wait_bytes(sums_out.at[core, pl.ds(0, CHUNKS - 2)], ag_sems.at[1])
        wait_bytes(rs.at[pl.ds(0, PAIRS - 1)], ag_sems.at[0])
        wait_bytes(half.at[pl.ds(0, CHUNKS - 2)], rs_sems.at[0])

    @pl.when(rank != 0)
    def _():
        pltpu.make_async_copy(reduced.at[pl.ds(0, 1)], sums_out.at[core, pl.ds(mine, 1)], load_sems.at[5]).wait()
        wait_bytes(sums_out.at[core, pl.ds(0, CHUNKS - 1)], ag_sems.at[1])
        wait_bytes(half.at[pl.ds(0, PAIRS - 1)], ag_sems.at[0])
        wait_bytes(half.at[pl.ds(0, CHUNKS - 1)], rs_sems.at[0])

    swap = remote(sums_out.at[core], sums_out.at[core], swap_sems.at[0], swap_sems.at[1], lat, mate)
    swap.start()
    wait_bytes(bias_lon.at[pl.ds(0, CHIPS - 1)], bias_sems.at[3])
    bias_out[...] = bias_lon[...].sum(0).sum(0, keepdims=True)

    wait_bytes(meta_mid.at[pl.ds(0, NLON - 1)], a2a_sems.at[0])
    wait_bytes(meta_nat.at[pl.ds(0, NLAT - 1)], a2a_sems.at[2])
    wait_bytes(feats.at[pl.ds(0, DEV - 1)], a2a_sems.at[4])
    wait_bytes(bias_lat.at[pl.ds(0, NLAT - 1)], bias_sems.at[0])
    wait_bytes(bias_lon.at[pl.ds(0, CHIPS - 1)], bias_sems.at[2])
    for copy in halo:
        copy.wait_send()
    store_enc.wait()
    own_ret.wait()
    wait_bytes(slot_grad.at[pl.ds(0, DEV - 1)], ret_sems.at[0])
    wait_bytes(ret_out.at[pl.ds(0, DEV - 1)], ret_sems.at[1])
    swap.wait()


def fused(feat, offsets, counts, cells, kern, bias, cot):
    vm = pltpu.VMEM
    dma = pltpu.SemaphoreType.DMA
    scratch = [
        vm((CAP, DEV, CH), BF),
        vm((2, SLOTS, 128), F32),
        vm((DEV, CAP, CH), BF),
        vm((DEV, 128), F32),
        vm((NLON, NLAT, 1, 128), F32),
        vm((NLON, NLAT, 1, 128), F32),
        vm((NLAT, NLON, 1, 128), F32),
        vm((DEV, CAP, CH), BF),
        vm((DEV, 1, 128), F32),
        vm((3, 3 * CH, CH), BF),
        vm((3, 3 * CH, CH), BF),
        vm((CELLS, CH), BF),
        vm((CELLS, CH), BF),
        vm((COLS, SLOTS), BF),
        vm((ROWS, SLOTS), F32),
        vm((ROWS, 16, SLOTS), BF),
        vm((CELLS, 128), F32),
        vm((2 * ROWS, SLOTS), BF),
        vm((2 * ROWS, 128), F32),
        vm((SLOTS, 128), BF),
        vm((SLOTS, 128), BF),
        vm((2, COLS, CH), BF),
        vm((2, ROWS, CH), BF),
        vm((2, 2, COLS, CH), BF),
        vm((2, 2, ROWS, CH), BF),
        vm((2, 4, 16, CH), BF),
        vm((2, 48, CH), F32),
        vm(((ROWS + 2) * COLS, 3 * CH), BF),
        vm(((ROWS + 2) * COLS, 3 * CH), BF),
        vm((8, CH), F32),
        vm((2, ROWS, CH), F32),
        vm((2, ROWS, CH), BF),
        vm((CELLS, CH), BF),
        vm((DEV, CAP, CH), BF),
        vm((9 * CH, CH), F32),
        vm((9 * 128, CH), F32),
        vm((8, CH), F32),
        vm((CHUNKS, 16, CH), BF),
        vm((PAIRS, 2, 16, CH), BF),
        vm((2, 16, CH), BF),
        vm((NLAT, 8, CH), F32),
        vm((8, CH), F32),
        vm((CHIPS, 8, CH), F32),
        pltpu.SemaphoreType.REGULAR,
        dma((8,)),
        dma((6,)),
        dma((2, 8)),
        dma((2, 8)),
        dma((2, 10)),
        dma((2,)),
        dma((2,)),
        dma((2,)),
        dma((2,)),
        dma((4,)),
    ]
    anywhere = pl.BlockSpec(memory_space=pl.ANY)
    local = pl.BlockSpec(memory_space=pltpu.VMEM)
    return pl.pallas_call(
        kernel,
        out_shape=[
            jax.ShapeDtypeStruct((CELLS, CH), BF),
            jax.ShapeDtypeStruct((2, CHUNKS, 16, CH), BF),
            jax.ShapeDtypeStruct((DEV, CAP, CH), BF),
            jax.ShapeDtypeStruct((1, CH), F32),
        ],
        in_specs=[anywhere, local, local, local, anywhere, local, anywhere],
        out_specs=[anywhere, anywhere, anywhere, local],
        scratch_shapes=scratch,
        compiler_params=pltpu.CompilerParams(collective_id=0, has_side_effects=True, vmem_limit_bytes=60 * 2**20),
        name="fused",
    )(feat, offsets, counts, cells, kern, bias, cot)


def body(features, offsets, counts, cell_index, kern, conv_bias, cotangent):
    encoded, sums, ret, bias_sum = fused(
        features[0], offsets[:, 0], counts, cell_index[0], kern.reshape(3, 3 * CH, CH),
        conv_bias.reshape(1, CH), cotangent.reshape(CELLS, CH),
    )
    scale = 1.0 / math.sqrt(CELLS * DEV)
    taps = sums.reshape(2, 3, 3, 128, CH).transpose(1, 2, 0, 3, 4).reshape(3, 3, CH, CH)
    weight_grad = taps.astype(F32) * scale
    bias_grad = bias_sum[0] * scale
    obs_grad = jnp.transpose(ret, (1, 0, 2))[None]
    return encoded.reshape(ROWS, COLS, CH), weight_grad, bias_grad, obs_grad


def solution(mesh):
    return jax.shard_map(
        body,
        mesh=mesh,
        in_specs=(
            P(("lat", "lon"), None, None, None),
            P(None, ("lat", "lon"), None, None),
            P(("lat", "lon"), None),
            P(("lat", "lon"), None, None),
            P(),
            P(),
            P("lat", "lon", None),
        ),
        out_specs=(P("lat", "lon", None), P(), P(), P(("lat", "lon"), None, None, None)),
        check_vma=False,
    )
```

```python
import functools
import math

import jax
import jax.numpy as jnp
from jax import lax
from jax.experimental import pallas as pl
from jax.experimental.pallas import tpu as pltpu
from jax.sharding import PartitionSpec as P

BF = jnp.bfloat16
F32 = jnp.float32
MESH = pl.DeviceIdType.MESH
ROWS, COLS, CH, CAP = 32, 128, 256, 16
NLAT, NLON = 8, 16
DEV = NLAT * NLON
SLOTS = DEV * CAP
CELLS = ROWS * COLS
PAIRS = DEV // 2
CHIPS = NLON // 2
CHUNKS = 72
TAPS = 9
LAG = 2


def iota(shape, dim):
    return lax.broadcasted_iota(jnp.int32, shape, dim)


def fiota(shape, dim):
    return iota(shape, dim).astype(F32)


def aligned(value, unit=128):
    return pl.multiple_of(value, unit)


def remote(src, dst, send, recv, lat, lon):
    return pltpu.make_async_remote_copy(
        src_ref=src, dst_ref=dst, send_sem=send, recv_sem=recv, device_id=(lat, lon), device_id_type=MESH
    )


def wait_bytes(ref, sem):
    pltpu.make_async_copy(ref, ref, sem).wait()


def expand_lanes(meta, onehot, wrf, wrb, dens, edges, edge_inv):
    per_dev = meta[...].reshape(DEV, 128).astype(BF)
    lane = iota((128, 384), 1)
    pick = jnp.where(iota((128, 384), 0) == (lane // 128) * CAP + lane % CAP, 1.0, 0.0).astype(BF)
    spread = jnp.dot(per_dev, pick, preferred_element_type=F32).reshape(16, 8, 384)
    lane8 = iota((8, 384), 1)
    mine = jnp.where(iota((8, 384), 0) == (lane8 % 128) // CAP, 1.0, 0.0)
    flat = (spread * mine[None]).sum(1)
    total = jnp.zeros((2 * ROWS, 128), F32)
    for g in range(16):
        wide = slice(g * 128, g * 128 + 128)
        w, row, col = flat[g : g + 1, 0:128], flat[g : g + 1, 128:256], flat[g : g + 1, 256:384]
        onehot[:, wide] = jnp.where(fiota((COLS, 128), 0) == col, 1.0, 0.0).astype(BF)
        by_row = jnp.where(fiota((ROWS, 128), 0) == row, w, 0.0)
        wrf[:, wide] = by_row
        first = jnp.where(col == 0.0, by_row, 0.0)
        last = jnp.where(col == float(COLS - 1), by_row, 0.0)
        both = jnp.concatenate([first, last], 0)
        edges[:, wide] = both.astype(BF)
        total = total + both
    edge_inv[...] = jnp.broadcast_to(1.0 / (total.sum(1, keepdims=True) + 1.0), (2 * ROWS, 128))

    def widen(r, _):
        wrb[r] = jnp.broadcast_to(wrf[pl.ds(r, 1), :], (16, SLOTS)).astype(BF)
        return 0

    lax.fori_loop(0, ROWS, widen, 0)
    density = lax.dot_general(
        onehot[...], wrf[...].astype(BF), (((1,), (1,)), ((), ())), preferred_element_type=F32
    )
    inv = 1.0 / (density + 1.0)
    for r in range(ROWS):
        dens[r * COLS : (r + 1) * COLS, :] = jnp.broadcast_to(inv[:, r : r + 1], (COLS, 128))


def expand_rows(meta, col_weight, row_of):
    lane = iota((128, 384), 1)
    pick = jnp.where(iota((128, 384), 0) // CAP == lane // 128, 1.0, 0.0).astype(BF)
    slot_lane = iota((CAP, 128), 1)
    mine = jnp.where(slot_lane % CAP == iota((CAP, 128), 0), 1.0, 0.0)

    def step(i, _):
        block = meta[pl.ds(i * 16, 16)]
        masked = (jnp.broadcast_to(block, (16, CAP, 128)) * mine[None]).reshape(256, 128).astype(BF)
        spread = jnp.dot(masked, pick, preferred_element_type=F32)
        base = aligned(i * 256, 256)
        col_weight[pl.ds(base, 256), :] = jnp.where(
            spread[:, 256:384] == fiota((256, 128), 1), spread[:, 0:128], 0.0
        ).astype(BF)
        row_of[pl.ds(base, 256), :] = spread[:, 128:256].astype(BF)
        return 0

    lax.fori_loop(0, DEV // 16, step, 0)


def twice(inv):
    return jnp.concatenate([inv, inv], 1)


def splat_edges(feats, onehot, wrb, dens, edges, edge_inv, rows_out, cols_out):
    hot = onehot[...].reshape(8, 16, SLOTS)
    lhs = jnp.concatenate(
        [(hot * wrb[0][None]).reshape(COLS, SLOTS), (hot * wrb[ROWS - 1][None]).reshape(COLS, SLOTS), edges[...]], 0
    )
    acc = jnp.dot(lhs, feats[...].reshape(SLOTS, CH), preferred_element_type=F32)
    rows_out[0] = (acc[0:COLS] * twice(dens[0:COLS, :])).astype(BF)
    rows_out[1] = (acc[COLS : 2 * COLS] * twice(dens[CELLS - COLS : CELLS, :])).astype(BF)
    cols = (acc[2 * COLS :] * twice(edge_inv[...])).astype(BF)
    cols_out[0] = cols[0:ROWS]
    cols_out[1] = cols[ROWS:]


def splat(feats, onehot, wrb, dens, x3, per=4):
    def step(i, _):
        r0 = i * per
        hot = onehot[...].reshape(8, 16, SLOTS)
        lhs = jnp.concatenate([(hot * wrb[r0 + k][None]).reshape(COLS, SLOTS) for k in range(per)], 0)
        acc = jnp.dot(lhs, feats[...].reshape(SLOTS, CH), preferred_element_type=F32)
        for k in range(per):
            base = aligned((r0 + k) * COLS)
            field = (acc[k * COLS : (k + 1) * COLS] * twice(dens[pl.ds(base, COLS), :])).astype(BF)
            wide = field.astype(F32)
            x3[pl.ds(base + COLS, COLS), 256:512] = field
            x3[pl.ds(base + COLS, COLS), 0:256] = pltpu.roll(wide, 1, 0).astype(BF)
            x3[pl.ds(base + COLS, COLS), 512:768] = pltpu.roll(wide, COLS - 1, 0).astype(BF)
        return 0

    lax.fori_loop(0, ROWS // per, step, 0)


def exchange_edges(lat, lon, rows, cols, h_row, h_col, h_cor, sems):
    up, down = lax.rem(lat + NLAT - 1, NLAT), lax.rem(lat + 1, NLAT)
    west, east = lax.rem(lon + NLON - 1, NLON), lax.rem(lon + 1, NLON)
    plan = (
        (rows[0], h_row.at[1], up, lon),
        (rows[1], h_row.at[0], down, lon),
        (cols.at[0], h_col.at[1], lat, west),
        (cols.at[1], h_col.at[0], lat, east),
        (cols.at[1, pl.ds(16, 16)], h_cor.at[0], down, east),
        (cols.at[0, pl.ds(16, 16)], h_cor.at[1], down, west),
        (cols.at[1, pl.ds(0, 16)], h_cor.at[2], up, east),
        (cols.at[0, pl.ds(0, 16)], h_cor.at[3], up, west),
    )
    return [remote(s, d, sems.at[0, i], sems.at[1, i], a, b) for i, (s, d, a, b) in enumerate(plan)]


def patch(arr, lat, h_row, h_col, h_cor, col_vals, left, right):
    top = jnp.where(lat == 0, 0.0, 1.0)
    bottom = jnp.where(lat == NLAT - 1, 0.0, 1.0)
    for side in range(2):
        col_vals[side, 0:32, :] = h_col[side].astype(F32)
        col_vals[side, 32:40, :] = jnp.broadcast_to(h_cor[side].astype(F32)[15:16] * top, (8, CH))
        col_vals[side, 40:48, :] = jnp.broadcast_to(h_cor[2 + side].astype(F32)[0:1] * bottom, (8, CH))
    sub = iota((16, CH), 0)

    def step(r, _):
        base = aligned((r + 1) * COLS)
        old = arr[pl.ds(base, 16), left : left + CH].astype(F32)
        arr[pl.ds(base, 16), left : left + CH] = jnp.where(sub == 0, col_vals[0, pl.ds(r, 1), :], old).astype(BF)
        far = aligned(base + COLS - 16, 16)
        old = arr[pl.ds(far, 16), right : right + CH].astype(F32)
        arr[pl.ds(far, 16), right : right + CH] = jnp.where(sub == 15, col_vals[1, pl.ds(r, 1), :], old).astype(BF)
        return 0

    lax.fori_loop(0, ROWS, step, 0)
    full = iota((COLS, CH), 0)
    for side, (base, keep) in enumerate(((0, top), ((ROWS + 1) * COLS, bottom))):
        at = 32 + 8 * side
        wide = h_row[side].astype(F32) * keep
        arr[base : base + COLS, 256:512] = wide.astype(BF)
        arr[base : base + COLS, left : left + CH] = jnp.where(
            full == 0, col_vals[0, at : at + 1, :], pltpu.roll(wide, 1, 0)
        ).astype(BF)
        arr[base : base + COLS, right : right + CH] = jnp.where(
            full == COLS - 1, col_vals[1, at : at + 1, :], pltpu.roll(wide, COLS - 1, 0)
        ).astype(BF)


def conv(x3, kc, bias, cot, enc, g3, gsum, gcol, per=4):
    gsum[...] = jnp.zeros_like(gsum)

    def step(i, _):
        r0 = i * per
        acc = jnp.broadcast_to(bias[...], (per * COLS, CH))
        for a in range(3):
            acc = acc + jnp.dot(
                x3[pl.ds(aligned((r0 + a) * COLS), per * COLS), :], kc[a], preferred_element_type=F32
            )
        base = aligned(r0 * COLS)
        gate = 0.5 * jnp.tanh(0.5 * acc) + 0.5
        silu = acc * gate
        field = x3[pl.ds(base + COLS, per * COLS), 256:512].astype(F32)
        enc[pl.ds(base, per * COLS), :] = (field + silu).astype(BF)
        grad = (cot[pl.ds(base, per * COLS), :].astype(F32) * (gate + silu * (1.0 - gate))).astype(BF)
        wide = grad.astype(F32)
        gsum[...] += wide.reshape(per * COLS // 8, 8, CH).sum(0)
        g3[pl.ds(base + COLS, per * COLS), 256:512] = grad
        for k in range(per):
            row = wide[k * COLS : (k + 1) * COLS]
            at = pl.ds(base + COLS + k * COLS, COLS)
            g3[at, 0:256] = pltpu.roll(row, COLS - 1, 0).astype(BF)
            g3[at, 512:768] = pltpu.roll(row, 1, 0).astype(BF)
            gcol[0, pl.ds(r0 + k, 1), :] = row[0:1]
            gcol[1, pl.ds(r0 + k, 1), :] = row[COLS - 1 : COLS]
        return 0

    lax.fori_loop(0, ROWS // per, step, 0)


def wgrad_tap(step, tap, x3, g3, dw):
    rows, lanes = pl.ds(aligned(tap // 3 * COLS), CELLS), pl.ds(aligned(lax.rem(tap, 3) * CH), CH)
    dw[step] = lax.dot_general(
        x3[rows, lanes], g3[COLS : COLS + CELLS, CH : 2 * CH], (((0,), (0,)), ((), ())), preferred_element_type=F32
    )


def grad_band(i, col_weight, row_of, scaled, slot_grad):
    base = aligned(i * 256, 256)
    weight, row = col_weight[pl.ds(base, 256), :], row_of[pl.ds(base, 256), :]
    lhs = jnp.concatenate(
        [jnp.where(row == jnp.array(r, BF), weight, jnp.zeros_like(weight)) for r in range(ROWS)], 1
    )
    grads = jnp.dot(lhs, scaled[...], preferred_element_type=F32).astype(BF)
    slot_grad[pl.ds(i * 16, 16)] = grads.reshape(16, CAP, CH)


def transpose_kernel(kc, kt):
    for a in range(3):
        for b in range(3):
            kt[a, b * CH : (b + 1) * CH, :] = kc[a, b * CH : (b + 1) * CH, :].T


def back_conv(g3, kt, cot, dens, scaled, per=4):
    def step(i, _):
        r0 = i * per
        base = aligned(r0 * COLS)
        acc = cot[pl.ds(base, per * COLS), :].astype(F32)
        for a in range(3):
            acc = acc + jnp.dot(
                g3[pl.ds(aligned((r0 + 2 - a) * COLS), per * COLS), :], kt[a], preferred_element_type=F32
            )
        scaled[pl.ds(base, per * COLS), :] = (acc * twice(dens[pl.ds(base, per * COLS), :])).astype(BF)
        return 0

    lax.fori_loop(0, ROWS // per, step, 0)


def place(p):
    q = lax.rem(p, 16)
    a = q // 2
    return a, lax.rem(2 * (p // 16 + a) + lax.rem(q, 2), NLON)


def spread_over(j):
    b = lax.rem(j, CHIPS)
    return lax.rem(j // CHIPS + b, NLAT), b


def slot_meta(offsets, counts, cells, turned, meta_src):
    live = iota((CAP, DEV), 0) < counts[...]
    radius = offsets[0] * offsets[0] + offsets[1] * offsets[1]
    weight = jnp.where(live, jnp.exp(-2.0 * radius), 0.0)
    row, col = cells[...] // COLS, cells[...] % COLS
    table = jnp.concatenate([weight, row.astype(F32), col.astype(F32), jnp.zeros((128 - 3 * CAP, DEV), F32)], 0)
    turned[...] = table.T

    def step(t, _):
        meta_src[lax.rem(t, NLON), t // NLON] = turned[pl.ds(t, 1), :]
        return 0

    lax.fori_loop(0, DEV, step, 0, unroll=8)


def turn_slots(by_slot, wide, by_dest):
    flat = by_slot[...].reshape(SLOTS, CH).astype(F32)
    wide[0], wide[1] = flat[:, :128], flat[:, 128:]

    def step(t, _):
        halves = [wide[h, pl.ds(t, CAP, stride=DEV), :] for h in range(2)]
        by_dest[t] = jnp.concatenate(halves, 1).astype(BF)
        return 0

    lax.fori_loop(0, DEV, step, 0, unroll=8)


def kernel(
    feat_in, offsets, counts, cells, kern_in, bias, cot_in,
    enc_out, sums_out, ret_out, bias_out,
    by_slot, wide, by_dest, turned, meta_src, meta_mid, meta_nat,
    feats, meta, kc, kt, cot, enc, onehot, wrf, wrb, dens, edges, edge_inv, col_weight, row_of,
    edge_rows, edge_cols, h_row, h_col, h_cor, col_vals, x3, g3, gsum, gcol, grad_cols, scaled, slot_grad,
    dw, pair_dw, pair_sum, half, rs, reduced, bias_lat, bias_mid, bias_lon, tail_chip, tail_lat, tail_part, tail_sum,
    round_sem, load_sems, a2a_sems, halo_sems, grad_halo_sems, pair_sems, rs_sems, ag_sems, swap_sems, ret_sems, bias_sems, tail_sems,
):
    lat, lon = lax.axis_index("lat"), lax.axis_index("lon")
    me = lat * NLON + lon
    core = lax.rem(lon, 2)
    mate = lon + 1 - 2 * core
    chip = lon // 2
    owner = lat * CHIPS + chip
    mine = lax.rem(lat - chip + CHIPS, CHIPS) * CHIPS + chip

    def over_lat(j):
        return lax.rem(lat + j, NLAT)

    def over_lon(j):
        return lax.rem(lon + j, NLON)

    load_feat = pltpu.make_async_copy(feat_in, by_slot, load_sems.at[1])
    load_kern = pltpu.make_async_copy(kern_in, kc, load_sems.at[2])
    load_cot = pltpu.make_async_copy(cot_in, cot, load_sems.at[3])
    load_feat.start()
    load_kern.start()
    load_cot.start()

    barrier = pltpu.get_barrier_semaphore()

    def greet_lon(j, _):
        pl.semaphore_signal(barrier, inc=1, device_id=(lat, over_lon(j)), device_id_type=MESH)
        return 0

    def greet_lat(j, _):
        pl.semaphore_signal(barrier, inc=1, device_id=(over_lat(j), lon), device_id_type=MESH)
        return 0

    def vouch(j, _):
        pl.semaphore_signal(round_sem, inc=1, device_id=(over_lat(j), lon), device_id_type=MESH)
        return 0

    lax.fori_loop(1, NLON, greet_lon, 0)
    lax.fori_loop(1, NLAT, greet_lat, 0)
    slot_meta(offsets, counts, cells, turned, meta_src)
    load_feat.wait()
    turn_slots(by_slot, wide, by_dest)
    pl.semaphore_wait(barrier, NLON + NLAT - 2)
    lax.fori_loop(1, NLAT, vouch, 0)

    def meta_lon(j, _):
        to = over_lon(j)
        remote(meta_src.at[to], meta_mid.at[lon], a2a_sems.at[0], a2a_sems.at[1], lat, to).start()
        return 0

    def meta_lat(j, _):
        to = over_lat(j)
        remote(meta_mid.at[pl.ds(0, NLON), to], meta_nat.at[lat], a2a_sems.at[2], a2a_sems.at[3], to, lon).start()
        return 0

    def send_feats(p, _):
        a, b = place(p)
        to_lat, to_lon = lax.rem(lat - a + NLAT, NLAT), lax.rem(lon - b + NLON, NLON)
        remote(by_dest.at[to_lat * NLON + to_lon], feats.at[p], a2a_sems.at[4], a2a_sems.at[5], to_lat, to_lon).start()
        return 0

    lax.fori_loop(1, NLON, meta_lon, 0)
    meta_mid[lon] = meta_src[lon]
    pl.semaphore_wait(round_sem, NLAT - 1)
    lax.fori_loop(1, DEV // 2, send_feats, 0)
    wait_bytes(meta_mid.at[pl.ds(0, NLON - 1)], a2a_sems.at[1])
    lax.fori_loop(1, NLAT, meta_lat, 0)
    meta_nat[lat] = meta_mid[:, lat]
    lax.fori_loop(DEV // 2, DEV, send_feats, 0)
    feats[0] = by_dest[me]

    load_kern.wait()
    transpose_kernel(kc, kt)
    wait_bytes(meta_nat.at[pl.ds(0, NLAT - 1)], a2a_sems.at[3])

    def reorder(p, _):
        a, b = place(p)
        meta[p] = meta_nat[over_lat(a), over_lon(b)]
        return 0

    lax.fori_loop(0, DEV, reorder, 0, unroll=4)
    expand_lanes(meta, onehot, wrf, wrb, dens, edges, edge_inv)
    expand_rows(meta, col_weight, row_of)

    wait_bytes(feats.at[pl.ds(0, DEV - 1)], a2a_sems.at[5])
    splat_edges(feats, onehot, wrb, dens, edges, edge_inv, edge_rows, edge_cols)
    halo = exchange_edges(
        lat, lon, (edge_rows.at[0], edge_rows.at[1]), edge_cols, h_row.at[0], h_col.at[0], h_cor.at[0], halo_sems
    )
    for copy in halo:
        copy.start()
    splat(feats, onehot, wrb, dens, x3)
    for copy in halo:
        copy.wait_recv()
    patch(x3, lat, h_row.at[0], h_col.at[0], h_cor.at[0], col_vals, 0, 512)

    load_cot.wait()
    conv(x3, kc, bias, cot, enc, g3, gsum, gcol)
    store_enc = pltpu.make_async_copy(enc, enc_out, load_sems.at[4])
    store_enc.start()
    grad_cols[...] = gcol[...].astype(BF)
    last = ROWS * COLS
    grad_halo = exchange_edges(
        lat, lon, (g3.at[pl.ds(COLS, COLS), pl.ds(CH, CH)], g3.at[pl.ds(last, COLS), pl.ds(CH, CH)]),
        grad_cols, h_row.at[1], h_col.at[1], h_cor.at[1], grad_halo_sems,
    )
    for copy in grad_halo:
        copy.start()

    pair_bias = remote(gsum, pair_sum, pair_sems.at[0, TAPS], pair_sems.at[1, TAPS], lat, mate)
    pair_bias.start()
    taps = [jnp.int32(8)] + [lax.rem(lat + chip + i, 8) for i in range(8)]
    pair = []

    def pair_total(step):
        pair[step].wait()
        total = dw[step, pl.ds(aligned(128 * core), 128), :] + pair_dw[step]
        half[step] = total.astype(BF).reshape(8, 16, CH)

    def last_tap_rows(_):
        pair_total(0)
        tail_chip[chip] = half[0, chip]

        def step(j, _):
            to = lax.rem(chip + j, CHIPS)
            remote(half.at[0, to], tail_chip.at[chip], tail_sems.at[0], tail_sems.at[1], lat, to * 2 + core).start()
            return 0

        lax.fori_loop(1, CHIPS, step, 0)

    def last_tap_columns(_):
        wait_bytes(tail_chip.at[pl.ds(0, CHIPS - 1)], tail_sems.at[1])
        tail_part[...] = tail_chip[...].astype(F32).sum(0).astype(BF)
        tail_lat[lat] = tail_part[...]

        def step(j, _):
            remote(tail_part, tail_lat.at[lat], tail_sems.at[2], tail_sems.at[3], over_lat(j), lon).start()
            return 0

        lax.fori_loop(1, NLAT, step, 0)

    def last_tap_gather(_):
        wait_bytes(tail_lat.at[pl.ds(0, NLAT - 1)], tail_sems.at[3])
        tail_sum[...] = tail_lat[...].astype(F32).sum(0).astype(BF)
        spot = sums_out.at[core, PAIRS + chip]
        pltpu.make_async_copy(tail_sum, spot, load_sems.at[6]).start()

        def step(j, _):
            to = lax.rem(chip + j, CHIPS)
            remote(tail_sum, spot, tail_sems.at[4], tail_sems.at[5], lat, to * 2 + core).start()
            return 0

        lax.fori_loop(1, CHIPS, step, 0)

    def bias_columns(_):
        pair_bias.wait()
        bias_lat[lat] = gsum[...] + pair_sum[...]

        def step(j, _):
            remote(bias_lat.at[lat], bias_lat.at[lat], bias_sems.at[0], bias_sems.at[1], over_lat(j), lon).start()
            return 0

        lax.fori_loop(1, NLAT, step, 0)

    def bias_rows(_):
        wait_bytes(bias_lat.at[pl.ds(0, NLAT - 1)], bias_sems.at[1])
        bias_mid[...] = bias_lat[...].sum(0)
        bias_lon[chip] = bias_mid[...]

        def step(j, _):
            to = lax.rem(chip + j, CHIPS)
            remote(bias_mid, bias_lon.at[chip], bias_sems.at[2], bias_sems.at[3], lat, to * 2 + core).start()
            return 0

        lax.fori_loop(1, CHIPS, step, 0)

    def send_tap(step):
        pair_total(step)
        tap = taps[step]

        def send(m, _):
            to_lat = lax.rem(tap + m, NLAT)
            here = jnp.logical_and(to_lat == lat, m == chip)

            @pl.when(jnp.logical_not(here))
            def _():
                remote(
                    half.at[step, m], rs.at[owner], rs_sems.at[0], rs_sems.at[1], to_lat, m * 2 + core
                ).start()

            @pl.when(here)
            def _():
                rs[owner] = half[step, m]

            return 0

        lax.fori_loop(0, CHIPS, send, 0)

    def send_pair(step):
        pair.append(
            remote(
                dw.at[step, pl.ds(aligned(128 * (1 - core)), 128)], pair_dw.at[step],
                pair_sems.at[0, step], pair_sems.at[1, step], lat, mate,
            )
        )
        pair[-1].start()

    beside = {1: bias_columns, 2: last_tap_rows, 4: bias_rows, 5: last_tap_columns, 8: last_tap_gather}
    for step in range(TAPS):
        wgrad_tap(step, taps[step], x3, g3, dw)
        send_pair(step)
        if step in beside:
            beside[step](step)
        if step > LAG:
            send_tap(step - LAG)

    for copy in grad_halo:
        copy.wait()
    patch(g3, lat, h_row.at[1], h_col.at[1], h_cor.at[1], col_vals, 512, 0)
    for step in range(TAPS - LAG, TAPS):
        send_tap(step)

    wait_bytes(rs.at[pl.ds(0, PAIRS - 1)], rs_sems.at[1])
    reduced[...] = rs[...].astype(F32).sum(0).astype(BF)
    own_sum = pltpu.make_async_copy(reduced, sums_out.at[core, mine], load_sems.at[5])
    own_sum.start()

    def send_sum(j, _):
        a, b = spread_over(j)
        to_chip = lax.rem(chip + b, CHIPS)
        remote(
            reduced, sums_out.at[core, mine], ag_sems.at[0], ag_sems.at[1], over_lat(a), to_chip * 2 + core
        ).start()
        return 0

    lax.fori_loop(1, PAIRS, send_sum, 0)
    back_conv(g3, kt, cot, dens, scaled)

    def band(i, _):
        grad_band(i, col_weight, row_of, scaled, slot_grad)

        def back(j, _):
            p = i * 16 + j
            a, b = place(p)

            @pl.when(p != 0)
            def _():
                remote(
                    slot_grad.at[p], ret_out.at[me], ret_sems.at[0], ret_sems.at[1], over_lat(a), over_lon(b)
                ).start()

            return 0

        lax.fori_loop(0, 16, back, 0)
        return 0

    lax.fori_loop(0, DEV // 16, band, 0)
    own_ret = pltpu.make_async_copy(slot_grad.at[0], ret_out.at[me], load_sems.at[7])
    own_ret.start()

    own_sum.wait()
    pltpu.make_async_copy(tail_sum, sums_out.at[core, PAIRS + chip], load_sems.at[6]).wait()
    wait_bytes(sums_out.at[core, pl.ds(0, PAIRS - 1)], ag_sems.at[1])
    wait_bytes(sums_out.at[core, pl.ds(0, CHIPS - 1)], tail_sems.at[5])
    swap = remote(sums_out.at[core], sums_out.at[core], swap_sems.at[0], swap_sems.at[1], lat, mate)
    swap.start()
    wait_bytes(bias_lon.at[pl.ds(0, CHIPS - 1)], bias_sems.at[3])
    bias_out[...] = bias_lon[...].sum(0).sum(0, keepdims=True)

    wait_bytes(meta_mid.at[pl.ds(0, NLON - 1)], a2a_sems.at[0])
    wait_bytes(meta_nat.at[pl.ds(0, NLAT - 1)], a2a_sems.at[2])
    wait_bytes(feats.at[pl.ds(0, DEV - 1)], a2a_sems.at[4])
    wait_bytes(bias_lat.at[pl.ds(0, NLAT - 1)], bias_sems.at[0])
    wait_bytes(bias_lon.at[pl.ds(0, CHIPS - 1)], bias_sems.at[2])
    wait_bytes(tail_chip.at[pl.ds(0, CHIPS - 1)], tail_sems.at[0])
    wait_bytes(tail_lat.at[pl.ds(0, NLAT - 1)], tail_sems.at[2])
    wait_bytes(tail_chip.at[pl.ds(0, CHIPS - 1)], tail_sems.at[4])
    wait_bytes(rs.at[pl.ds(0, PAIRS - 1)], rs_sems.at[0])
    wait_bytes(rs.at[pl.ds(0, PAIRS - 1)], ag_sems.at[0])
    for copy in halo:
        copy.wait_send()
    store_enc.wait()
    own_ret.wait()
    wait_bytes(slot_grad.at[pl.ds(0, DEV - 1)], ret_sems.at[0])
    wait_bytes(ret_out.at[pl.ds(0, DEV - 1)], ret_sems.at[1])
    swap.wait()


def fused(feat, offsets, counts, cells, kern, bias, cot):
    vm = pltpu.VMEM
    dma = pltpu.SemaphoreType.DMA
    scratch = [
        vm((CAP, DEV, CH), BF),
        vm((2, SLOTS, 128), F32),
        vm((DEV, CAP, CH), BF),
        vm((DEV, 128), F32),
        vm((NLON, NLAT, 1, 128), F32),
        vm((NLON, NLAT, 1, 128), F32),
        vm((NLAT, NLON, 1, 128), F32),
        vm((DEV, CAP, CH), BF),
        vm((DEV, 1, 128), F32),
        vm((3, 3 * CH, CH), BF),
        vm((3, 3 * CH, CH), BF),
        vm((CELLS, CH), BF),
        vm((CELLS, CH), BF),
        vm((COLS, SLOTS), BF),
        vm((ROWS, SLOTS), F32),
        vm((ROWS, 16, SLOTS), BF),
        vm((CELLS, 128), F32),
        vm((2 * ROWS, SLOTS), BF),
        vm((2 * ROWS, 128), F32),
        vm((SLOTS, 128), BF),
        vm((SLOTS, 128), BF),
        vm((2, COLS, CH), BF),
        vm((2, ROWS, CH), BF),
        vm((2, 2, COLS, CH), BF),
        vm((2, 2, ROWS, CH), BF),
        vm((2, 4, 16, CH), BF),
        vm((2, 48, CH), F32),
        vm(((ROWS + 2) * COLS, 3 * CH), BF),
        vm(((ROWS + 2) * COLS, 3 * CH), BF),
        vm((8, CH), F32),
        vm((2, ROWS, CH), F32),
        vm((2, ROWS, CH), BF),
        vm((CELLS, CH), BF),
        vm((DEV, CAP, CH), BF),
        vm((TAPS, CH, CH), F32),
        vm((TAPS, 128, CH), F32),
        vm((8, CH), F32),
        vm((TAPS, CHIPS, 16, CH), BF),
        vm((PAIRS, 16, CH), BF),
        vm((16, CH), BF),
        vm((NLAT, 8, CH), F32),
        vm((8, CH), F32),
        vm((CHIPS, 8, CH), F32),
        vm((CHIPS, 16, CH), BF),
        vm((NLAT, 16, CH), BF),
        vm((16, CH), BF),
        vm((16, CH), BF),
        pltpu.SemaphoreType.REGULAR,
        dma((8,)),
        dma((6,)),
        dma((2, 8)),
        dma((2, 8)),
        dma((2, 10)),
        dma((2,)),
        dma((2,)),
        dma((2,)),
        dma((2,)),
        dma((4,)),
        dma((6,)),
    ]
    anywhere = pl.BlockSpec(memory_space=pl.ANY)
    local = pl.BlockSpec(memory_space=pltpu.VMEM)
    return pl.pallas_call(
        kernel,
        out_shape=[
            jax.ShapeDtypeStruct((CELLS, CH), BF),
            jax.ShapeDtypeStruct((2, CHUNKS, 16, CH), BF),
            jax.ShapeDtypeStruct((DEV, CAP, CH), BF),
            jax.ShapeDtypeStruct((1, CH), F32),
        ],
        in_specs=[anywhere, local, local, local, anywhere, local, anywhere],
        out_specs=[anywhere, anywhere, anywhere, local],
        scratch_shapes=scratch,
        compiler_params=pltpu.CompilerParams(collective_id=0, has_side_effects=True, vmem_limit_bytes=60 * 2**20),
        name="fused",
    )(feat, offsets, counts, cells, kern, bias, cot)


def body(features, offsets, counts, cell_index, kern, conv_bias, cotangent):
    encoded, sums, ret, bias_sum = fused(
        features[0], offsets[:, 0], counts, cell_index[0], kern.reshape(3, 3 * CH, CH),
        conv_bias.reshape(1, CH), cotangent.reshape(CELLS, CH),
    )
    scale = 1.0 / math.sqrt(CELLS * DEV)
    taps = sums.reshape(2, 3, 3, 128, CH).transpose(1, 2, 0, 3, 4).reshape(3, 3, CH, CH)
    weight_grad = taps.astype(F32) * scale
    bias_grad = bias_sum[0] * scale
    obs_grad = jnp.transpose(ret, (1, 0, 2))[None]
    return encoded.reshape(ROWS, COLS, CH), weight_grad, bias_grad, obs_grad


def solution(mesh):
    return jax.shard_map(
        body,
        mesh=mesh,
        in_specs=(
            P(("lat", "lon"), None, None, None),
            P(None, ("lat", "lon"), None, None),
            P(("lat", "lon"), None),
            P(("lat", "lon"), None, None),
            P(),
            P(),
            P("lat", "lon", None),
        ),
        out_specs=(P("lat", "lon", None), P(), P(), P(("lat", "lon"), None, None, None)),
        check_vma=False,
    )
```

```python
import functools
import math

import jax
import jax.numpy as jnp
from jax import lax
from jax.experimental import pallas as pl
from jax.experimental.pallas import tpu as pltpu
from jax.sharding import PartitionSpec as P

BF = jnp.bfloat16
F32 = jnp.float32
MESH = pl.DeviceIdType.MESH
ROWS, COLS, CH, CAP = 32, 128, 256, 16
NLAT, NLON = 8, 16
DEV = NLAT * NLON
SLOTS = DEV * CAP
CELLS = ROWS * COLS
PAIRS = DEV // 2
CHIPS = NLON // 2
CHUNKS = 72
TAPS = 9
LAG = 2


def iota(shape, dim):
    return lax.broadcasted_iota(jnp.int32, shape, dim)


def fiota(shape, dim):
    return iota(shape, dim).astype(F32)


def aligned(value, unit=128):
    return pl.multiple_of(value, unit)


def remote(src, dst, send, recv, lat, lon):
    return pltpu.make_async_remote_copy(
        src_ref=src, dst_ref=dst, send_sem=send, recv_sem=recv, device_id=(lat, lon), device_id_type=MESH
    )


def wait_bytes(ref, sem):
    pltpu.make_async_copy(ref, ref, sem).wait()


def expand_lanes(meta, onehot, wrf, wrb, dens, edges, edge_inv):
    per_dev = meta[...].reshape(DEV, 128).astype(BF)
    lane = iota((128, 384), 1)
    pick = jnp.where(iota((128, 384), 0) == (lane // 128) * CAP + lane % CAP, 1.0, 0.0).astype(BF)
    spread = jnp.dot(per_dev, pick, preferred_element_type=F32).reshape(16, 8, 384)
    lane8 = iota((8, 384), 1)
    mine = jnp.where(iota((8, 384), 0) == (lane8 % 128) // CAP, 1.0, 0.0)
    flat = (spread * mine[None]).sum(1)
    total = jnp.zeros((2 * ROWS, 128), F32)
    for g in range(16):
        wide = slice(g * 128, g * 128 + 128)
        w, row, col = flat[g : g + 1, 0:128], flat[g : g + 1, 128:256], flat[g : g + 1, 256:384]
        onehot[:, wide] = jnp.where(fiota((COLS, 128), 0) == col, 1.0, 0.0).astype(BF)
        by_row = jnp.where(fiota((ROWS, 128), 0) == row, w, 0.0)
        wrf[:, wide] = by_row
        first = jnp.where(col == 0.0, by_row, 0.0)
        last = jnp.where(col == float(COLS - 1), by_row, 0.0)
        both = jnp.concatenate([first, last], 0)
        edges[:, wide] = both.astype(BF)
        total = total + both
    edge_inv[...] = jnp.broadcast_to(1.0 / (total.sum(1, keepdims=True) + 1.0), (2 * ROWS, 128))

    def widen(r, _):
        wrb[r] = jnp.broadcast_to(wrf[pl.ds(r, 1), :], (16, SLOTS)).astype(BF)
        return 0

    lax.fori_loop(0, ROWS, widen, 0)
    density = lax.dot_general(
        onehot[...], wrf[...].astype(BF), (((1,), (1,)), ((), ())), preferred_element_type=F32
    )
    inv = 1.0 / (density + 1.0)
    for r in range(ROWS):
        dens[r * COLS : (r + 1) * COLS, :] = jnp.broadcast_to(inv[:, r : r + 1], (COLS, 128))


def expand_rows(meta, col_weight, row_of):
    lane = iota((128, 384), 1)
    pick = jnp.where(iota((128, 384), 0) // CAP == lane // 128, 1.0, 0.0).astype(BF)
    slot_lane = iota((CAP, 128), 1)
    mine = jnp.where(slot_lane % CAP == iota((CAP, 128), 0), 1.0, 0.0)

    def step(i, _):
        block = meta[pl.ds(i * 16, 16)]
        masked = (jnp.broadcast_to(block, (16, CAP, 128)) * mine[None]).reshape(256, 128).astype(BF)
        spread = jnp.dot(masked, pick, preferred_element_type=F32)
        base = aligned(i * 256, 256)
        col_weight[pl.ds(base, 256), :] = jnp.where(
            spread[:, 256:384] == fiota((256, 128), 1), spread[:, 0:128], 0.0
        ).astype(BF)
        row_of[pl.ds(base, 256), :] = spread[:, 128:256].astype(BF)
        return 0

    lax.fori_loop(0, DEV // 16, step, 0)


def twice(inv):
    return jnp.concatenate([inv, inv], 1)


def splat_edges(feats, onehot, wrb, dens, edges, edge_inv, rows_out, cols_out):
    hot = onehot[...].reshape(8, 16, SLOTS)
    lhs = jnp.concatenate(
        [(hot * wrb[0][None]).reshape(COLS, SLOTS), (hot * wrb[ROWS - 1][None]).reshape(COLS, SLOTS), edges[...]], 0
    )
    acc = jnp.dot(lhs, feats[...].reshape(SLOTS, CH), preferred_element_type=F32)
    rows_out[0] = (acc[0:COLS] * twice(dens[0:COLS, :])).astype(BF)
    rows_out[1] = (acc[COLS : 2 * COLS] * twice(dens[CELLS - COLS : CELLS, :])).astype(BF)
    cols = (acc[2 * COLS :] * twice(edge_inv[...])).astype(BF)
    cols_out[0] = cols[0:ROWS]
    cols_out[1] = cols[ROWS:]


def splat(feats, onehot, wrb, dens, x3, per=4):
    def step(i, _):
        r0 = i * per
        hot = onehot[...].reshape(8, 16, SLOTS)
        lhs = jnp.concatenate([(hot * wrb[r0 + k][None]).reshape(COLS, SLOTS) for k in range(per)], 0)
        acc = jnp.dot(lhs, feats[...].reshape(SLOTS, CH), preferred_element_type=F32)
        for k in range(per):
            base = aligned((r0 + k) * COLS)
            field = (acc[k * COLS : (k + 1) * COLS] * twice(dens[pl.ds(base, COLS), :])).astype(BF)
            wide = field.astype(F32)
            x3[pl.ds(base + COLS, COLS), 256:512] = field
            x3[pl.ds(base + COLS, COLS), 0:256] = pltpu.roll(wide, 1, 0).astype(BF)
            x3[pl.ds(base + COLS, COLS), 512:768] = pltpu.roll(wide, COLS - 1, 0).astype(BF)
        return 0

    lax.fori_loop(0, ROWS // per, step, 0)


def exchange_edges(lat, lon, rows, cols, h_row, h_col, h_cor, sems):
    up, down = lax.rem(lat + NLAT - 1, NLAT), lax.rem(lat + 1, NLAT)
    west, east = lax.rem(lon + NLON - 1, NLON), lax.rem(lon + 1, NLON)
    plan = (
        (rows[0], h_row.at[1], up, lon),
        (rows[1], h_row.at[0], down, lon),
        (cols.at[0], h_col.at[1], lat, west),
        (cols.at[1], h_col.at[0], lat, east),
        (cols.at[1, pl.ds(16, 16)], h_cor.at[0], down, east),
        (cols.at[0, pl.ds(16, 16)], h_cor.at[1], down, west),
        (cols.at[1, pl.ds(0, 16)], h_cor.at[2], up, east),
        (cols.at[0, pl.ds(0, 16)], h_cor.at[3], up, west),
    )
    return [remote(s, d, sems.at[0, i], sems.at[1, i], a, b) for i, (s, d, a, b) in enumerate(plan)]


def patch(arr, lat, h_row, h_col, h_cor, col_vals, left, right):
    top = jnp.where(lat == 0, 0.0, 1.0)
    bottom = jnp.where(lat == NLAT - 1, 0.0, 1.0)
    for side in range(2):
        col_vals[side, 0:32, :] = h_col[side].astype(F32)
        col_vals[side, 32:40, :] = jnp.broadcast_to(h_cor[side].astype(F32)[15:16] * top, (8, CH))
        col_vals[side, 40:48, :] = jnp.broadcast_to(h_cor[2 + side].astype(F32)[0:1] * bottom, (8, CH))
    sub = iota((16, CH), 0)

    def step(r, _):
        base = aligned((r + 1) * COLS)
        old = arr[pl.ds(base, 16), left : left + CH].astype(F32)
        arr[pl.ds(base, 16), left : left + CH] = jnp.where(sub == 0, col_vals[0, pl.ds(r, 1), :], old).astype(BF)
        far = aligned(base + COLS - 16, 16)
        old = arr[pl.ds(far, 16), right : right + CH].astype(F32)
        arr[pl.ds(far, 16), right : right + CH] = jnp.where(sub == 15, col_vals[1, pl.ds(r, 1), :], old).astype(BF)
        return 0

    lax.fori_loop(0, ROWS, step, 0)
    full = iota((COLS, CH), 0)
    for side, (base, keep) in enumerate(((0, top), ((ROWS + 1) * COLS, bottom))):
        at = 32 + 8 * side
        wide = h_row[side].astype(F32) * keep
        arr[base : base + COLS, 256:512] = wide.astype(BF)
        arr[base : base + COLS, left : left + CH] = jnp.where(
            full == 0, col_vals[0, at : at + 1, :], pltpu.roll(wide, 1, 0)
        ).astype(BF)
        arr[base : base + COLS, right : right + CH] = jnp.where(
            full == COLS - 1, col_vals[1, at : at + 1, :], pltpu.roll(wide, COLS - 1, 0)
        ).astype(BF)


def conv(x3, kc, bias, cot, enc, g3, gsum, gcol, per=4):
    gsum[...] = jnp.zeros_like(gsum)

    def step(i, _):
        r0 = i * per
        acc = jnp.broadcast_to(bias[...], (per * COLS, CH))
        for a in range(3):
            acc = acc + jnp.dot(
                x3[pl.ds(aligned((r0 + a) * COLS), per * COLS), :], kc[a], preferred_element_type=F32
            )
        base = aligned(r0 * COLS)
        gate = 0.5 * jnp.tanh(0.5 * acc) + 0.5
        silu = acc * gate
        field = x3[pl.ds(base + COLS, per * COLS), 256:512].astype(F32)
        enc[pl.ds(base, per * COLS), :] = (field + silu).astype(BF)
        grad = (cot[pl.ds(base, per * COLS), :].astype(F32) * (gate + silu * (1.0 - gate))).astype(BF)
        wide = grad.astype(F32)
        gsum[...] += wide.reshape(per * COLS // 8, 8, CH).sum(0)
        g3[pl.ds(base + COLS, per * COLS), 256:512] = grad
        for k in range(per):
            row = wide[k * COLS : (k + 1) * COLS]
            at = pl.ds(base + COLS + k * COLS, COLS)
            g3[at, 0:256] = pltpu.roll(row, COLS - 1, 0).astype(BF)
            g3[at, 512:768] = pltpu.roll(row, 1, 0).astype(BF)
            gcol[0, pl.ds(r0 + k, 1), :] = row[0:1]
            gcol[1, pl.ds(r0 + k, 1), :] = row[COLS - 1 : COLS]
        return 0

    lax.fori_loop(0, ROWS // per, step, 0)


def wgrad_tap(step, tap, x3, g3, dw):
    rows, lanes = pl.ds(aligned(tap // 3 * COLS), CELLS), pl.ds(aligned(lax.rem(tap, 3) * CH), CH)
    dw[step] = lax.dot_general(
        x3[rows, lanes], g3[COLS : COLS + CELLS, CH : 2 * CH], (((0,), (0,)), ((), ())), preferred_element_type=F32
    )


def grad_band(i, col_weight, row_of, scaled, slot_grad):
    base = aligned(i * 256, 256)
    weight, row = col_weight[pl.ds(base, 256), :], row_of[pl.ds(base, 256), :]
    lhs = jnp.concatenate(
        [jnp.where(row == jnp.array(r, BF), weight, jnp.zeros_like(weight)) for r in range(ROWS)], 1
    )
    grads = jnp.dot(lhs, scaled[...], preferred_element_type=F32).astype(BF)
    slot_grad[pl.ds(i * 16, 16)] = grads.reshape(16, CAP, CH)


def transpose_kernel(kc, kt):
    for a in range(3):
        for b in range(3):
            kt[a, b * CH : (b + 1) * CH, :] = kc[a, b * CH : (b + 1) * CH, :].T


def back_conv(g3, kt, cot, dens, scaled, per=4):
    def step(i, _):
        r0 = i * per
        base = aligned(r0 * COLS)
        acc = cot[pl.ds(base, per * COLS), :].astype(F32)
        for a in range(3):
            acc = acc + jnp.dot(
                g3[pl.ds(aligned((r0 + 2 - a) * COLS), per * COLS), :], kt[a], preferred_element_type=F32
            )
        scaled[pl.ds(base, per * COLS), :] = (acc * twice(dens[pl.ds(base, per * COLS), :])).astype(BF)
        return 0

    lax.fori_loop(0, ROWS // per, step, 0)


def place(p):
    q = lax.rem(p, 16)
    a = q // 2
    return a, lax.rem(2 * (p // 16 + a) + lax.rem(q, 2), NLON)


def spread_over(j):
    b = lax.rem(j, CHIPS)
    return lax.rem(j // CHIPS + b, NLAT), b


def slot_meta(offsets, counts, cells, turned, meta_src):
    live = iota((CAP, DEV), 0) < counts[...]
    radius = offsets[0] * offsets[0] + offsets[1] * offsets[1]
    weight = jnp.where(live, jnp.exp(-2.0 * radius), 0.0)
    row, col = cells[...] // COLS, cells[...] % COLS
    table = jnp.concatenate([weight, row.astype(F32), col.astype(F32), jnp.zeros((128 - 3 * CAP, DEV), F32)], 0)
    turned[...] = table.T

    def step(t, _):
        meta_src[lax.rem(t, NLON), t // NLON] = turned[pl.ds(t, 1), :]
        return 0

    lax.fori_loop(0, DEV, step, 0, unroll=8)


def turn_slots(by_slot, wide, by_dest):
    flat = by_slot[...].reshape(SLOTS, CH).astype(F32)
    wide[0], wide[1] = flat[:, :128], flat[:, 128:]

    def step(t, _):
        halves = [wide[h, pl.ds(t, CAP, stride=DEV), :] for h in range(2)]
        by_dest[t] = jnp.concatenate(halves, 1).astype(BF)
        return 0

    lax.fori_loop(0, DEV, step, 0, unroll=8)


def kernel(
    feat_in, offsets, counts, cells, kern_in, bias, cot_in,
    enc_out, sums_out, ret_out, bias_out,
    by_slot, wide, by_dest, turned, meta_src, meta_mid, meta_nat,
    feats, meta, kc, kt, cot, enc, onehot, wrf, wrb, dens, edges, edge_inv, col_weight, row_of,
    edge_rows, edge_cols, h_row, h_col, h_cor, col_vals, x3, g3, gsum, gcol, grad_cols, scaled, slot_grad,
    dw, pair_dw, pair_sum, half, rs, reduced, bias_lat, bias_mid, bias_lon, tail_chip, tail_lat, tail_part, tail_sum,
    round_sem, load_sems, a2a_sems, halo_sems, grad_halo_sems, pair_sems, rs_sems, ag_sems, swap_sems, ret_sems, bias_sems, tail_sems,
):
    lat, lon = lax.axis_index("lat"), lax.axis_index("lon")
    me = lat * NLON + lon
    core = lax.rem(lon, 2)
    mate = lon + 1 - 2 * core
    chip = lon // 2
    owner = lat * CHIPS + chip
    mine = lax.rem(lat - chip + CHIPS, CHIPS) * CHIPS + chip

    def over_lat(j):
        return lax.rem(lat + j, NLAT)

    def over_lon(j):
        return lax.rem(lon + j, NLON)

    load_feat = pltpu.make_async_copy(feat_in, by_slot, load_sems.at[1])
    load_kern = pltpu.make_async_copy(kern_in, kc, load_sems.at[2])
    load_cot = pltpu.make_async_copy(cot_in, cot, load_sems.at[3])
    load_feat.start()
    load_kern.start()
    load_cot.start()

    barrier = pltpu.get_barrier_semaphore()

    def greet_lon(j, _):
        pl.semaphore_signal(barrier, inc=1, device_id=(lat, over_lon(j)), device_id_type=MESH)
        return 0

    def greet_lat(j, _):
        pl.semaphore_signal(barrier, inc=1, device_id=(over_lat(j), lon), device_id_type=MESH)
        return 0

    def vouch(j, _):
        pl.semaphore_signal(round_sem, inc=1, device_id=(over_lat(j), lon), device_id_type=MESH)
        return 0

    lax.fori_loop(1, NLON, greet_lon, 0)
    lax.fori_loop(1, NLAT, greet_lat, 0)
    slot_meta(offsets, counts, cells, turned, meta_src)
    pl.semaphore_wait(barrier, NLON + NLAT - 2)
    lax.fori_loop(1, NLAT, vouch, 0)

    def meta_lon(j, _):
        to = over_lon(j)
        remote(meta_src.at[to], meta_mid.at[lon], a2a_sems.at[0], a2a_sems.at[1], lat, to).start()
        return 0

    def meta_lat(j, _):
        to = over_lat(j)
        remote(meta_mid.at[pl.ds(0, NLON), to], meta_nat.at[lat], a2a_sems.at[2], a2a_sems.at[3], to, lon).start()
        return 0

    def send_feats(p, _):
        a, b = place(p)
        to_lat, to_lon = lax.rem(lat - a + NLAT, NLAT), lax.rem(lon - b + NLON, NLON)
        remote(by_dest.at[to_lat * NLON + to_lon], feats.at[p], a2a_sems.at[4], a2a_sems.at[5], to_lat, to_lon).start()
        return 0

    lax.fori_loop(1, NLON, meta_lon, 0)
    meta_mid[lon] = meta_src[lon]
    load_feat.wait()
    turn_slots(by_slot, wide, by_dest)
    pl.semaphore_wait(round_sem, NLAT - 1)
    lax.fori_loop(1, DEV // 2, send_feats, 0)
    wait_bytes(meta_mid.at[pl.ds(0, NLON - 1)], a2a_sems.at[1])
    lax.fori_loop(1, NLAT, meta_lat, 0)
    meta_nat[lat] = meta_mid[:, lat]
    lax.fori_loop(DEV // 2, DEV, send_feats, 0)
    feats[0] = by_dest[me]

    load_kern.wait()
    transpose_kernel(kc, kt)
    wait_bytes(meta_nat.at[pl.ds(0, NLAT - 1)], a2a_sems.at[3])

    def reorder(p, _):
        a, b = place(p)
        meta[p] = meta_nat[over_lat(a), over_lon(b)]
        return 0

    lax.fori_loop(0, DEV, reorder, 0, unroll=4)
    expand_lanes(meta, onehot, wrf, wrb, dens, edges, edge_inv)
    expand_rows(meta, col_weight, row_of)

    wait_bytes(feats.at[pl.ds(0, DEV - 1)], a2a_sems.at[5])
    splat_edges(feats, onehot, wrb, dens, edges, edge_inv, edge_rows, edge_cols)
    halo = exchange_edges(
        lat, lon, (edge_rows.at[0], edge_rows.at[1]), edge_cols, h_row.at[0], h_col.at[0], h_cor.at[0], halo_sems
    )
    for copy in halo:
        copy.start()
    splat(feats, onehot, wrb, dens, x3)
    for copy in halo:
        copy.wait_recv()
    patch(x3, lat, h_row.at[0], h_col.at[0], h_cor.at[0], col_vals, 0, 512)

    load_cot.wait()
    conv(x3, kc, bias, cot, enc, g3, gsum, gcol)
    store_enc = pltpu.make_async_copy(enc, enc_out, load_sems.at[4])
    store_enc.start()
    grad_cols[...] = gcol[...].astype(BF)
    last = ROWS * COLS
    grad_halo = exchange_edges(
        lat, lon, (g3.at[pl.ds(COLS, COLS), pl.ds(CH, CH)], g3.at[pl.ds(last, COLS), pl.ds(CH, CH)]),
        grad_cols, h_row.at[1], h_col.at[1], h_cor.at[1], grad_halo_sems,
    )
    for copy in grad_halo:
        copy.start()

    pair_bias = remote(gsum, pair_sum, pair_sems.at[0, TAPS], pair_sems.at[1, TAPS], lat, mate)
    pair_bias.start()
    taps = [jnp.int32(8)] + [lax.rem(lat + chip + i, 8) for i in range(8)]
    pair = []

    def pair_total(step):
        pair[step].wait()
        total = dw[step, pl.ds(aligned(128 * core), 128), :] + pair_dw[step]
        half[step] = total.astype(BF).reshape(8, 16, CH)

    def last_tap_rows():
        pair_total(0)
        tail_chip[chip] = half[0, chip]

        def step(j, _):
            to = lax.rem(chip + j, CHIPS)
            remote(half.at[0, to], tail_chip.at[chip], tail_sems.at[0], tail_sems.at[1], lat, to * 2 + core).start()
            return 0

        lax.fori_loop(1, CHIPS, step, 0)

    def last_tap_columns():
        wait_bytes(tail_chip.at[pl.ds(0, CHIPS - 1)], tail_sems.at[1])
        tail_part[...] = tail_chip[...].astype(F32).sum(0).astype(BF)
        tail_lat[lat] = tail_part[...]

        def step(j, _):
            remote(tail_part, tail_lat.at[lat], tail_sems.at[2], tail_sems.at[3], over_lat(j), lon).start()
            return 0

        lax.fori_loop(1, NLAT, step, 0)

    def last_tap_gather():
        wait_bytes(tail_lat.at[pl.ds(0, NLAT - 1)], tail_sems.at[3])
        tail_sum[...] = tail_lat[...].astype(F32).sum(0).astype(BF)
        spot = sums_out.at[core, PAIRS + chip]
        pltpu.make_async_copy(tail_sum, spot, load_sems.at[6]).start()

        def step(j, _):
            to = lax.rem(chip + j, CHIPS)
            remote(tail_sum, spot, tail_sems.at[4], tail_sems.at[5], lat, to * 2 + core).start()
            return 0

        lax.fori_loop(1, CHIPS, step, 0)

    def bias_columns():
        pair_bias.wait()
        bias_lat[lat] = gsum[...] + pair_sum[...]

        def step(j, _):
            remote(bias_lat.at[lat], bias_lat.at[lat], bias_sems.at[0], bias_sems.at[1], over_lat(j), lon).start()
            return 0

        lax.fori_loop(1, NLAT, step, 0)

    def bias_rows():
        wait_bytes(bias_lat.at[pl.ds(0, NLAT - 1)], bias_sems.at[1])
        bias_mid[...] = bias_lat[...].sum(0)
        bias_lon[chip] = bias_mid[...]

        def step(j, _):
            to = lax.rem(chip + j, CHIPS)
            remote(bias_mid, bias_lon.at[chip], bias_sems.at[2], bias_sems.at[3], lat, to * 2 + core).start()
            return 0

        lax.fori_loop(1, CHIPS, step, 0)

    def send_tap(step):
        pair_total(step)
        tap = taps[step]

        def send(m, _):
            to_lat = lax.rem(tap + m, NLAT)
            here = jnp.logical_and(to_lat == lat, m == chip)

            @pl.when(jnp.logical_not(here))
            def _():
                remote(
                    half.at[step, m], rs.at[owner], rs_sems.at[0], rs_sems.at[1], to_lat, m * 2 + core
                ).start()

            @pl.when(here)
            def _():
                rs[owner] = half[step, m]

            return 0

        lax.fori_loop(0, CHIPS, send, 0)

    def send_pair(step):
        pair.append(
            remote(
                dw.at[step, pl.ds(aligned(128 * (1 - core)), 128)], pair_dw.at[step],
                pair_sems.at[0, step], pair_sems.at[1, step], lat, mate,
            )
        )
        pair[-1].start()

    beside = {3: last_tap_rows, 6: bias_columns}
    for step in range(TAPS):
        wgrad_tap(step, taps[step], x3, g3, dw)
        send_pair(step)
        if step in beside:
            beside[step]()
        if step > LAG:
            send_tap(step - LAG)

    for copy in grad_halo:
        copy.wait()
    patch(g3, lat, h_row.at[1], h_col.at[1], h_cor.at[1], col_vals, 512, 0)
    for step in range(TAPS - LAG, TAPS):
        send_tap(step)

    last_tap_columns()
    bias_rows()
    back_conv(g3, kt, cot, dens, scaled)

    wait_bytes(rs.at[pl.ds(0, PAIRS - 1)], rs_sems.at[1])
    reduced[...] = rs[...].astype(F32).sum(0).astype(BF)
    own_sum = pltpu.make_async_copy(reduced, sums_out.at[core, mine], load_sems.at[5])
    own_sum.start()

    def send_sum(j, _):
        a, b = spread_over(j)
        to_chip = lax.rem(chip + b, CHIPS)
        remote(
            reduced, sums_out.at[core, mine], ag_sems.at[0], ag_sems.at[1], over_lat(a), to_chip * 2 + core
        ).start()
        return 0

    lax.fori_loop(1, PAIRS, send_sum, 0)
    last_tap_gather()

    def band(i, _):
        grad_band(i, col_weight, row_of, scaled, slot_grad)

        def back(j, _):
            p = i * 16 + j
            a, b = place(p)

            @pl.when(p != 0)
            def _():
                remote(
                    slot_grad.at[p], ret_out.at[me], ret_sems.at[0], ret_sems.at[1], over_lat(a), over_lon(b)
                ).start()

            return 0

        lax.fori_loop(0, 16, back, 0)
        return 0

    lax.fori_loop(0, DEV // 16, band, 0)
    own_ret = pltpu.make_async_copy(slot_grad.at[0], ret_out.at[me], load_sems.at[7])
    own_ret.start()

    own_sum.wait()
    pltpu.make_async_copy(tail_sum, sums_out.at[core, PAIRS + chip], load_sems.at[6]).wait()
    wait_bytes(sums_out.at[core, pl.ds(0, PAIRS - 1)], ag_sems.at[1])
    wait_bytes(sums_out.at[core, pl.ds(0, CHIPS - 1)], tail_sems.at[5])
    swap = remote(sums_out.at[core], sums_out.at[core], swap_sems.at[0], swap_sems.at[1], lat, mate)
    swap.start()
    wait_bytes(bias_lon.at[pl.ds(0, CHIPS - 1)], bias_sems.at[3])
    bias_out[...] = bias_lon[...].sum(0).sum(0, keepdims=True)

    wait_bytes(meta_mid.at[pl.ds(0, NLON - 1)], a2a_sems.at[0])
    wait_bytes(meta_nat.at[pl.ds(0, NLAT - 1)], a2a_sems.at[2])
    wait_bytes(feats.at[pl.ds(0, DEV - 1)], a2a_sems.at[4])
    wait_bytes(bias_lat.at[pl.ds(0, NLAT - 1)], bias_sems.at[0])
    wait_bytes(bias_lon.at[pl.ds(0, CHIPS - 1)], bias_sems.at[2])
    wait_bytes(tail_chip.at[pl.ds(0, CHIPS - 1)], tail_sems.at[0])
    wait_bytes(tail_lat.at[pl.ds(0, NLAT - 1)], tail_sems.at[2])
    wait_bytes(tail_chip.at[pl.ds(0, CHIPS - 1)], tail_sems.at[4])
    wait_bytes(rs.at[pl.ds(0, PAIRS - 1)], rs_sems.at[0])
    wait_bytes(rs.at[pl.ds(0, PAIRS - 1)], ag_sems.at[0])
    for copy in halo:
        copy.wait_send()
    store_enc.wait()
    own_ret.wait()
    wait_bytes(slot_grad.at[pl.ds(0, DEV - 1)], ret_sems.at[0])
    wait_bytes(ret_out.at[pl.ds(0, DEV - 1)], ret_sems.at[1])
    swap.wait()


def fused(feat, offsets, counts, cells, kern, bias, cot):
    vm = pltpu.VMEM
    dma = pltpu.SemaphoreType.DMA
    scratch = [
        vm((CAP, DEV, CH), BF),
        vm((2, SLOTS, 128), F32),
        vm((DEV, CAP, CH), BF),
        vm((DEV, 128), F32),
        vm((NLON, NLAT, 1, 128), F32),
        vm((NLON, NLAT, 1, 128), F32),
        vm((NLAT, NLON, 1, 128), F32),
        vm((DEV, CAP, CH), BF),
        vm((DEV, 1, 128), F32),
        vm((3, 3 * CH, CH), BF),
        vm((3, 3 * CH, CH), BF),
        vm((CELLS, CH), BF),
        vm((CELLS, CH), BF),
        vm((COLS, SLOTS), BF),
        vm((ROWS, SLOTS), F32),
        vm((ROWS, 16, SLOTS), BF),
        vm((CELLS, 128), F32),
        vm((2 * ROWS, SLOTS), BF),
        vm((2 * ROWS, 128), F32),
        vm((SLOTS, 128), BF),
        vm((SLOTS, 128), BF),
        vm((2, COLS, CH), BF),
        vm((2, ROWS, CH), BF),
        vm((2, 2, COLS, CH), BF),
        vm((2, 2, ROWS, CH), BF),
        vm((2, 4, 16, CH), BF),
        vm((2, 48, CH), F32),
        vm(((ROWS + 2) * COLS, 3 * CH), BF),
        vm(((ROWS + 2) * COLS, 3 * CH), BF),
        vm((8, CH), F32),
        vm((2, ROWS, CH), F32),
        vm((2, ROWS, CH), BF),
        vm((CELLS, CH), BF),
        vm((DEV, CAP, CH), BF),
        vm((TAPS, CH, CH), F32),
        vm((TAPS, 128, CH), F32),
        vm((8, CH), F32),
        vm((TAPS, CHIPS, 16, CH), BF),
        vm((PAIRS, 16, CH), BF),
        vm((16, CH), BF),
        vm((NLAT, 8, CH), F32),
        vm((8, CH), F32),
        vm((CHIPS, 8, CH), F32),
        vm((CHIPS, 16, CH), BF),
        vm((NLAT, 16, CH), BF),
        vm((16, CH), BF),
        vm((16, CH), BF),
        pltpu.SemaphoreType.REGULAR,
        dma((8,)),
        dma((6,)),
        dma((2, 8)),
        dma((2, 8)),
        dma((2, 10)),
        dma((2,)),
        dma((2,)),
        dma((2,)),
        dma((2,)),
        dma((4,)),
        dma((6,)),
    ]
    anywhere = pl.BlockSpec(memory_space=pl.ANY)
    local = pl.BlockSpec(memory_space=pltpu.VMEM)
    return pl.pallas_call(
        kernel,
        out_shape=[
            jax.ShapeDtypeStruct((CELLS, CH), BF),
            jax.ShapeDtypeStruct((2, CHUNKS, 16, CH), BF),
            jax.ShapeDtypeStruct((DEV, CAP, CH), BF),
            jax.ShapeDtypeStruct((1, CH), F32),
        ],
        in_specs=[anywhere, local, local, local, anywhere, local, anywhere],
        out_specs=[anywhere, anywhere, anywhere, local],
        scratch_shapes=scratch,
        compiler_params=pltpu.CompilerParams(collective_id=0, has_side_effects=True, vmem_limit_bytes=60 * 2**20),
        name="fused",
    )(feat, offsets, counts, cells, kern, bias, cot)


def finish_kernel(
    enc_in, sums_in, ret_in, bias_in, enc_out, grad_out, bias_out, obs_out, enc, sums, ret, grad, wide, obs, sems, out_sems
):
    scale = 1.0 / math.sqrt(CELLS * DEV)
    load_ret = pltpu.make_async_copy(ret_in, ret, sems.at[0])
    load_sums = pltpu.make_async_copy(sums_in, sums, sems.at[1])
    load_enc = pltpu.make_async_copy(enc_in, enc, sems.at[2])
    load_sums.start()
    load_ret.start()
    load_enc.start()
    bias_out[...] = bias_in[...] * scale
    copies = []

    def store(src, dst):
        copies.append(pltpu.make_async_copy(src, dst, out_sems.at[len(copies)]))
        copies[-1].start()

    load_sums.wait()
    for tap in range(TAPS):
        for core in range(2):
            rows = sums[core, tap * CHIPS : (tap + 1) * CHIPS].reshape(128, CH)
            grad[tap, core * 128 : (core + 1) * 128, :] = rows.astype(F32) * scale
        store(grad.at[tap], grad_out.at[tap])
    load_enc.wait()
    store(enc, enc_out)
    load_ret.wait()
    flat = ret[...].reshape(SLOTS, CH).astype(F32)
    wide[0], wide[1] = flat[:, :128], flat[:, 128:]
    for k in range(CAP):
        halves = [wide[h, pl.ds(k, DEV, stride=CAP), :] for h in range(2)]
        obs[k] = jnp.concatenate(halves, 1).astype(BF)
        if k % 4 == 3:
            store(obs.at[pl.ds(k - 3, 4)], obs_out.at[pl.ds(k - 3, 4)])
    for copy in copies:
        copy.wait()


def finish(encoded, sums, ret, bias_sum):
    vm = pltpu.VMEM
    anywhere = pl.BlockSpec(memory_space=pl.ANY)
    local = pl.BlockSpec(memory_space=pltpu.VMEM)
    return pl.pallas_call(
        finish_kernel,
        out_shape=[
            jax.ShapeDtypeStruct((CELLS, CH), BF),
            jax.ShapeDtypeStruct((TAPS, CH, CH), F32),
            jax.ShapeDtypeStruct((1, CH), F32),
            jax.ShapeDtypeStruct((CAP, DEV, CH), BF),
        ],
        in_specs=[anywhere, anywhere, anywhere, local],
        out_specs=[anywhere, anywhere, local, anywhere],
        scratch_shapes=[
            vm((CELLS, CH), BF),
            vm((2, CHUNKS, 16, CH), BF),
            vm((DEV, CAP, CH), BF),
            vm((TAPS, CH, CH), F32),
            vm((2, SLOTS, 128), F32),
            vm((CAP, DEV, CH), BF),
            pltpu.SemaphoreType.DMA((3,)),
            pltpu.SemaphoreType.DMA((16,)),
        ],
        compiler_params=pltpu.CompilerParams(vmem_limit_bytes=56 * 2**20),
        name="finish",
    )(encoded, sums, ret, bias_sum)


def body(features, offsets, counts, cell_index, kern, conv_bias, cotangent):
    encoded, sums, ret, bias_sum = fused(
        features[0], offsets[:, 0], counts, cell_index[0], kern.reshape(3, 3 * CH, CH),
        conv_bias.reshape(1, CH), cotangent.reshape(CELLS, CH),
    )
    encoded, weight_grad, bias_grad, obs_grad = finish(encoded, sums, ret, bias_sum)
    return (
        encoded.reshape(ROWS, COLS, CH),
        weight_grad.reshape(3, 3, CH, CH),
        bias_grad.reshape(CH),
        obs_grad[None],
    )


def solution(mesh):
    return jax.shard_map(
        body,
        mesh=mesh,
        in_specs=(
            P(("lat", "lon"), None, None, None),
            P(None, ("lat", "lon"), None, None),
            P(("lat", "lon"), None),
            P(("lat", "lon"), None, None),
            P(),
            P(),
            P("lat", "lon", None),
        ),
        out_specs=(P("lat", "lon", None), P(), P(), P(("lat", "lon"), None, None, None)),
        check_vma=False,
    )
```

```python
import functools
import math

import jax
import jax.numpy as jnp
from jax import lax
from jax.experimental import pallas as pl
from jax.experimental.pallas import tpu as pltpu
from jax.sharding import PartitionSpec as P

BF = jnp.bfloat16
F32 = jnp.float32
MESH = pl.DeviceIdType.MESH
ROWS, COLS, CH, CAP = 32, 128, 256, 16
NLAT, NLON = 8, 16
DEV = NLAT * NLON
SLOTS = DEV * CAP
CELLS = ROWS * COLS
PAIRS = DEV // 2
CHIPS = NLON // 2
CHUNKS = 72
TAPS = 9
LAG = 2


def iota(shape, dim):
    return lax.broadcasted_iota(jnp.int32, shape, dim)


def fiota(shape, dim):
    return iota(shape, dim).astype(F32)


def aligned(value, unit=128):
    return pl.multiple_of(value, unit)


def remote(src, dst, send, recv, lat, lon):
    return pltpu.make_async_remote_copy(
        src_ref=src, dst_ref=dst, send_sem=send, recv_sem=recv, device_id=(lat, lon), device_id_type=MESH
    )


def wait_bytes(ref, sem):
    pltpu.make_async_copy(ref, ref, sem).wait()


def expand_lanes(meta, onehot, wrf, wrb, dens, edges, edge_inv):
    per_dev = meta[...].reshape(DEV, 128).astype(BF)
    lane = iota((128, 384), 1)
    pick = jnp.where(iota((128, 384), 0) == (lane // 128) * CAP + lane % CAP, 1.0, 0.0).astype(BF)
    spread = jnp.dot(per_dev, pick, preferred_element_type=F32).reshape(16, 8, 384)
    lane8 = iota((8, 384), 1)
    mine = jnp.where(iota((8, 384), 0) == (lane8 % 128) // CAP, 1.0, 0.0)
    flat = (spread * mine[None]).sum(1)
    total = jnp.zeros((2 * ROWS, 128), F32)
    for g in range(16):
        wide = slice(g * 128, g * 128 + 128)
        w, row, col = flat[g : g + 1, 0:128], flat[g : g + 1, 128:256], flat[g : g + 1, 256:384]
        onehot[:, wide] = jnp.where(fiota((COLS, 128), 0) == col, 1.0, 0.0).astype(BF)
        by_row = jnp.where(fiota((ROWS, 128), 0) == row, w, 0.0)
        wrf[:, wide] = by_row
        first = jnp.where(col == 0.0, by_row, 0.0)
        last = jnp.where(col == float(COLS - 1), by_row, 0.0)
        both = jnp.concatenate([first, last], 0)
        edges[:, wide] = both.astype(BF)
        total = total + both
    edge_inv[...] = jnp.broadcast_to(1.0 / (total.sum(1, keepdims=True) + 1.0), (2 * ROWS, 128))

    def widen(r, _):
        wrb[r] = jnp.broadcast_to(wrf[pl.ds(r, 1), :], (16, SLOTS)).astype(BF)
        return 0

    lax.fori_loop(0, ROWS, widen, 0)
    density = lax.dot_general(
        onehot[...], wrf[...].astype(BF), (((1,), (1,)), ((), ())), preferred_element_type=F32
    )
    inv = 1.0 / (density + 1.0)
    for r in range(ROWS):
        dens[r * COLS : (r + 1) * COLS, :] = jnp.broadcast_to(inv[:, r : r + 1], (COLS, 128))


def expand_rows(meta, col_weight, row_of):
    lane = iota((128, 384), 1)
    pick = jnp.where(iota((128, 384), 0) // CAP == lane // 128, 1.0, 0.0).astype(BF)
    slot_lane = iota((CAP, 128), 1)
    mine = jnp.where(slot_lane % CAP == iota((CAP, 128), 0), 1.0, 0.0)

    def step(i, _):
        block = meta[pl.ds(i * 16, 16)]
        masked = (jnp.broadcast_to(block, (16, CAP, 128)) * mine[None]).reshape(256, 128).astype(BF)
        spread = jnp.dot(masked, pick, preferred_element_type=F32)
        base = aligned(i * 256, 256)
        col_weight[pl.ds(base, 256), :] = jnp.where(
            spread[:, 256:384] == fiota((256, 128), 1), spread[:, 0:128], 0.0
        ).astype(BF)
        row_of[pl.ds(base, 256), :] = spread[:, 128:256].astype(BF)
        return 0

    lax.fori_loop(0, DEV // 16, step, 0)


def twice(inv):
    return jnp.concatenate([inv, inv], 1)


def splat_edges(feats, onehot, wrb, dens, edges, edge_inv, rows_out, cols_out):
    hot = onehot[...].reshape(8, 16, SLOTS)
    lhs = jnp.concatenate(
        [(hot * wrb[0][None]).reshape(COLS, SLOTS), (hot * wrb[ROWS - 1][None]).reshape(COLS, SLOTS), edges[...]], 0
    )
    acc = jnp.dot(lhs, feats[...].reshape(SLOTS, CH), preferred_element_type=F32)
    rows_out[0] = (acc[0:COLS] * twice(dens[0:COLS, :])).astype(BF)
    rows_out[1] = (acc[COLS : 2 * COLS] * twice(dens[CELLS - COLS : CELLS, :])).astype(BF)
    cols = (acc[2 * COLS :] * twice(edge_inv[...])).astype(BF)
    cols_out[0] = cols[0:ROWS]
    cols_out[1] = cols[ROWS:]


def splat(feats, onehot, wrb, dens, x3, per=4):
    def step(i, _):
        r0 = i * per
        hot = onehot[...].reshape(8, 16, SLOTS)
        lhs = jnp.concatenate([(hot * wrb[r0 + k][None]).reshape(COLS, SLOTS) for k in range(per)], 0)
        acc = jnp.dot(lhs, feats[...].reshape(SLOTS, CH), preferred_element_type=F32)
        for k in range(per):
            base = aligned((r0 + k) * COLS)
            field = (acc[k * COLS : (k + 1) * COLS] * twice(dens[pl.ds(base, COLS), :])).astype(BF)
            wide = field.astype(F32)
            x3[pl.ds(base + COLS, COLS), 256:512] = field
            x3[pl.ds(base + COLS, COLS), 0:256] = pltpu.roll(wide, 1, 0).astype(BF)
            x3[pl.ds(base + COLS, COLS), 512:768] = pltpu.roll(wide, COLS - 1, 0).astype(BF)
        return 0

    lax.fori_loop(0, ROWS // per, step, 0)


def exchange_edges(lat, lon, rows, cols, h_row, h_col, h_cor, sems):
    up, down = lax.rem(lat + NLAT - 1, NLAT), lax.rem(lat + 1, NLAT)
    west, east = lax.rem(lon + NLON - 1, NLON), lax.rem(lon + 1, NLON)
    plan = (
        (rows[0], h_row.at[1], up, lon),
        (rows[1], h_row.at[0], down, lon),
        (cols.at[0], h_col.at[1], lat, west),
        (cols.at[1], h_col.at[0], lat, east),
        (cols.at[1, pl.ds(16, 16)], h_cor.at[0], down, east),
        (cols.at[0, pl.ds(16, 16)], h_cor.at[1], down, west),
        (cols.at[1, pl.ds(0, 16)], h_cor.at[2], up, east),
        (cols.at[0, pl.ds(0, 16)], h_cor.at[3], up, west),
    )
    return [remote(s, d, sems.at[0, i], sems.at[1, i], a, b) for i, (s, d, a, b) in enumerate(plan)]


def patch(arr, lat, h_row, h_col, h_cor, col_vals, left, right):
    top = jnp.where(lat == 0, 0.0, 1.0)
    bottom = jnp.where(lat == NLAT - 1, 0.0, 1.0)
    for side in range(2):
        col_vals[side, 0:32, :] = h_col[side].astype(F32)
        col_vals[side, 32:40, :] = jnp.broadcast_to(h_cor[side].astype(F32)[15:16] * top, (8, CH))
        col_vals[side, 40:48, :] = jnp.broadcast_to(h_cor[2 + side].astype(F32)[0:1] * bottom, (8, CH))
    sub = iota((16, CH), 0)

    def step(r, _):
        base = aligned((r + 1) * COLS)
        old = arr[pl.ds(base, 16), left : left + CH].astype(F32)
        arr[pl.ds(base, 16), left : left + CH] = jnp.where(sub == 0, col_vals[0, pl.ds(r, 1), :], old).astype(BF)
        far = aligned(base + COLS - 16, 16)
        old = arr[pl.ds(far, 16), right : right + CH].astype(F32)
        arr[pl.ds(far, 16), right : right + CH] = jnp.where(sub == 15, col_vals[1, pl.ds(r, 1), :], old).astype(BF)
        return 0

    lax.fori_loop(0, ROWS, step, 0)
    full = iota((COLS, CH), 0)
    for side, (base, keep) in enumerate(((0, top), ((ROWS + 1) * COLS, bottom))):
        at = 32 + 8 * side
        wide = h_row[side].astype(F32) * keep
        arr[base : base + COLS, 256:512] = wide.astype(BF)
        arr[base : base + COLS, left : left + CH] = jnp.where(
            full == 0, col_vals[0, at : at + 1, :], pltpu.roll(wide, 1, 0)
        ).astype(BF)
        arr[base : base + COLS, right : right + CH] = jnp.where(
            full == COLS - 1, col_vals[1, at : at + 1, :], pltpu.roll(wide, COLS - 1, 0)
        ).astype(BF)


def conv(x3, kc, bias, cot, enc, g3, gsum, gcol, per=8):
    gsum[...] = jnp.zeros_like(gsum)

    def step(i, _):
        r0 = i * per
        acc = jnp.broadcast_to(bias[...], (per * COLS, CH))
        for a in range(3):
            acc = acc + jnp.dot(
                x3[pl.ds(aligned((r0 + a) * COLS), per * COLS), :], kc[a], preferred_element_type=F32
            )
        base = aligned(r0 * COLS)
        gate = 0.5 * jnp.tanh(0.5 * acc) + 0.5
        silu = acc * gate
        field = x3[pl.ds(base + COLS, per * COLS), 256:512].astype(F32)
        enc[pl.ds(base, per * COLS), :] = (field + silu).astype(BF)
        grad = (cot[pl.ds(base, per * COLS), :].astype(F32) * (gate + silu * (1.0 - gate))).astype(BF)
        wide = grad.astype(F32)
        gsum[...] += wide.reshape(per * COLS // 8, 8, CH).sum(0)
        g3[pl.ds(base + COLS, per * COLS), 256:512] = grad
        for k in range(per):
            row = wide[k * COLS : (k + 1) * COLS]
            at = pl.ds(base + COLS + k * COLS, COLS)
            g3[at, 0:256] = pltpu.roll(row, COLS - 1, 0).astype(BF)
            g3[at, 512:768] = pltpu.roll(row, 1, 0).astype(BF)
            gcol[0, pl.ds(r0 + k, 1), :] = row[0:1]
            gcol[1, pl.ds(r0 + k, 1), :] = row[COLS - 1 : COLS]
        return 0

    lax.fori_loop(0, ROWS // per, step, 0)


def wgrad_tap(step, tap, x3, g3, dw):
    rows, lanes = pl.ds(aligned(tap // 3 * COLS), CELLS), pl.ds(aligned(lax.rem(tap, 3) * CH), CH)
    dw[step] = lax.dot_general(
        x3[rows, lanes], g3[COLS : COLS + CELLS, CH : 2 * CH], (((0,), (0,)), ((), ())), preferred_element_type=F32
    )


def grad_band(i, col_weight, row_of, scaled, slot_grad):
    base = aligned(i * 256, 256)
    weight, row = col_weight[pl.ds(base, 256), :], row_of[pl.ds(base, 256), :]
    lhs = jnp.concatenate(
        [jnp.where(row == jnp.array(r, BF), weight, jnp.zeros_like(weight)) for r in range(ROWS)], 1
    )
    grads = jnp.dot(lhs, scaled[...], preferred_element_type=F32).astype(BF)
    slot_grad[pl.ds(i * 16, 16)] = grads.reshape(16, CAP, CH)


def transpose_kernel(kc, kt):
    for a in range(3):
        for b in range(3):
            kt[a, b * CH : (b + 1) * CH, :] = kc[a, b * CH : (b + 1) * CH, :].T


def back_conv(first, count, g3, kt, cot, dens, scaled, per=8):
    def step(i, _):
        r0 = first + i * per
        base = aligned(r0 * COLS)
        acc = cot[pl.ds(base, per * COLS), :].astype(F32)
        for a in range(3):
            acc = acc + jnp.dot(
                g3[pl.ds(aligned((r0 + 2 - a) * COLS), per * COLS), :], kt[a], preferred_element_type=F32
            )
        scaled[pl.ds(base, per * COLS), :] = (acc * twice(dens[pl.ds(base, per * COLS), :])).astype(BF)
        return 0

    lax.fori_loop(0, count // per, step, 0)


def place(p):
    q = lax.rem(p, 16)
    a = q // 2
    return a, lax.rem(2 * (p // 16 + a) + lax.rem(q, 2), NLON)


def spread_over(j):
    b = lax.rem(j, CHIPS)
    return lax.rem(j // CHIPS + b, NLAT), b


def slot_meta(offsets, counts, cells, turned, meta_src):
    live = iota((CAP, DEV), 0) < counts[...]
    radius = offsets[0] * offsets[0] + offsets[1] * offsets[1]
    weight = jnp.where(live, jnp.exp(-2.0 * radius), 0.0)
    row, col = cells[...] // COLS, cells[...] % COLS
    table = jnp.concatenate([weight, row.astype(F32), col.astype(F32), jnp.zeros((128 - 3 * CAP, DEV), F32)], 0)
    turned[...] = table.T

    def step(t, _):
        meta_src[lax.rem(t, NLON), t // NLON] = turned[pl.ds(t, 1), :]
        return 0

    lax.fori_loop(0, DEV, step, 0, unroll=8)


def turn_slots(by_slot, wide, by_dest):
    flat = by_slot[...].reshape(SLOTS, CH).astype(F32)
    wide[0], wide[1] = flat[:, :128], flat[:, 128:]

    def step(t, _):
        halves = [wide[h, pl.ds(t, CAP, stride=DEV), :] for h in range(2)]
        by_dest[t] = jnp.concatenate(halves, 1).astype(BF)
        return 0

    lax.fori_loop(0, DEV, step, 0, unroll=8)


def kernel(
    feat_in, offsets, counts, cells, kern_in, bias, cot_in,
    enc_out, sums_out, ret_out, bias_out,
    by_slot, wide, by_dest, turned, meta_src, meta_mid, meta_nat,
    feats, meta, kc, kt, cot, enc, onehot, wrf, wrb, dens, edges, edge_inv, col_weight, row_of,
    edge_rows, edge_cols, h_row, h_col, h_cor, col_vals, x3, g3, gsum, gcol, grad_cols, scaled, slot_grad,
    dw, pair_dw, pair_sum, half, rs, reduced, bias_lat, bias_mid, bias_lon, tail_chip, tail_lat, tail_part, tail_sum,
    round_sem, load_sems, a2a_sems, halo_sems, grad_halo_sems, pair_sems, rs_sems, ag_sems, swap_sems, ret_sems, bias_sems, tail_sems,
):
    lat, lon = lax.axis_index("lat"), lax.axis_index("lon")
    me = lat * NLON + lon
    core = lax.rem(lon, 2)
    mate = lon + 1 - 2 * core
    chip = lon // 2
    owner = lat * CHIPS + chip
    mine = lax.rem(lat - chip + CHIPS, CHIPS) * CHIPS + chip

    def over_lat(j):
        return lax.rem(lat + j, NLAT)

    def over_lon(j):
        return lax.rem(lon + j, NLON)

    load_feat = pltpu.make_async_copy(feat_in, by_slot, load_sems.at[1])
    load_kern = pltpu.make_async_copy(kern_in, kc, load_sems.at[2])
    load_cot = pltpu.make_async_copy(cot_in, cot, load_sems.at[3])
    load_feat.start()
    load_kern.start()
    load_cot.start()

    barrier = pltpu.get_barrier_semaphore()

    def greet_lon(j, _):
        pl.semaphore_signal(barrier, inc=1, device_id=(lat, over_lon(j)), device_id_type=MESH)
        return 0

    def greet_lat(j, _):
        pl.semaphore_signal(barrier, inc=1, device_id=(over_lat(j), lon), device_id_type=MESH)
        return 0

    def vouch(j, _):
        pl.semaphore_signal(round_sem, inc=1, device_id=(over_lat(j), lon), device_id_type=MESH)
        return 0

    lax.fori_loop(1, NLON, greet_lon, 0)
    lax.fori_loop(1, NLAT, greet_lat, 0)
    slot_meta(offsets, counts, cells, turned, meta_src)
    pl.semaphore_wait(barrier, NLON + NLAT - 2)
    lax.fori_loop(1, NLAT, vouch, 0)

    def meta_lon(j, _):
        to = over_lon(j)
        remote(meta_src.at[to], meta_mid.at[lon], a2a_sems.at[0], a2a_sems.at[1], lat, to).start()
        return 0

    def meta_lat(j, _):
        to = over_lat(j)
        remote(meta_mid.at[pl.ds(0, NLON), to], meta_nat.at[lat], a2a_sems.at[2], a2a_sems.at[3], to, lon).start()
        return 0

    def send_feats(p, _):
        a, b = place(p)
        to_lat, to_lon = lax.rem(lat - a + NLAT, NLAT), lax.rem(lon - b + NLON, NLON)
        remote(by_dest.at[to_lat * NLON + to_lon], feats.at[p], a2a_sems.at[4], a2a_sems.at[5], to_lat, to_lon).start()
        return 0

    lax.fori_loop(1, NLON, meta_lon, 0)
    meta_mid[lon] = meta_src[lon]
    load_feat.wait()
    turn_slots(by_slot, wide, by_dest)
    pl.semaphore_wait(round_sem, NLAT - 1)
    lax.fori_loop(1, DEV // 2, send_feats, 0)
    wait_bytes(meta_mid.at[pl.ds(0, NLON - 1)], a2a_sems.at[1])
    lax.fori_loop(1, NLAT, meta_lat, 0)
    meta_nat[lat] = meta_mid[:, lat]
    lax.fori_loop(DEV // 2, DEV, send_feats, 0)
    feats[0] = by_dest[me]

    load_kern.wait()
    transpose_kernel(kc, kt)
    wait_bytes(meta_nat.at[pl.ds(0, NLAT - 1)], a2a_sems.at[3])

    def reorder(p, _):
        a, b = place(p)
        meta[p] = meta_nat[over_lat(a), over_lon(b)]
        return 0

    lax.fori_loop(0, DEV, reorder, 0, unroll=4)
    expand_lanes(meta, onehot, wrf, wrb, dens, edges, edge_inv)
    expand_rows(meta, col_weight, row_of)

    wait_bytes(feats.at[pl.ds(0, DEV - 1)], a2a_sems.at[5])
    splat_edges(feats, onehot, wrb, dens, edges, edge_inv, edge_rows, edge_cols)
    halo = exchange_edges(
        lat, lon, (edge_rows.at[0], edge_rows.at[1]), edge_cols, h_row.at[0], h_col.at[0], h_cor.at[0], halo_sems
    )
    for copy in halo:
        copy.start()
    splat(feats, onehot, wrb, dens, x3)
    for copy in halo:
        copy.wait_recv()
    patch(x3, lat, h_row.at[0], h_col.at[0], h_cor.at[0], col_vals, 0, 512)

    load_cot.wait()
    conv(x3, kc, bias, cot, enc, g3, gsum, gcol)
    store_enc = pltpu.make_async_copy(enc, enc_out, load_sems.at[4])
    store_enc.start()
    grad_cols[...] = gcol[...].astype(BF)
    last = ROWS * COLS
    grad_halo = exchange_edges(
        lat, lon, (g3.at[pl.ds(COLS, COLS), pl.ds(CH, CH)], g3.at[pl.ds(last, COLS), pl.ds(CH, CH)]),
        grad_cols, h_row.at[1], h_col.at[1], h_cor.at[1], grad_halo_sems,
    )
    for copy in grad_halo:
        copy.start()

    pair_bias = remote(gsum, pair_sum, pair_sems.at[0, TAPS], pair_sems.at[1, TAPS], lat, mate)
    pair_bias.start()
    taps = [jnp.int32(8)] + [lax.rem(lat + chip + i, 8) for i in range(8)]
    pair = []

    def pair_total(step):
        pair[step].wait()
        total = dw[step, pl.ds(aligned(128 * core), 128), :] + pair_dw[step]
        half[step] = total.astype(BF).reshape(8, 16, CH)

    def last_tap_rows():
        pair_total(0)
        tail_chip[chip] = half[0, chip]

        def step(j, _):
            to = lax.rem(chip + j, CHIPS)
            remote(half.at[0, to], tail_chip.at[chip], tail_sems.at[0], tail_sems.at[1], lat, to * 2 + core).start()
            return 0

        lax.fori_loop(1, CHIPS, step, 0)

    def last_tap_columns():
        wait_bytes(tail_chip.at[pl.ds(0, CHIPS - 1)], tail_sems.at[1])
        tail_part[...] = tail_chip[...].astype(F32).sum(0).astype(BF)
        tail_lat[lat] = tail_part[...]

        def step(j, _):
            remote(tail_part, tail_lat.at[lat], tail_sems.at[2], tail_sems.at[3], over_lat(j), lon).start()
            return 0

        lax.fori_loop(1, NLAT, step, 0)

    def last_tap_gather():
        wait_bytes(tail_lat.at[pl.ds(0, NLAT - 1)], tail_sems.at[3])
        tail_sum[...] = tail_lat[...].astype(F32).sum(0).astype(BF)
        spot = sums_out.at[core, PAIRS + chip]
        pltpu.make_async_copy(tail_sum, spot, load_sems.at[6]).start()

        def step(j, _):
            to = lax.rem(chip + j, CHIPS)
            remote(tail_sum, spot, tail_sems.at[4], tail_sems.at[5], lat, to * 2 + core).start()
            return 0

        lax.fori_loop(1, CHIPS, step, 0)

    def bias_columns():
        pair_bias.wait()
        bias_lat[lat] = gsum[...] + pair_sum[...]

        def step(j, _):
            remote(bias_lat.at[lat], bias_lat.at[lat], bias_sems.at[0], bias_sems.at[1], over_lat(j), lon).start()
            return 0

        lax.fori_loop(1, NLAT, step, 0)

    def bias_rows():
        wait_bytes(bias_lat.at[pl.ds(0, NLAT - 1)], bias_sems.at[1])
        bias_mid[...] = bias_lat[...].sum(0)
        bias_lon[chip] = bias_mid[...]

        def step(j, _):
            to = lax.rem(chip + j, CHIPS)
            remote(bias_mid, bias_lon.at[chip], bias_sems.at[2], bias_sems.at[3], lat, to * 2 + core).start()
            return 0

        lax.fori_loop(1, CHIPS, step, 0)

    def send_tap(step):
        pair_total(step)
        tap = taps[step]

        def send(m, _):
            to_lat = lax.rem(tap + m, NLAT)
            here = jnp.logical_and(to_lat == lat, m == chip)

            @pl.when(jnp.logical_not(here))
            def _():
                remote(
                    half.at[step, m], rs.at[owner], rs_sems.at[0], rs_sems.at[1], to_lat, m * 2 + core
                ).start()

            @pl.when(here)
            def _():
                rs[owner] = half[step, m]

            return 0

        lax.fori_loop(0, CHIPS, send, 0)

    def send_pair(step):
        pair.append(
            remote(
                dw.at[step, pl.ds(aligned(128 * (1 - core)), 128)], pair_dw.at[step],
                pair_sems.at[0, step], pair_sems.at[1, step], lat, mate,
            )
        )
        pair[-1].start()

    beside = {3: last_tap_rows, 6: bias_columns}
    for step in range(TAPS):
        wgrad_tap(step, taps[step], x3, g3, dw)
        send_pair(step)
        if step in beside:
            beside[step]()
        if step > LAG:
            send_tap(step - LAG)

    for copy in grad_halo:
        copy.wait()
    patch(g3, lat, h_row.at[1], h_col.at[1], h_cor.at[1], col_vals, 512, 0)
    for step in range(TAPS - LAG, TAPS):
        send_tap(step)

    last_tap_columns()
    bias_rows()
    back_conv(0, ROWS // 2, g3, kt, cot, dens, scaled)

    wait_bytes(rs.at[pl.ds(0, PAIRS - 1)], rs_sems.at[1])
    reduced[...] = rs[...].astype(F32).sum(0).astype(BF)
    own_sum = pltpu.make_async_copy(reduced, sums_out.at[core, mine], load_sems.at[5])
    own_sum.start()

    def send_sum(j, _):
        a, b = spread_over(j)
        to_chip = lax.rem(chip + b, CHIPS)
        remote(
            reduced, sums_out.at[core, mine], ag_sems.at[0], ag_sems.at[1], over_lat(a), to_chip * 2 + core
        ).start()
        return 0

    lax.fori_loop(1, PAIRS, send_sum, 0)
    back_conv(ROWS // 2, ROWS // 2, g3, kt, cot, dens, scaled)
    last_tap_gather()

    def band(i, _):
        grad_band(i, col_weight, row_of, scaled, slot_grad)

        def back(j, _):
            p = i * 16 + j
            a, b = place(p)

            @pl.when(p != 0)
            def _():
                remote(
                    slot_grad.at[p], ret_out.at[me], ret_sems.at[0], ret_sems.at[1], over_lat(a), over_lon(b)
                ).start()

            return 0

        lax.fori_loop(0, 16, back, 0)
        return 0

    lax.fori_loop(0, 6, band, 0)

    own_sum.wait()
    pltpu.make_async_copy(tail_sum, sums_out.at[core, PAIRS + chip], load_sems.at[6]).wait()
    wait_bytes(sums_out.at[core, pl.ds(0, PAIRS - 1)], ag_sems.at[1])
    wait_bytes(sums_out.at[core, pl.ds(0, CHIPS - 1)], tail_sems.at[5])
    swap = remote(sums_out.at[core], sums_out.at[core], swap_sems.at[0], swap_sems.at[1], lat, mate)
    swap.start()

    lax.fori_loop(6, DEV // 16, band, 0)
    own_ret = pltpu.make_async_copy(slot_grad.at[0], ret_out.at[me], load_sems.at[7])
    own_ret.start()
    wait_bytes(bias_lon.at[pl.ds(0, CHIPS - 1)], bias_sems.at[3])
    bias_out[...] = bias_lon[...].sum(0).sum(0, keepdims=True)

    wait_bytes(meta_mid.at[pl.ds(0, NLON - 1)], a2a_sems.at[0])
    wait_bytes(meta_nat.at[pl.ds(0, NLAT - 1)], a2a_sems.at[2])
    wait_bytes(feats.at[pl.ds(0, DEV - 1)], a2a_sems.at[4])
    wait_bytes(bias_lat.at[pl.ds(0, NLAT - 1)], bias_sems.at[0])
    wait_bytes(bias_lon.at[pl.ds(0, CHIPS - 1)], bias_sems.at[2])
    wait_bytes(tail_chip.at[pl.ds(0, CHIPS - 1)], tail_sems.at[0])
    wait_bytes(tail_lat.at[pl.ds(0, NLAT - 1)], tail_sems.at[2])
    wait_bytes(tail_chip.at[pl.ds(0, CHIPS - 1)], tail_sems.at[4])
    wait_bytes(rs.at[pl.ds(0, PAIRS - 1)], rs_sems.at[0])
    wait_bytes(rs.at[pl.ds(0, PAIRS - 1)], ag_sems.at[0])
    for copy in halo:
        copy.wait_send()
    store_enc.wait()
    own_ret.wait()
    wait_bytes(slot_grad.at[pl.ds(0, DEV - 1)], ret_sems.at[0])
    wait_bytes(ret_out.at[pl.ds(0, DEV - 1)], ret_sems.at[1])
    swap.wait()


def fused(feat, offsets, counts, cells, kern, bias, cot):
    vm = pltpu.VMEM
    dma = pltpu.SemaphoreType.DMA
    scratch = [
        vm((CAP, DEV, CH), BF),
        vm((2, SLOTS, 128), F32),
        vm((DEV, CAP, CH), BF),
        vm((DEV, 128), F32),
        vm((NLON, NLAT, 1, 128), F32),
        vm((NLON, NLAT, 1, 128), F32),
        vm((NLAT, NLON, 1, 128), F32),
        vm((DEV, CAP, CH), BF),
        vm((DEV, 1, 128), F32),
        vm((3, 3 * CH, CH), BF),
        vm((3, 3 * CH, CH), BF),
        vm((CELLS, CH), BF),
        vm((CELLS, CH), BF),
        vm((COLS, SLOTS), BF),
        vm((ROWS, SLOTS), F32),
        vm((ROWS, 16, SLOTS), BF),
        vm((CELLS, 128), F32),
        vm((2 * ROWS, SLOTS), BF),
        vm((2 * ROWS, 128), F32),
        vm((SLOTS, 128), BF),
        vm((SLOTS, 128), BF),
        vm((2, COLS, CH), BF),
        vm((2, ROWS, CH), BF),
        vm((2, 2, COLS, CH), BF),
        vm((2, 2, ROWS, CH), BF),
        vm((2, 4, 16, CH), BF),
        vm((2, 48, CH), F32),
        vm(((ROWS + 2) * COLS, 3 * CH), BF),
        vm(((ROWS + 2) * COLS, 3 * CH), BF),
        vm((8, CH), F32),
        vm((2, ROWS, CH), F32),
        vm((2, ROWS, CH), BF),
        vm((CELLS, CH), BF),
        vm((DEV, CAP, CH), BF),
        vm((TAPS, CH, CH), F32),
        vm((TAPS, 128, CH), F32),
        vm((8, CH), F32),
        vm((TAPS, CHIPS, 16, CH), BF),
        vm((PAIRS, 16, CH), BF),
        vm((16, CH), BF),
        vm((NLAT, 8, CH), F32),
        vm((8, CH), F32),
        vm((CHIPS, 8, CH), F32),
        vm((CHIPS, 16, CH), BF),
        vm((NLAT, 16, CH), BF),
        vm((16, CH), BF),
        vm((16, CH), BF),
        pltpu.SemaphoreType.REGULAR,
        dma((8,)),
        dma((6,)),
        dma((2, 8)),
        dma((2, 8)),
        dma((2, 10)),
        dma((2,)),
        dma((2,)),
        dma((2,)),
        dma((2,)),
        dma((4,)),
        dma((6,)),
    ]
    anywhere = pl.BlockSpec(memory_space=pl.ANY)
    local = pl.BlockSpec(memory_space=pltpu.VMEM)
    return pl.pallas_call(
        kernel,
        out_shape=[
            jax.ShapeDtypeStruct((CELLS, CH), BF),
            jax.ShapeDtypeStruct((2, CHUNKS, 16, CH), BF),
            jax.ShapeDtypeStruct((DEV, CAP, CH), BF),
            jax.ShapeDtypeStruct((1, CH), F32),
        ],
        in_specs=[anywhere, local, local, local, anywhere, local, anywhere],
        out_specs=[anywhere, anywhere, anywhere, local],
        scratch_shapes=scratch,
        compiler_params=pltpu.CompilerParams(collective_id=0, has_side_effects=True, vmem_limit_bytes=60 * 2**20),
        name="fused",
    )(feat, offsets, counts, cells, kern, bias, cot)


def finish_kernel(
    enc_in, sums_in, ret_in, bias_in, enc_out, grad_out, bias_out, obs_out, enc, sums, ret, grad, wide, obs, sems, out_sems
):
    scale = 1.0 / math.sqrt(CELLS * DEV)
    load_ret = pltpu.make_async_copy(ret_in, ret, sems.at[0])
    load_sums = pltpu.make_async_copy(sums_in, sums, sems.at[1])
    load_enc = pltpu.make_async_copy(enc_in, enc, sems.at[2])
    load_sums.start()
    load_ret.start()
    load_enc.start()
    bias_out[...] = bias_in[...] * scale
    copies = []

    def store(src, dst):
        copies.append(pltpu.make_async_copy(src, dst, out_sems.at[len(copies)]))
        copies[-1].start()

    load_sums.wait()
    for tap in range(TAPS):
        for core in range(2):
            rows = sums[core, tap * CHIPS : (tap + 1) * CHIPS].reshape(128, CH)
            grad[tap, core * 128 : (core + 1) * 128, :] = rows.astype(F32) * scale
        store(grad.at[tap], grad_out.at[tap])
    load_enc.wait()
    store(enc, enc_out)
    load_ret.wait()
    flat = ret[...].reshape(SLOTS, CH).astype(F32)
    wide[0], wide[1] = flat[:, :128], flat[:, 128:]
    for k in range(CAP):
        halves = [wide[h, pl.ds(k, DEV, stride=CAP), :] for h in range(2)]
        obs[k] = jnp.concatenate(halves, 1).astype(BF)
        if k % 4 == 3:
            store(obs.at[pl.ds(k - 3, 4)], obs_out.at[pl.ds(k - 3, 4)])
    for copy in copies:
        copy.wait()


def finish(encoded, sums, ret, bias_sum):
    vm = pltpu.VMEM
    anywhere = pl.BlockSpec(memory_space=pl.ANY)
    local = pl.BlockSpec(memory_space=pltpu.VMEM)
    return pl.pallas_call(
        finish_kernel,
        out_shape=[
            jax.ShapeDtypeStruct((CELLS, CH), BF),
            jax.ShapeDtypeStruct((TAPS, CH, CH), F32),
            jax.ShapeDtypeStruct((1, CH), F32),
            jax.ShapeDtypeStruct((CAP, DEV, CH), BF),
        ],
        in_specs=[anywhere, anywhere, anywhere, local],
        out_specs=[anywhere, anywhere, local, anywhere],
        scratch_shapes=[
            vm((CELLS, CH), BF),
            vm((2, CHUNKS, 16, CH), BF),
            vm((DEV, CAP, CH), BF),
            vm((TAPS, CH, CH), F32),
            vm((2, SLOTS, 128), F32),
            vm((CAP, DEV, CH), BF),
            pltpu.SemaphoreType.DMA((3,)),
            pltpu.SemaphoreType.DMA((16,)),
        ],
        compiler_params=pltpu.CompilerParams(vmem_limit_bytes=56 * 2**20),
        name="finish",
    )(encoded, sums, ret, bias_sum)


def body(features, offsets, counts, cell_index, kern, conv_bias, cotangent):
    encoded, sums, ret, bias_sum = fused(
        features[0], offsets[:, 0], counts, cell_index[0], kern.reshape(3, 3 * CH, CH),
        conv_bias.reshape(1, CH), cotangent.reshape(CELLS, CH),
    )
    encoded, weight_grad, bias_grad, obs_grad = finish(encoded, sums, ret, bias_sum)
    return (
        encoded.reshape(ROWS, COLS, CH),
        weight_grad.reshape(3, 3, CH, CH),
        bias_grad.reshape(CH),
        obs_grad[None],
    )


def solution(mesh):
    return jax.shard_map(
        body,
        mesh=mesh,
        in_specs=(
            P(("lat", "lon"), None, None, None),
            P(None, ("lat", "lon"), None, None),
            P(("lat", "lon"), None),
            P(("lat", "lon"), None, None),
            P(),
            P(),
            P("lat", "lon", None),
        ),
        out_specs=(P("lat", "lon", None), P(), P(), P(("lat", "lon"), None, None, None)),
        check_vma=False,
    )
```

```python
import functools
import math

import jax
import jax.numpy as jnp
from jax import lax
from jax.experimental import pallas as pl
from jax.experimental.pallas import tpu as pltpu
from jax.sharding import PartitionSpec as P

BF = jnp.bfloat16
F32 = jnp.float32
MESH = pl.DeviceIdType.MESH
ROWS, COLS, CH, CAP = 32, 128, 256, 16
NLAT, NLON = 8, 16
DEV = NLAT * NLON
SLOTS = DEV * CAP
CELLS = ROWS * COLS
PAIRS = DEV // 2
CHIPS = NLON // 2
CHUNKS = 72
TAPS = 9
LAG = 2


def iota(shape, dim):
    return lax.broadcasted_iota(jnp.int32, shape, dim)


def fiota(shape, dim):
    return iota(shape, dim).astype(F32)


def aligned(value, unit=128):
    return pl.multiple_of(value, unit)


def remote(src, dst, send, recv, lat, lon):
    return pltpu.make_async_remote_copy(
        src_ref=src, dst_ref=dst, send_sem=send, recv_sem=recv, device_id=(lat, lon), device_id_type=MESH
    )


def wait_bytes(ref, sem):
    pltpu.make_async_copy(ref, ref, sem).wait()


def expand_lanes(meta, onehot, wrf, wrb, dens, edges, edge_inv):
    per_dev = meta[...].reshape(DEV, 128).astype(BF)
    lane = iota((128, 384), 1)
    pick = jnp.where(iota((128, 384), 0) == (lane // 128) * CAP + lane % CAP, 1.0, 0.0).astype(BF)
    spread = jnp.dot(per_dev, pick, preferred_element_type=F32).reshape(16, 8, 384)
    lane8 = iota((8, 384), 1)
    mine = jnp.where(iota((8, 384), 0) == (lane8 % 128) // CAP, 1.0, 0.0)
    flat = (spread * mine[None]).sum(1)
    total = jnp.zeros((2 * ROWS, 128), F32)
    for g in range(16):
        wide = slice(g * 128, g * 128 + 128)
        w, row, col = flat[g : g + 1, 0:128], flat[g : g + 1, 128:256], flat[g : g + 1, 256:384]
        onehot[:, wide] = jnp.where(fiota((COLS, 128), 0) == col, 1.0, 0.0).astype(BF)
        by_row = jnp.where(fiota((ROWS, 128), 0) == row, w, 0.0)
        wrf[:, wide] = by_row
        first = jnp.where(col == 0.0, by_row, 0.0)
        last = jnp.where(col == float(COLS - 1), by_row, 0.0)
        both = jnp.concatenate([first, last], 0)
        edges[:, wide] = both.astype(BF)
        total = total + both
    edge_inv[...] = jnp.broadcast_to(1.0 / (total.sum(1, keepdims=True) + 1.0), (2 * ROWS, 128))

    def widen(r, _):
        wrb[r] = jnp.broadcast_to(wrf[pl.ds(r, 1), :], (16, SLOTS)).astype(BF)
        return 0

    lax.fori_loop(0, ROWS, widen, 0)
    density = lax.dot_general(
        onehot[...], wrf[...].astype(BF), (((1,), (1,)), ((), ())), preferred_element_type=F32
    )
    inv = 1.0 / (density + 1.0)
    for r in range(ROWS):
        dens[r * COLS : (r + 1) * COLS, :] = jnp.broadcast_to(inv[:, r : r + 1], (COLS, 128))


def expand_rows(meta, col_weight, row_of):
    lane = iota((128, 384), 1)
    pick = jnp.where(iota((128, 384), 0) // CAP == lane // 128, 1.0, 0.0).astype(BF)
    slot_lane = iota((CAP, 128), 1)
    mine = jnp.where(slot_lane % CAP == iota((CAP, 128), 0), 1.0, 0.0)

    def step(i, _):
        block = meta[pl.ds(i * 16, 16)]
        masked = (jnp.broadcast_to(block, (16, CAP, 128)) * mine[None]).reshape(256, 128).astype(BF)
        spread = jnp.dot(masked, pick, preferred_element_type=F32)
        base = aligned(i * 256, 256)
        col_weight[pl.ds(base, 256), :] = jnp.where(
            spread[:, 256:384] == fiota((256, 128), 1), spread[:, 0:128], 0.0
        ).astype(BF)
        row_of[pl.ds(base, 256), :] = spread[:, 128:256].astype(BF)
        return 0

    lax.fori_loop(0, DEV // 16, step, 0)


def twice(inv):
    return jnp.concatenate([inv, inv], 1)


def splat_edges(feats, onehot, wrb, dens, edges, edge_inv, rows_out, cols_out):
    hot = onehot[...].reshape(8, 16, SLOTS)
    lhs = jnp.concatenate(
        [(hot * wrb[0][None]).reshape(COLS, SLOTS), (hot * wrb[ROWS - 1][None]).reshape(COLS, SLOTS), edges[...]], 0
    )
    acc = jnp.dot(lhs, feats[...].reshape(SLOTS, CH), preferred_element_type=F32)
    rows_out[0] = (acc[0:COLS] * twice(dens[0:COLS, :])).astype(BF)
    rows_out[1] = (acc[COLS : 2 * COLS] * twice(dens[CELLS - COLS : CELLS, :])).astype(BF)
    cols = (acc[2 * COLS :] * twice(edge_inv[...])).astype(BF)
    cols_out[0] = cols[0:ROWS]
    cols_out[1] = cols[ROWS:]


def splat(feats, onehot, wrb, dens, x3, per=4):
    def step(i, _):
        r0 = i * per
        hot = onehot[...].reshape(8, 16, SLOTS)
        lhs = jnp.concatenate([(hot * wrb[r0 + k][None]).reshape(COLS, SLOTS) for k in range(per)], 0)
        acc = jnp.dot(lhs, feats[...].reshape(SLOTS, CH), preferred_element_type=F32)
        for k in range(per):
            base = aligned((r0 + k) * COLS)
            field = (acc[k * COLS : (k + 1) * COLS] * twice(dens[pl.ds(base, COLS), :])).astype(BF)
            wide = field.astype(F32)
            x3[pl.ds(base + COLS, COLS), 256:512] = field
            x3[pl.ds(base + COLS, COLS), 0:256] = pltpu.roll(wide, 1, 0).astype(BF)
            x3[pl.ds(base + COLS, COLS), 512:768] = pltpu.roll(wide, COLS - 1, 0).astype(BF)
        return 0

    lax.fori_loop(0, ROWS // per, step, 0)


def exchange_edges(lat, lon, rows, cols, h_row, h_col, h_cor, sems):
    up, down = lax.rem(lat + NLAT - 1, NLAT), lax.rem(lat + 1, NLAT)
    west, east = lax.rem(lon + NLON - 1, NLON), lax.rem(lon + 1, NLON)
    plan = (
        (rows[0], h_row.at[1], up, lon),
        (rows[1], h_row.at[0], down, lon),
        (cols.at[0], h_col.at[1], lat, west),
        (cols.at[1], h_col.at[0], lat, east),
        (cols.at[1, pl.ds(16, 16)], h_cor.at[0], down, east),
        (cols.at[0, pl.ds(16, 16)], h_cor.at[1], down, west),
        (cols.at[1, pl.ds(0, 16)], h_cor.at[2], up, east),
        (cols.at[0, pl.ds(0, 16)], h_cor.at[3], up, west),
    )
    return [remote(s, d, sems.at[0, i], sems.at[1, i], a, b) for i, (s, d, a, b) in enumerate(plan)]


def patch(arr, lat, h_row, h_col, h_cor, col_vals, left, right):
    top = jnp.where(lat == 0, 0.0, 1.0)
    bottom = jnp.where(lat == NLAT - 1, 0.0, 1.0)
    for side in range(2):
        col_vals[side, 0:32, :] = h_col[side].astype(F32)
        col_vals[side, 32:40, :] = jnp.broadcast_to(h_cor[side].astype(F32)[15:16] * top, (8, CH))
        col_vals[side, 40:48, :] = jnp.broadcast_to(h_cor[2 + side].astype(F32)[0:1] * bottom, (8, CH))
    sub = iota((16, CH), 0)

    def step(r, _):
        base = aligned((r + 1) * COLS)
        old = arr[pl.ds(base, 16), left : left + CH].astype(F32)
        arr[pl.ds(base, 16), left : left + CH] = jnp.where(sub == 0, col_vals[0, pl.ds(r, 1), :], old).astype(BF)
        far = aligned(base + COLS - 16, 16)
        old = arr[pl.ds(far, 16), right : right + CH].astype(F32)
        arr[pl.ds(far, 16), right : right + CH] = jnp.where(sub == 15, col_vals[1, pl.ds(r, 1), :], old).astype(BF)
        return 0

    lax.fori_loop(0, ROWS, step, 0)
    full = iota((COLS, CH), 0)
    for side, (base, keep) in enumerate(((0, top), ((ROWS + 1) * COLS, bottom))):
        at = 32 + 8 * side
        wide = h_row[side].astype(F32) * keep
        arr[base : base + COLS, 256:512] = wide.astype(BF)
        arr[base : base + COLS, left : left + CH] = jnp.where(
            full == 0, col_vals[0, at : at + 1, :], pltpu.roll(wide, 1, 0)
        ).astype(BF)
        arr[base : base + COLS, right : right + CH] = jnp.where(
            full == COLS - 1, col_vals[1, at : at + 1, :], pltpu.roll(wide, COLS - 1, 0)
        ).astype(BF)


def conv(x3, kc, bias, cot, enc, g3, gsum, gcol, per=8):
    gsum[...] = jnp.zeros_like(gsum)

    def step(i, _):
        r0 = i * per
        acc = jnp.broadcast_to(bias[...], (per * COLS, CH))
        for a in range(3):
            acc = acc + jnp.dot(
                x3[pl.ds(aligned((r0 + a) * COLS), per * COLS), :], kc[a], preferred_element_type=F32
            )
        base = aligned(r0 * COLS)
        gate = 0.5 * jnp.tanh(0.5 * acc) + 0.5
        silu = acc * gate
        field = x3[pl.ds(base + COLS, per * COLS), 256:512].astype(F32)
        enc[pl.ds(base, per * COLS), :] = (field + silu).astype(BF)
        grad = (cot[pl.ds(base, per * COLS), :].astype(F32) * (gate + silu * (1.0 - gate))).astype(BF)
        wide = grad.astype(F32)
        gsum[...] += wide.reshape(per * COLS // 8, 8, CH).sum(0)
        g3[pl.ds(base + COLS, per * COLS), 256:512] = grad
        for k in range(per):
            row = wide[k * COLS : (k + 1) * COLS]
            at = pl.ds(base + COLS + k * COLS, COLS)
            g3[at, 0:256] = pltpu.roll(row, COLS - 1, 0).astype(BF)
            g3[at, 512:768] = pltpu.roll(row, 1, 0).astype(BF)
            gcol[0, pl.ds(r0 + k, 1), :] = row[0:1]
            gcol[1, pl.ds(r0 + k, 1), :] = row[COLS - 1 : COLS]
        return 0

    lax.fori_loop(0, ROWS // per, step, 0)


def wgrad_tap(step, tap, x3, g3, dw):
    rows, lanes = pl.ds(aligned(tap // 3 * COLS), CELLS), pl.ds(aligned(lax.rem(tap, 3) * CH), CH)
    dw[step] = lax.dot_general(
        x3[rows, lanes], g3[COLS : COLS + CELLS, CH : 2 * CH], (((0,), (0,)), ((), ())), preferred_element_type=F32
    )


def grad_band(i, col_weight, row_of, scaled, slot_grad):
    base = aligned(i * 256, 256)
    weight, row = col_weight[pl.ds(base, 256), :], row_of[pl.ds(base, 256), :]
    lhs = jnp.concatenate(
        [jnp.where(row == jnp.array(r, BF), weight, jnp.zeros_like(weight)) for r in range(ROWS)], 1
    )
    grads = jnp.dot(lhs, scaled[...], preferred_element_type=F32).astype(BF)
    slot_grad[pl.ds(i * 16, 16)] = grads.reshape(16, CAP, CH)


def transpose_kernel(kc, kt):
    for a in range(3):
        for b in range(3):
            kt[a, b * CH : (b + 1) * CH, :] = kc[a, b * CH : (b + 1) * CH, :].T


def back_conv(first, count, g3, kt, cot, dens, scaled, per=8):
    def step(i, _):
        r0 = first + i * per
        base = aligned(r0 * COLS)
        acc = cot[pl.ds(base, per * COLS), :].astype(F32)
        for a in range(3):
            acc = acc + jnp.dot(
                g3[pl.ds(aligned((r0 + 2 - a) * COLS), per * COLS), :], kt[a], preferred_element_type=F32
            )
        scaled[pl.ds(base, per * COLS), :] = (acc * twice(dens[pl.ds(base, per * COLS), :])).astype(BF)
        return 0

    lax.fori_loop(0, count // per, step, 0)


def place(p):
    q = lax.rem(p, 16)
    a = q // 2
    return a, lax.rem(2 * (p // 16 + a) + lax.rem(q, 2), NLON)


def spread_over(j):
    b = lax.rem(j, CHIPS)
    return lax.rem(j // CHIPS + b, NLAT), b


def slot_meta(offsets, counts, cells, turned, meta_src):
    live = iota((CAP, DEV), 0) < counts[...]
    radius = offsets[0] * offsets[0] + offsets[1] * offsets[1]
    weight = jnp.where(live, jnp.exp(-2.0 * radius), 0.0)
    row, col = cells[...] // COLS, cells[...] % COLS
    table = jnp.concatenate([weight, row.astype(F32), col.astype(F32), jnp.zeros((128 - 3 * CAP, DEV), F32)], 0)
    turned[...] = table.T

    def step(t, _):
        meta_src[lax.rem(t, NLON), t // NLON] = turned[pl.ds(t, 1), :]
        return 0

    lax.fori_loop(0, DEV, step, 0, unroll=8)


def turn_slots(by_slot, wide, by_dest):
    flat = by_slot[...].reshape(SLOTS, CH).astype(F32)
    wide[0], wide[1] = flat[:, :128], flat[:, 128:]

    def step(t, _):
        halves = [wide[h, pl.ds(t, CAP, stride=DEV), :] for h in range(2)]
        by_dest[t] = jnp.concatenate(halves, 1).astype(BF)
        return 0

    lax.fori_loop(0, DEV, step, 0, unroll=8)


def kernel(
    feat_in, offsets, counts, cells, kern_in, bias, cot_in,
    enc_out, sums_out, ret_out, bias_out,
    by_slot, wide, by_dest, turned, meta_src, meta_mid, meta_nat,
    feats, meta, kc, kt, cot, enc, onehot, wrf, wrb, dens, edges, edge_inv, col_weight, row_of,
    edge_rows, edge_cols, h_row, h_col, h_cor, col_vals, x3, g3, gsum, gcol, grad_cols, scaled, slot_grad,
    dw, pair_dw, pair_sum, half, rs, reduced, bias_lat, bias_mid, bias_lon, tail_chip, tail_lat, tail_part, tail_sum,
    round_sem, load_sems, a2a_sems, halo_sems, grad_halo_sems, pair_sems, rs_sems, ag_sems, swap_sems, ret_sems, bias_sems, tail_sems,
):
    lat, lon = lax.axis_index("lat"), lax.axis_index("lon")
    me = lat * NLON + lon
    core = lax.rem(lon, 2)
    mate = lon + 1 - 2 * core
    chip = lon // 2
    owner = lat * CHIPS + chip
    mine = lax.rem(lat - chip + CHIPS, CHIPS) * CHIPS + chip

    def over_lat(j):
        return lax.rem(lat + j, NLAT)

    def over_lon(j):
        return lax.rem(lon + j, NLON)

    load_feat = pltpu.make_async_copy(feat_in, by_slot, load_sems.at[1])
    load_kern = pltpu.make_async_copy(kern_in, kc, load_sems.at[2])
    load_cot = pltpu.make_async_copy(cot_in, cot, load_sems.at[3])
    load_feat.start()
    load_kern.start()
    load_cot.start()

    barrier = pltpu.get_barrier_semaphore()

    def greet_lon(j, _):
        pl.semaphore_signal(barrier, inc=1, device_id=(lat, over_lon(j)), device_id_type=MESH)
        return 0

    def greet_lat(j, _):
        pl.semaphore_signal(barrier, inc=1, device_id=(over_lat(j), lon), device_id_type=MESH)
        return 0

    def vouch(j, _):
        pl.semaphore_signal(round_sem, inc=1, device_id=(over_lat(j), lon), device_id_type=MESH)
        return 0

    lax.fori_loop(1, NLON, greet_lon, 0)
    lax.fori_loop(1, NLAT, greet_lat, 0)
    slot_meta(offsets, counts, cells, turned, meta_src)
    pl.semaphore_wait(barrier, NLON + NLAT - 2)
    lax.fori_loop(1, NLAT, vouch, 0)

    def meta_lon(j, _):
        to = over_lon(j)
        remote(meta_src.at[to], meta_mid.at[lon], a2a_sems.at[0], a2a_sems.at[1], lat, to).start()
        return 0

    def meta_lat(j, _):
        to = over_lat(j)
        remote(meta_mid.at[pl.ds(0, NLON), to], meta_nat.at[lat], a2a_sems.at[2], a2a_sems.at[3], to, lon).start()
        return 0

    def send_feats(p, _):
        a, b = place(p)
        to_lat, to_lon = lax.rem(lat - a + NLAT, NLAT), lax.rem(lon - b + NLON, NLON)
        remote(by_dest.at[to_lat * NLON + to_lon], feats.at[p], a2a_sems.at[4], a2a_sems.at[5], to_lat, to_lon).start()
        return 0

    lax.fori_loop(1, NLON, meta_lon, 0)
    meta_mid[lon] = meta_src[lon]
    load_feat.wait()
    turn_slots(by_slot, wide, by_dest)
    pl.semaphore_wait(round_sem, NLAT - 1)
    lax.fori_loop(1, DEV // 2, send_feats, 0)
    wait_bytes(meta_mid.at[pl.ds(0, NLON - 1)], a2a_sems.at[1])
    lax.fori_loop(1, NLAT, meta_lat, 0)
    meta_nat[lat] = meta_mid[:, lat]
    lax.fori_loop(DEV // 2, DEV, send_feats, 0)
    feats[0] = by_dest[me]

    load_kern.wait()
    transpose_kernel(kc, kt)
    wait_bytes(meta_nat.at[pl.ds(0, NLAT - 1)], a2a_sems.at[3])

    def reorder(p, _):
        a, b = place(p)
        meta[p] = meta_nat[over_lat(a), over_lon(b)]
        return 0

    lax.fori_loop(0, DEV, reorder, 0, unroll=4)
    expand_lanes(meta, onehot, wrf, wrb, dens, edges, edge_inv)
    expand_rows(meta, col_weight, row_of)

    wait_bytes(feats.at[pl.ds(0, DEV - 1)], a2a_sems.at[5])
    splat_edges(feats, onehot, wrb, dens, edges, edge_inv, edge_rows, edge_cols)
    halo = exchange_edges(
        lat, lon, (edge_rows.at[0], edge_rows.at[1]), edge_cols, h_row.at[0], h_col.at[0], h_cor.at[0], halo_sems
    )
    for copy in halo:
        copy.start()
    splat(feats, onehot, wrb, dens, x3)
    for copy in halo:
        copy.wait_recv()
    patch(x3, lat, h_row.at[0], h_col.at[0], h_cor.at[0], col_vals, 0, 512)

    load_cot.wait()
    conv(x3, kc, bias, cot, enc, g3, gsum, gcol)
    store_enc = pltpu.make_async_copy(enc, enc_out, load_sems.at[4])
    store_enc.start()
    grad_cols[...] = gcol[...].astype(BF)
    last = ROWS * COLS
    grad_halo = exchange_edges(
        lat, lon, (g3.at[pl.ds(COLS, COLS), pl.ds(CH, CH)], g3.at[pl.ds(last, COLS), pl.ds(CH, CH)]),
        grad_cols, h_row.at[1], h_col.at[1], h_cor.at[1], grad_halo_sems,
    )
    for copy in grad_halo:
        copy.start()

    pair_bias = remote(gsum, pair_sum, pair_sems.at[0, TAPS], pair_sems.at[1, TAPS], lat, mate)
    pair_bias.start()
    taps = [jnp.int32(8)] + [lax.rem(lat + chip + i, 8) for i in range(8)]
    pair = []

    def pair_total(step):
        pair[step].wait()
        total = dw[step, pl.ds(aligned(128 * core), 128), :] + pair_dw[step]
        half[step] = total.astype(BF).reshape(8, 16, CH)

    def last_tap_rows():
        pair_total(0)
        tail_chip[chip] = half[0, chip]

        def step(j, _):
            to = lax.rem(chip + j, CHIPS)
            remote(half.at[0, to], tail_chip.at[chip], tail_sems.at[0], tail_sems.at[1], lat, to * 2 + core).start()
            return 0

        lax.fori_loop(1, CHIPS, step, 0)

    def last_tap_columns():
        wait_bytes(tail_chip.at[pl.ds(0, CHIPS - 1)], tail_sems.at[1])
        tail_part[...] = tail_chip[...].astype(F32).sum(0).astype(BF)
        tail_lat[lat] = tail_part[...]

        def step(j, _):
            remote(tail_part, tail_lat.at[lat], tail_sems.at[2], tail_sems.at[3], over_lat(j), lon).start()
            return 0

        lax.fori_loop(1, NLAT, step, 0)

    def last_tap_gather():
        wait_bytes(tail_lat.at[pl.ds(0, NLAT - 1)], tail_sems.at[3])
        tail_sum[...] = tail_lat[...].astype(F32).sum(0).astype(BF)
        spot = sums_out.at[core, PAIRS + chip]
        pltpu.make_async_copy(tail_sum, spot, load_sems.at[6]).start()

        def step(j, _):
            to = lax.rem(chip + j, CHIPS)
            remote(tail_sum, spot, tail_sems.at[4], tail_sems.at[5], lat, to * 2 + core).start()
            return 0

        lax.fori_loop(1, CHIPS, step, 0)

    def bias_columns():
        pair_bias.wait()
        bias_lat[lat] = gsum[...] + pair_sum[...]

        def step(j, _):
            remote(bias_lat.at[lat], bias_lat.at[lat], bias_sems.at[0], bias_sems.at[1], over_lat(j), lon).start()
            return 0

        lax.fori_loop(1, NLAT, step, 0)

    def bias_rows():
        wait_bytes(bias_lat.at[pl.ds(0, NLAT - 1)], bias_sems.at[1])
        bias_mid[...] = bias_lat[...].sum(0)
        bias_lon[chip] = bias_mid[...]

        def step(j, _):
            to = lax.rem(chip + j, CHIPS)
            remote(bias_mid, bias_lon.at[chip], bias_sems.at[2], bias_sems.at[3], lat, to * 2 + core).start()
            return 0

        lax.fori_loop(1, CHIPS, step, 0)

    def send_tap(step):
        pair_total(step)
        tap = taps[step]

        def send(m, _):
            to_lat = lax.rem(tap + m, NLAT)
            here = jnp.logical_and(to_lat == lat, m == chip)

            @pl.when(jnp.logical_not(here))
            def _():
                remote(
                    half.at[step, m], rs.at[owner], rs_sems.at[0], rs_sems.at[1], to_lat, m * 2 + core
                ).start()

            @pl.when(here)
            def _():
                rs[owner] = half[step, m]

            return 0

        lax.fori_loop(0, CHIPS, send, 0)

    def send_pair(step):
        pair.append(
            remote(
                dw.at[step, pl.ds(aligned(128 * (1 - core)), 128)], pair_dw.at[step],
                pair_sems.at[0, step], pair_sems.at[1, step], lat, mate,
            )
        )
        pair[-1].start()

    beside = {3: last_tap_rows, 6: bias_columns}
    for step in range(TAPS):
        wgrad_tap(step, taps[step], x3, g3, dw)
        send_pair(step)
        if step in beside:
            beside[step]()
        if step > LAG:
            send_tap(step - LAG)

    for copy in grad_halo:
        copy.wait()
    patch(g3, lat, h_row.at[1], h_col.at[1], h_cor.at[1], col_vals, 512, 0)
    for step in range(TAPS - LAG, TAPS):
        send_tap(step)

    last_tap_columns()
    bias_rows()
    back_conv(0, ROWS // 2, g3, kt, cot, dens, scaled)

    wait_bytes(rs.at[pl.ds(0, PAIRS - 1)], rs_sems.at[1])
    reduced[...] = rs[...].astype(F32).sum(0).astype(BF)
    own_sum = pltpu.make_async_copy(reduced, sums_out.at[core, mine], load_sems.at[5])
    own_sum.start()

    def send_sum(j, _):
        a, b = spread_over(j)
        to_chip = lax.rem(chip + b, CHIPS)
        remote(
            reduced, sums_out.at[core, mine], ag_sems.at[0], ag_sems.at[1], over_lat(a), to_chip * 2 + core
        ).start()
        return 0

    lax.fori_loop(1, PAIRS, send_sum, 0)
    back_conv(ROWS // 2, ROWS // 2, g3, kt, cot, dens, scaled)
    last_tap_gather()

    def band(i, _):
        grad_band(i, col_weight, row_of, scaled, slot_grad)

        def back(j, _):
            p = i * 16 + j
            a, b = place(p)

            @pl.when(p != 0)
            def _():
                remote(
                    slot_grad.at[p], ret_out.at[me], ret_sems.at[0], ret_sems.at[1], over_lat(a), over_lon(b)
                ).start()

            return 0

        lax.fori_loop(0, 16, back, 0)
        return 0

    lax.fori_loop(0, DEV // 16, band, 0)
    own_ret = pltpu.make_async_copy(slot_grad.at[0], ret_out.at[me], load_sems.at[7])
    own_ret.start()

    own_sum.wait()
    pltpu.make_async_copy(tail_sum, sums_out.at[core, PAIRS + chip], load_sems.at[6]).wait()
    wait_bytes(sums_out.at[core, pl.ds(0, PAIRS - 1)], ag_sems.at[1])
    wait_bytes(sums_out.at[core, pl.ds(0, CHIPS - 1)], tail_sems.at[5])
    swap = remote(sums_out.at[core], sums_out.at[core], swap_sems.at[0], swap_sems.at[1], lat, mate)
    swap.start()
    wait_bytes(bias_lon.at[pl.ds(0, CHIPS - 1)], bias_sems.at[3])
    bias_out[...] = bias_lon[...].sum(0).sum(0, keepdims=True)

    wait_bytes(meta_mid.at[pl.ds(0, NLON - 1)], a2a_sems.at[0])
    wait_bytes(meta_nat.at[pl.ds(0, NLAT - 1)], a2a_sems.at[2])
    wait_bytes(feats.at[pl.ds(0, DEV - 1)], a2a_sems.at[4])
    wait_bytes(bias_lat.at[pl.ds(0, NLAT - 1)], bias_sems.at[0])
    wait_bytes(bias_lon.at[pl.ds(0, CHIPS - 1)], bias_sems.at[2])
    wait_bytes(tail_chip.at[pl.ds(0, CHIPS - 1)], tail_sems.at[0])
    wait_bytes(tail_lat.at[pl.ds(0, NLAT - 1)], tail_sems.at[2])
    wait_bytes(tail_chip.at[pl.ds(0, CHIPS - 1)], tail_sems.at[4])
    wait_bytes(rs.at[pl.ds(0, PAIRS - 1)], rs_sems.at[0])
    wait_bytes(rs.at[pl.ds(0, PAIRS - 1)], ag_sems.at[0])
    for copy in halo:
        copy.wait_send()
    store_enc.wait()
    own_ret.wait()
    wait_bytes(slot_grad.at[pl.ds(0, DEV - 1)], ret_sems.at[0])
    wait_bytes(ret_out.at[pl.ds(0, DEV - 1)], ret_sems.at[1])
    swap.wait()


def fused(feat, offsets, counts, cells, kern, bias, cot):
    vm = pltpu.VMEM
    dma = pltpu.SemaphoreType.DMA
    scratch = [
        vm((CAP, DEV, CH), BF),
        vm((2, SLOTS, 128), F32),
        vm((DEV, CAP, CH), BF),
        vm((DEV, 128), F32),
        vm((NLON, NLAT, 1, 128), F32),
        vm((NLON, NLAT, 1, 128), F32),
        vm((NLAT, NLON, 1, 128), F32),
        vm((DEV, CAP, CH), BF),
        vm((DEV, 1, 128), F32),
        vm((3, 3 * CH, CH), BF),
        vm((3, 3 * CH, CH), BF),
        vm((CELLS, CH), BF),
        vm((CELLS, CH), BF),
        vm((COLS, SLOTS), BF),
        vm((ROWS, SLOTS), F32),
        vm((ROWS, 16, SLOTS), BF),
        vm((CELLS, 128), F32),
        vm((2 * ROWS, SLOTS), BF),
        vm((2 * ROWS, 128), F32),
        vm((SLOTS, 128), BF),
        vm((SLOTS, 128), BF),
        vm((2, COLS, CH), BF),
        vm((2, ROWS, CH), BF),
        vm((2, 2, COLS, CH), BF),
        vm((2, 2, ROWS, CH), BF),
        vm((2, 4, 16, CH), BF),
        vm((2, 48, CH), F32),
        vm(((ROWS + 2) * COLS, 3 * CH), BF),
        vm(((ROWS + 2) * COLS, 3 * CH), BF),
        vm((8, CH), F32),
        vm((2, ROWS, CH), F32),
        vm((2, ROWS, CH), BF),
        vm((CELLS, CH), BF),
        vm((DEV, CAP, CH), BF),
        vm((TAPS, CH, CH), F32),
        vm((TAPS, 128, CH), F32),
        vm((8, CH), F32),
        vm((TAPS, CHIPS, 16, CH), BF),
        vm((PAIRS, 16, CH), BF),
        vm((16, CH), BF),
        vm((NLAT, 8, CH), F32),
        vm((8, CH), F32),
        vm((CHIPS, 8, CH), F32),
        vm((CHIPS, 16, CH), BF),
        vm((NLAT, 16, CH), BF),
        vm((16, CH), BF),
        vm((16, CH), BF),
        pltpu.SemaphoreType.REGULAR,
        dma((8,)),
        dma((6,)),
        dma((2, 8)),
        dma((2, 8)),
        dma((2, 10)),
        dma((2,)),
        dma((2,)),
        dma((2,)),
        dma((2,)),
        dma((4,)),
        dma((6,)),
    ]
    anywhere = pl.BlockSpec(memory_space=pl.ANY)
    local = pl.BlockSpec(memory_space=pltpu.VMEM)
    return pl.pallas_call(
        kernel,
        out_shape=[
            jax.ShapeDtypeStruct((CELLS, CH), BF),
            jax.ShapeDtypeStruct((2, CHUNKS, 16, CH), BF),
            jax.ShapeDtypeStruct((DEV, CAP, CH), BF),
            jax.ShapeDtypeStruct((1, CH), F32),
        ],
        in_specs=[anywhere, local, local, local, anywhere, local, anywhere],
        out_specs=[anywhere, anywhere, anywhere, local],
        scratch_shapes=scratch,
        compiler_params=pltpu.CompilerParams(collective_id=0, has_side_effects=True, vmem_limit_bytes=60 * 2**20),
        name="fused",
    )(feat, offsets, counts, cells, kern, bias, cot)


def finish_kernel(
    enc_in, sums_in, ret_in, bias_in, enc_out, grad_out, bias_out, obs_out, enc, sums, ret, grad, wide, obs, sems, out_sems
):
    scale = 1.0 / math.sqrt(CELLS * DEV)
    load_ret = pltpu.make_async_copy(ret_in, ret, sems.at[0])
    load_sums = pltpu.make_async_copy(sums_in, sums, sems.at[1])
    load_enc = pltpu.make_async_copy(enc_in, enc, sems.at[2])
    load_sums.start()
    load_ret.start()
    load_enc.start()
    bias_out[...] = bias_in[...] * scale
    copies = []

    def store(src, dst):
        copies.append(pltpu.make_async_copy(src, dst, out_sems.at[len(copies)]))
        copies[-1].start()

    load_sums.wait()
    for tap in range(TAPS):
        for core in range(2):
            rows = sums[core, tap * CHIPS : (tap + 1) * CHIPS].reshape(128, CH)
            grad[tap, core * 128 : (core + 1) * 128, :] = rows.astype(F32) * scale
        store(grad.at[tap], grad_out.at[tap])
    load_enc.wait()
    store(enc, enc_out)
    load_ret.wait()
    flat = ret[...].reshape(SLOTS, CH).astype(F32)
    wide[0], wide[1] = flat[:, :128], flat[:, 128:]
    for k in range(CAP):
        halves = [wide[h, pl.ds(k, DEV, stride=CAP), :] for h in range(2)]
        obs[k] = jnp.concatenate(halves, 1).astype(BF)
        if k % 4 == 3:
            store(obs.at[pl.ds(k - 3, 4)], obs_out.at[pl.ds(k - 3, 4)])
    for copy in copies:
        copy.wait()


def finish(encoded, sums, ret, bias_sum):
    vm = pltpu.VMEM
    anywhere = pl.BlockSpec(memory_space=pl.ANY)
    local = pl.BlockSpec(memory_space=pltpu.VMEM)
    return pl.pallas_call(
        finish_kernel,
        out_shape=[
            jax.ShapeDtypeStruct((CELLS, CH), BF),
            jax.ShapeDtypeStruct((TAPS, CH, CH), F32),
            jax.ShapeDtypeStruct((1, CH), F32),
            jax.ShapeDtypeStruct((CAP, DEV, CH), BF),
        ],
        in_specs=[anywhere, anywhere, anywhere, local],
        out_specs=[anywhere, anywhere, local, anywhere],
        scratch_shapes=[
            vm((CELLS, CH), BF),
            vm((2, CHUNKS, 16, CH), BF),
            vm((DEV, CAP, CH), BF),
            vm((TAPS, CH, CH), F32),
            vm((2, SLOTS, 128), F32),
            vm((CAP, DEV, CH), BF),
            pltpu.SemaphoreType.DMA((3,)),
            pltpu.SemaphoreType.DMA((16,)),
        ],
        compiler_params=pltpu.CompilerParams(vmem_limit_bytes=56 * 2**20),
        name="finish",
    )(encoded, sums, ret, bias_sum)


def body(features, offsets, counts, cell_index, kern, conv_bias, cotangent):
    encoded, sums, ret, bias_sum = fused(
        features[0], offsets[:, 0], counts, cell_index[0], kern.reshape(3, 3 * CH, CH),
        conv_bias.reshape(1, CH), cotangent.reshape(CELLS, CH),
    )
    encoded, weight_grad, bias_grad, obs_grad = finish(encoded, sums, ret, bias_sum)
    return (
        encoded.reshape(ROWS, COLS, CH),
        weight_grad.reshape(3, 3, CH, CH),
        bias_grad.reshape(CH),
        obs_grad[None],
    )


def solution(mesh):
    return jax.shard_map(
        body,
        mesh=mesh,
        in_specs=(
            P(("lat", "lon"), None, None, None),
            P(None, ("lat", "lon"), None, None),
            P(("lat", "lon"), None),
            P(("lat", "lon"), None, None),
            P(),
            P(),
            P("lat", "lon", None),
        ),
        out_specs=(P("lat", "lon", None), P(), P(), P(("lat", "lon"), None, None, None)),
        check_vma=False,
    )
```
